32 devices in a mesh: tm: 8 (over y, x, core), batch: 4 (over z).
Axes of the slice: x: 2, y: 2, z: 4, core: 2. Of those that a mesh axis runs over, the one named last changes fastest.
Arguments:
- features: bfloat16 [4, 896, 2, 1024], P('batch', 'tm'), may hold values from -52 to 52
- lengths: int32 [4, 24], P('batch'), may hold values from 8 to 63, as said below
- conv1_weight: bfloat16 [2048, 9, 1024], P('tm', None, 'batch'), may hold values from -0.0625 to 0.0625
- norm1_gain: float32 [2048], P('tm'), may hold values from 0.25 to 1.75
- norm1_bias: float32 [2048], P('tm'), may hold values from -2.5 to 2.5
- conv2_weight: bfloat16 [2048, 9, 2048], P('tm', None, 'batch'), may hold values from -0.046875 to 0.046875
- norm2_gain: float32 [2048], P('tm'), may hold values from 0.25 to 1.75
- norm2_bias: float32 [2048], P('tm'), may hold values from -2.5 to 2.5
- out_grad: bfloat16 [4, 896, 2, 2048], P('batch', 'tm'), may hold values from -6 to 6
Outputs:
- block_out: bfloat16 [4, 896, 2, 2048], P('batch', 'tm')
- input_grad: bfloat16 [4, 896, 2, 1024], P('batch', 'tm')
- conv1_grad: float32 [2048, 9, 1024], P('tm', None, 'batch')
- gain1_grad: float32 [2048], P('tm')
- bias1_grad: float32 [2048], P('tm')
- conv2_grad: float32 [2048, 9, 2048], P('tm', None, 'batch')
- gain2_grad: float32 [2048], P('tm')
- bias2_grad: float32 [2048], P('tm')
The draws below stay inside these ranges and needn't reach their ends.
Inputs may be any that keep to these rules, and one draw needn't show every extreme that they name: `lengths`: clips 0 to 7 of a group are padded to 16 frames, the next 8 to 32 and the last 8 to 64; a clip's length is at least half of its padded frames and below them. In every group the first clip of each padded length has one frame less than its padded frames and the second exactly half of them.
All inputs are finite; a program needn't handle non-finite values.
Results may differ from the reference program's by a relative error of at most 0.019.
Values may be sent and summed in bfloat16 or wider, within the bound.
No kernel may reach another device: no remote copies, remote signals or barrier semaphores. Data moves between devices by JAX's collectives and lax.ppermute only.
A program may use at most 320 MiB of HBM per device.

```python
import jax
import jax.numpy as jnp
from jax import lax

C1 = 1024
C2 = 2048
MELS = 2
TAPS = 9
CLIPS = 8
GF = 896
G = 4


def draw_features(key, part):
    main_key = jax.random.fold_in(key, 11)
    chan_key = jax.random.fold_in(key, 12)
    group_pos = jnp.arange(G, dtype=jnp.float32)[:, None, None, None] / (G - 1)
    channel_scale = jnp.exp(jax.random.uniform(chan_key, (1, 1, 1, C1), jnp.float32, -1.2, 1.2))
    base_draw = jax.random.truncated_normal(main_key, -4.0, 4.0, (G, GF, MELS, C1), jnp.float32)
    group_scale = 3.0 ** group_pos
    return (base_draw * group_scale * channel_scale).astype(jnp.bfloat16)


def draw_lengths(key, part):
    padded = jnp.repeat(jnp.array([16, 32, 64], dtype=jnp.int32), CLIPS)
    halves = padded // 2
    random_bits = jax.random.randint(key, (G, 3 * CLIPS), 0, 1 << 20, dtype=jnp.int32)
    drawn_lengths = halves[None, :] + random_bits % halves[None, :]
    position = jnp.arange(3 * CLIPS, dtype=jnp.int32) % CLIPS
    drawn_lengths = jnp.where(position[None, :] == 0, padded[None, :] - 1, drawn_lengths)
    drawn_lengths = jnp.where(position[None, :] == 1, halves[None, :], drawn_lengths)
    return drawn_lengths.astype(jnp.int32)


def shard_levels(rng, shape, pieces, least, largest):
    def one(dim, parts):
        heights = jax.random.uniform(jax.random.fold_in(jax.random.fold_in(rng, 6), dim), (parts,), jnp.float32, least / len(pieces), largest / len(pieces))
        return jnp.repeat(jnp.exp(heights), shape[dim] // parts).reshape((-1,) + (1,) * (len(shape) - dim - 1))

    factor_of = one(*pieces[0])
    for cut in pieces[1:]:
        factor_of = factor_of * one(*cut)
    return factor_of


def centred(rng, extent, scale, reach, cuts=(), kind=jnp.bfloat16):
    values = jax.random.normal(rng, extent, jnp.float32) * scale
    if len(cuts) > 0:
        values = shard_levels(rng, extent, cuts, -0.22, 0.18) * values
    return jnp.clip(values, min=-reach, max=reach).astype(kind)


def setup_inputs(seed: int = 0) -> dict:
    seeds = jax.random.split(jax.random.key(seed), 10)
    features = draw_features(jax.random.fold_in(seeds[9], 71), 0)
    lengths = draw_lengths(jax.random.fold_in(seeds[9], 71), 0)
    conv1_weight = centred(seeds[2], (C2, TAPS, C1), (TAPS * C1) ** -0.5, 0.0625, ((0, 8), (2, 4)))
    norm1_gain = jnp.clip(1.0 + 0.15 * jax.random.normal(seeds[3], (C2,), jnp.float32), 0.25, 1.75)
    norm1_bias = centred(seeds[4], (C2,), 0.5, 2.5, ((0, 8),), jnp.float32)
    conv2_weight = centred(seeds[5], (C2, TAPS, C2), (TAPS * C2) ** -0.5, 0.046875, ((0, 8), (2, 4)))
    norm2_gain = jnp.clip(1.0 + 0.15 * jax.random.normal(seeds[6], (C2,), jnp.float32), 0.25, 1.75)
    norm2_bias = centred(seeds[7], (C2,), 0.5, 2.5, ((0, 8),), jnp.float32)
    out_grad = centred(seeds[8], (G, GF, MELS, C2), 1.0, 6.0, ((0, 4), (1, 8)))
    return dict(features=features, lengths=lengths, conv1_weight=conv1_weight, norm1_gain=norm1_gain, norm1_bias=norm1_bias, conv2_weight=conv2_weight, norm2_gain=norm2_gain, norm2_bias=norm2_bias, out_grad=out_grad)


@jax.custom_vjp
def low(v):
    return lax.optimization_barrier(v.astype(jnp.bfloat16)).astype(jnp.float32)

@jax.custom_vjp
def low_back(v):
    return v

def low_keep(v):
    return (low(v), None)

def low_pass(kept, grad):
    return (grad,)

def back_keep(v):
    return (v, None)

def back_low(kept, grad):
    return (low(grad),)
low.defvjp(low_keep, low_pass)
low_back.defvjp(back_keep, back_low)

def frame_valid(lengths_row, frame_total, clip_count):
    frame_ids = jnp.arange(frame_total, dtype=jnp.int32)
    first_end = 16 * clip_count
    second_end = 48 * clip_count
    clip_index = jnp.where(frame_ids < first_end, frame_ids // 16, jnp.where(frame_ids < second_end, clip_count + (frame_ids - first_end) // 32, 2 * clip_count + (frame_ids - second_end) // 64)).astype(jnp.int32)
    offset = jnp.where(frame_ids < first_end, frame_ids % 16, jnp.where(frame_ids < second_end, (frame_ids - first_end) % 32, (frame_ids - second_end) % 64)).astype(jnp.int32)
    clip_ids = jnp.arange(3 * clip_count, dtype=jnp.int32)
    picked = jnp.where(clip_index[:, None] == clip_ids[None, :], lengths_row.astype(jnp.int32)[None, :], jnp.zeros((), jnp.int32))
    length_here = lax.optimization_barrier(jnp.sum(picked, axis=1)).astype(jnp.int32)
    return offset < length_here

def convolve(source, weight):
    frame_total = source.shape[1]
    mel_count = source.shape[2]
    padded = jnp.pad(source, ((0, 0), (1, 1), (1, 1), (0, 0)))
    running = None
    for tap_row in range(3):
        for tap_col in range(3):
            term = jnp.einsum('gtmc,oc->gtmo', padded[:, tap_row:tap_row + frame_total, tap_col:tap_col + mel_count], weight[:, 3 * tap_row + tap_col, :], precision=lax.Precision.HIGHEST)
            running = term if running is None else running + term
    return running

def normalize(before, pixel_mask, scale_row, shift_row, pixel_total):
    average = lax.optimization_barrier(jnp.sum(before * pixel_mask, axis=(0, 1, 2))) / pixel_total
    variance = lax.optimization_barrier(jnp.sum(before * before * pixel_mask, axis=(0, 1, 2))) / pixel_total - average * average
    scaled = (before - average) * lax.rsqrt(variance + 1e-05)
    return pixel_mask * jax.nn.silu(scale_row * scaled + shift_row)

def reference(features, lengths, conv1_weight, norm1_gain, norm1_bias, conv2_weight, norm2_gain, norm2_bias, out_grad):

    def valid_row(lengths_row):
        return frame_valid(lengths_row, GF, CLIPS)
    valid_mask = jax.vmap(valid_row)(lengths)
    pixel_mask = jnp.where(valid_mask, jnp.ones((), jnp.float32), jnp.zeros((), jnp.float32))[:, :, None, None]
    pixel_total = jnp.sum(lengths.astype(jnp.float32)) * MELS

    def forward(inputs, weight_one, gain_one, bias_one, weight_two, gain_two, bias_two):
        masked = inputs * pixel_mask
        pre_one = low_back(convolve(masked, weight_one))
        hidden = low(normalize(pre_one, pixel_mask, gain_one, bias_one, pixel_total))
        pre_two = low_back(convolve(hidden, weight_two))
        return normalize(pre_two, pixel_mask, gain_two, bias_two, pixel_total)
    primals = (features.astype(jnp.float32), conv1_weight.astype(jnp.float32), norm1_gain.astype(jnp.float32), norm1_bias.astype(jnp.float32), conv2_weight.astype(jnp.float32), norm2_gain.astype(jnp.float32), norm2_bias.astype(jnp.float32))
    result, pullback = jax.vjp(forward, *primals)
    grads = pullback(out_grad.astype(jnp.float32))
    return (result.astype(jnp.bfloat16), grads[0].astype(jnp.bfloat16), grads[1], grads[2], grads[3], grads[4], grads[5], grads[6])
```

```python
import jax
import jax.numpy as jnp
from jax import lax
from jax.sharding import PartitionSpec as P


def frame_valid(lengths_row, frame_total, clip_count):
    frame_ids = jnp.arange(frame_total, dtype=jnp.int32)
    first_end = 16 * clip_count
    second_end = 48 * clip_count
    clip_index = jnp.where(
        frame_ids < first_end,
        frame_ids // 16,
        jnp.where(
            frame_ids < second_end,
            clip_count + (frame_ids - first_end) // 32,
            2 * clip_count + (frame_ids - second_end) // 64,
        ),
    )
    offset = jnp.where(
        frame_ids < first_end,
        frame_ids % 16,
        jnp.where(
            frame_ids < second_end, (frame_ids - first_end) % 32, (frame_ids - second_end) % 64
        ),
    )
    clip_ids = jnp.arange(3 * clip_count, dtype=jnp.int32)
    picked = jnp.where(
        clip_index[:, None] == clip_ids[None, :], lengths_row[None, :], jnp.zeros((), jnp.int32)
    )
    length_here = jnp.sum(picked, axis=1)
    return offset < length_here


def silu_slope(value):
    sigma = jax.nn.sigmoid(value)
    return sigma * (1.0 + value * (1.0 - sigma))


def per_device(
    features,
    lengths,
    conv1_weight,
    norm1_gain,
    norm1_bias,
    conv2_weight,
    norm2_gain,
    norm2_bias,
    out_grad,
):
    f32, bf16 = jnp.float32, jnp.bfloat16
    n = lax.axis_size("tm")
    planes = lax.axis_size("batch")
    chips = n // 2
    square = chips == 4
    me = lax.axis_index("tm")
    plane = lax.axis_index("batch")
    chip, core = me // 2, me % 2
    own_frames, mels, width1 = features.shape[1:]
    frames = own_frames * n
    part = conv2_weight.shape[0]
    slice2 = conv2_weight.shape[2]
    per_plane = chips // planes
    half2 = slice2 // 2
    block = half2 // chips
    sub = width1 // (planes * chips)
    hz = planes // 2
    clip_count = lengths.shape[1] // 3
    same_core = [[c + 2 * p for p in range(chips)] for c in range(2)]
    groups = range(planes)

    def to_core(x):
        return lax.ppermute(x, "tm", [(i, i ^ 1) for i in range(n)])

    def to_chip(x, bits):
        return lax.ppermute(x, "tm", [(i, i ^ (2 * bits)) for i in range(n)])

    def to_right(x):
        return lax.ppermute(x, "batch", [(z, (z + 1) % planes) for z in range(planes)])

    def chip_order(x, axis):
        if not square:
            return x
        shape = x.shape
        x = x.reshape(shape[:axis] + (2, 2) + shape[axis + 1 :])
        x = jnp.where(chip // 2 == 1, jnp.flip(x, axis), x)
        x = jnp.where(chip % 2 == 1, jnp.flip(x, axis + 1), x)
        return x.reshape(shape)

    def core_order(x, axis):
        return jnp.where(core == 1, jnp.flip(x, axis), x)

    def gather_chips(x):
        if not square:
            return lax.all_gather(x, "tm", axis=1, tiled=True, axis_index_groups=same_core)
        return jnp.concatenate([x] + [to_chip(x, b) for b in (1, 2, 3)], axis=1)

    def scatter_chips(x):
        if not square:
            return lax.psum_scatter(
                x, "tm", scatter_dimension=1, tiled=True, axis_index_groups=same_core
            ).astype(f32)
        lanes = x.shape[1] // 4
        parts = [x[:, b * lanes : (b + 1) * lanes] for b in range(4)]
        got = [parts[0]] + [to_chip(parts[b], b) for b in (1, 2, 3)]
        got = [v.astype(f32) for v in got]
        return (got[0] + got[1]) + (got[2] + got[3])

    def plane_sum(x):
        terms = [x] + [
            lax.ppermute(x, "batch", [(z, z ^ s) for z in range(planes)])
            for s in range(1, planes)
        ]
        while len(terms) > 1:
            terms = [terms[k] + terms[k + 1] for k in range(0, len(terms), 2)]
        return terms[0]

    def ring_gather(x):
        out = [x]
        for _ in range(planes - 1):
            out.append(to_right(out[-1]))
        return out

    def ring_sum(make):
        total = make(1 % planes)
        for step in range(2, planes + 1):
            moved = to_right(total.astype(bf16))
            total = make(step % planes) + moved.astype(f32)
        return total

    def pad_rows(x):
        return jnp.pad(x, ((1, 1), (0, 0)))

    def contract(rows, matrix, dims):
        return lax.dot_general(rows, matrix, (dims, ((), ())), preferred_element_type=f32)

    def conv(x, taps):
        padded = pad_rows(x)
        total = None
        for a in range(3):
            term = contract(padded[a : a + frames], taps[a], ((1,), (1,)))
            total = term if total is None else total + term
        return total

    def conv_t(dy, taps):
        padded = pad_rows(dy)
        total = None
        for a in range(3):
            term = contract(padded[2 - a : 2 - a + frames], taps[a], ((1,), (0,)))
            total = term if total is None else total + term
        return total

    def conv_w(x, dy):
        padded = pad_rows(x)
        return [contract(dy, padded[a : a + frames], ((0,), (0,))) for a in range(3)]

    w1 = conv1_weight.reshape(part, 9, chips, sub).transpose(2, 0, 1, 3)
    w1 = lax.all_to_all(w1, "tm", 0, 0, tiled=True, axis_index_groups=same_core)
    w1 = lax.all_to_all(
        w1.reshape(planes, per_plane * part, 9, sub), "batch", 0, 0, tiled=True
    )
    w1 = w1.reshape(2, hz, chips, block, 9, sub).transpose(2, 3, 4, 0, 1, 5)
    w1 = core_order(chip_order(w1, 0), 3)

    def taps1():
        mats = []
        for a in range(3):
            outs = []
            for mo in range(mels):
                ins = [w1[:, :, 3 * a + mi - mo + 1] for mi in range(mels)]
                outs.append(jnp.stack(ins, axis=3))
            mat = jnp.stack(outs, axis=1)
            mats.append(mat.reshape(chips * mels * block, 2 * mels * hz * sub))
        return mats

    w2 = conv2_weight.reshape(part, 9, per_plane, 2, part).transpose(0, 1, 3, 2, 4)
    w2 = w2.reshape(part, 9, 2, chips, block)
    w2 = core_order(chip_order(w2, 3), 2)

    def taps2():
        mats = []
        for a in range(3):
            outs = []
            for mo in range(mels):
                ins = [w2[:, 3 * a + mi - mo + 1] for mi in range(mels)]
                outs.append(jnp.stack(ins, axis=3))
            mat = jnp.stack(outs, axis=0)
            mats.append(mat.reshape(mels * part, 2 * chips * mels * block))
        return mats

    weights1, weights2 = taps1(), taps2()

    all_lengths = lax.all_gather(lengths[0], "batch")
    count = jnp.sum(all_lengths.astype(f32)) * mels
    valid = [
        frame_valid(
            lax.dynamic_index_in_dim(all_lengths, (plane - r) % planes, 0, keepdims=False),
            frames,
            clip_count,
        ).astype(f32)[:, None]
        for r in groups
    ]
    own_valid = frame_valid(lengths[0], frames, clip_count).astype(bf16)
    here_valid = lax.dynamic_slice_in_dim(own_valid, me * own_frames, own_frames, 0)

    masked = features[0] * here_valid[:, None, None]
    masked = masked.reshape(own_frames, mels, 2, hz, chips, sub).transpose(4, 2, 0, 1, 3, 5)
    masked = masked.reshape(n * own_frames, mels * hz * sub)
    masked = lax.all_to_all(masked, "tm", 0, 0, tiled=True)
    mine = ring_gather(masked)
    inputs = [jnp.concatenate([x, to_core(x)], axis=1) for x in mine]

    pre1 = [scatter_chips(conv(x, weights1).astype(bf16)) for x in inputs]

    def per_channel(x, width):
        return jnp.sum(x.reshape(mels, width), axis=0)

    def per_lane(x):
        return jnp.tile(x, mels)[None]

    def rows_sum(x):
        return jnp.sum(x, axis=0)

    def norm_stats(total, square_total):
        average = total / count
        variance = square_total / count - average * average
        return average, lax.rsqrt(variance + 1e-05)

    sums = sum(rows_sum(x * v) for x, v in zip(pre1, valid))
    squares = sum(rows_sum(x * x * v) for x, v in zip(pre1, valid))
    mean1, rstd1 = norm_stats(per_channel(sums, block), per_channel(squares, block))

    both1 = lax.all_gather(jnp.stack([norm1_gain, norm1_bias]), "tm")
    both1 = both1.transpose(1, 0, 2).reshape(2, planes, per_plane, 2, part)
    both1 = lax.dynamic_index_in_dim(both1, plane, 1, keepdims=False)
    both1 = lax.dynamic_index_in_dim(both1, core, 2, keepdims=False).reshape(2, half2)
    both1 = lax.dynamic_slice_in_dim(both1, chip * block, block, 1)
    gain1, bias1 = both1[0], both1[1]

    xhat1 = [(x - per_lane(mean1)) * per_lane(rstd1) for x in pre1]
    z1 = [per_lane(gain1) * x + per_lane(bias1) for x in xhat1]
    act1 = [(v * jax.nn.silu(z)).astype(bf16) for v, z in zip(valid, z1)]

    hidden = {}

    def hidden_of(r):
        if r not in hidden:
            half = gather_chips(act1[r])
            hidden[r] = jnp.concatenate([half, to_core(half)], axis=1)
        return hidden[r]

    pre2 = ring_sum(lambda r: conv(hidden_of(r), weights2))
    v0 = valid[0]
    sums2 = jnp.stack([rows_sum(pre2 * v0), rows_sum(pre2 * pre2 * v0)])
    sums2 = plane_sum(sums2.reshape(2, mels, part).sum(axis=1))
    mean2, rstd2 = norm_stats(sums2[0], sums2[1])
    xhat2 = (pre2 - per_lane(mean2)) * per_lane(rstd2)
    z2 = per_lane(norm2_gain) * xhat2 + per_lane(norm2_bias)
    out_local = (v0 * jax.nn.silu(z2)).astype(bf16)
    block_out = lax.all_to_all(
        out_local.reshape(n, own_frames, mels, part), "tm", 0, 0, tiled=True
    )
    block_out = block_out.transpose(1, 2, 0, 3).reshape(1, own_frames, mels, n * part)

    grad_in = out_grad[0].reshape(own_frames, mels, n, part).transpose(2, 0, 1, 3)
    grad_in = lax.all_to_all(grad_in, "tm", 0, 0, tiled=True).reshape(frames, mels * part)
    dz2 = grad_in.astype(f32) * v0 * silu_slope(z2)
    grads2 = jnp.stack([rows_sum(dz2), rows_sum(dz2 * xhat2)])
    grads2 = plane_sum(grads2.reshape(2, mels, part).sum(axis=1))
    bias2_grad, gain2_grad = grads2[0], grads2[1]
    dpre2 = (
        v0
        * per_lane(norm2_gain * rstd2)
        * (dz2 - (per_lane(bias2_grad) + xhat2 * per_lane(gain2_grad)) / count)
    ).astype(bf16)

    dpre2 = ring_gather(dpre2)
    half_lanes = chips * mels * block

    def back2(r):
        dact = conv_t(dpre2[r], weights2)
        other = to_core(dact[:, half_lanes:].astype(bf16))
        return scatter_chips((dact[:, :half_lanes] + other.astype(f32)).astype(bf16))

    dact1 = [back2(r) for r in groups]
    wgrad2 = [conv_w(hidden_of(r), dpre2[r]) for r in groups]

    def mel_taps(mats, cols, place):
        taps = []
        for a in range(3):
            mat = mats[a]
            for b in range(3):
                total = None
                for mo in range(mels):
                    mi = mo + b - 1
                    if 0 <= mi < mels:
                        term = place(mat, mo, mi)
                        total = term if total is None else total + term
                taps.append(total)
        return taps

    mats2 = [
        sum(wgrad2[r][a] for r in groups).reshape(mels, part, 2, chips, mels, block)
        for a in range(3)
    ]
    conv2_grad = jnp.stack(
        mel_taps(mats2, None, lambda m, mo, mi: m[mo, :, :, :, mi]), axis=1
    )
    conv2_grad = chip_order(core_order(conv2_grad, 2), 3)
    conv2_grad = conv2_grad.reshape(part, 9, 2, per_plane, part).transpose(0, 1, 3, 2, 4)
    conv2_grad = conv2_grad.reshape(part, 9, slice2)

    dz1 = [d * v * silu_slope(z) for d, v, z in zip(dact1, valid, z1)]
    bias1_sum = per_channel(sum(rows_sum(d) for d in dz1), block)
    gain1_sum = per_channel(sum(rows_sum(d * x) for d, x in zip(dz1, xhat1)), block)
    dpre1 = [
        (
            v
            * per_lane(gain1 * rstd1)
            * (d - (per_lane(bias1_sum) + x * per_lane(gain1_sum)) / count)
        ).astype(bf16)
        for v, d, x in zip(valid, dz1, xhat1)
    ]
    both = lax.all_gather(jnp.stack([gain1_sum, bias1_sum]), ("batch", "tm"))
    both = both.reshape(planes, chips, 2, 2, block).transpose(3, 0, 2, 1, 4)
    both = both.reshape(2, planes, 2, per_plane, part).transpose(0, 1, 3, 2, 4)
    both = lax.dynamic_index_in_dim(both.reshape(2, n, part), me, 1, keepdims=False)
    gain1_grad, bias1_grad = both[0], both[1]

    spread = {}

    def spread_of(r):
        if r not in spread:
            spread[r] = gather_chips(dpre1[r])
        return spread[r]

    own_lanes = mels * hz * sub

    def back1(r):
        dx = conv_t(spread_of(r), weights1)
        other = to_core(dx[:, own_lanes:].astype(bf16))
        return dx[:, :own_lanes] + other.astype(f32)

    dx = ring_sum(back1).astype(bf16)
    dx = lax.all_to_all(dx.reshape(n, own_frames, own_lanes), "tm", 0, 0, tiled=True)
    dx = dx.reshape(chips, 2, own_frames, mels, hz, sub).transpose(2, 3, 1, 4, 0, 5)
    input_grad = dx.reshape(1, own_frames, mels, width1) * here_valid[None, :, None, None]

    wgrad1 = [conv_w(inputs[r], spread_of(r)) for r in groups]
    mats1 = [
        sum(wgrad1[r][a] for r in groups).reshape(chips, mels, block, 2, mels, hz, sub)
        for a in range(3)
    ]
    grad1 = jnp.stack(
        mel_taps(mats1, None, lambda m, mo, mi: m[:, mo, :, :, mi]), axis=2
    ).astype(bf16)
    grad1 = chip_order(core_order(grad1, 3), 0)
    grad1 = grad1.transpose(3, 4, 0, 1, 2, 5).reshape(planes, half2, 9, sub)
    grad1 = lax.all_to_all(grad1, "batch", 0, 0, tiled=True)
    grad1 = lax.all_to_all(
        grad1.reshape(chips, part, 9, sub), "tm", 0, 0, tiled=True, axis_index_groups=same_core
    )
    conv1_grad = grad1.transpose(1, 2, 0, 3).reshape(part, 9, chips * sub).astype(f32)

    return (
        block_out,
        input_grad,
        conv1_grad,
        gain1_grad,
        bias1_grad,
        conv2_grad,
        gain2_grad,
        bias2_grad,
    )


def solution(mesh):
    return jax.shard_map(
        per_device,
        mesh=mesh,
        in_specs=(
            P("batch", "tm", None, None),
            P("batch", None),
            P("tm", None, "batch"),
            P("tm"),
            P("tm"),
            P("tm", None, "batch"),
            P("tm"),
            P("tm"),
            P("batch", "tm", None, None),
        ),
        out_specs=(
            P("batch", "tm", None, None),
            P("batch", "tm", None, None),
            P("tm", None, "batch"),
            P("tm"),
            P("tm"),
            P("tm", None, "batch"),
            P("tm"),
            P("tm"),
        ),
        check_vma=False,
    )
```

```python
import functools

import jax
import jax.numpy as jnp
from jax import lax
from jax.experimental import pallas as pl
from jax.experimental.pallas import tpu as pltpu
from jax.sharding import PartitionSpec as P

f32, bf16 = jnp.float32, jnp.bfloat16


def frame_valid(lengths_row, frame_total, clip_count):
    frame_ids = jnp.arange(frame_total, dtype=jnp.int32)
    first_end = 16 * clip_count
    second_end = 48 * clip_count
    clip_index = jnp.where(
        frame_ids < first_end,
        frame_ids // 16,
        jnp.where(
            frame_ids < second_end,
            clip_count + (frame_ids - first_end) // 32,
            2 * clip_count + (frame_ids - second_end) // 64,
        ),
    )
    offset = jnp.where(
        frame_ids < first_end,
        frame_ids % 16,
        jnp.where(
            frame_ids < second_end, (frame_ids - first_end) % 32, (frame_ids - second_end) % 64
        ),
    )
    clip_ids = jnp.arange(3 * clip_count, dtype=jnp.int32)
    picked = jnp.where(
        clip_index[:, None] == clip_ids[None, :], lengths_row[None, :], jnp.zeros((), jnp.int32)
    )
    length_here = jnp.sum(picked, axis=1)
    return offset < length_here


def silu_slope(value):
    sigma = jax.nn.sigmoid(value)
    return sigma * (1.0 + value * (1.0 - sigma))


def tap_weights(weight, tap_row, mel_count):
    row_blocks = []
    for mel_out in range(mel_count):
        col_blocks = []
        for mel_in in range(mel_count):
            offset = mel_in - mel_out + 1
            col_blocks.append(weight[:, 3 * tap_row + offset, :])
        row_blocks.append(jnp.concatenate(col_blocks, axis=1))
    return jnp.concatenate(row_blocks, axis=0)


def convolve(source, weight):
    frame_total, mel_count, width_in = source.shape
    width_out = weight.shape[0]
    flat_rows = jnp.pad(source.reshape(frame_total, mel_count * width_in), ((1, 1), (0, 0)))
    running = jnp.zeros((frame_total, mel_count * width_out), jnp.float32)
    for tap_row in range(3):
        running = running + lax.dot_general(
            flat_rows[tap_row : tap_row + frame_total],
            tap_weights(weight, tap_row, mel_count),
            (((1,), (1,)), ((), ())),
            preferred_element_type=jnp.float32,
        )
    return running.reshape(frame_total, mel_count, width_out)


def weight_grad(source, grad):
    frame_total, mel_count, width_in = source.shape
    width_out = grad.shape[2]
    flat_rows = jnp.pad(source.reshape(frame_total, mel_count * width_in), ((1, 1), (0, 0)))
    grad_flat = grad.reshape(frame_total, mel_count * width_out)
    tap_list = []
    for tap_row in range(3):
        product = lax.dot_general(
            grad_flat,
            flat_rows[tap_row : tap_row + frame_total],
            (((0,), (0,)), ((), ())),
            preferred_element_type=jnp.float32,
        )
        product = product.reshape(mel_count, width_out, mel_count, width_in)
        for offset in range(3):
            summed = jnp.zeros((width_out, width_in), jnp.float32)
            for mel_out in range(mel_count):
                mel_in = mel_out + offset - 1
                if 0 <= mel_in < mel_count:
                    summed = summed + product[mel_out, :, mel_in, :]
            tap_list.append(summed)
    return jnp.stack(tap_list, axis=1)


def transposed(grad_padded, weight, row_count, mel_count):
    width_in = weight.shape[2]
    running = jnp.zeros((row_count, mel_count * width_in), jnp.float32)
    for tap_row in range(3):
        running = running + jnp.dot(
            grad_padded[2 - tap_row : 2 - tap_row + row_count],
            tap_weights(weight, tap_row, mel_count),
            preferred_element_type=jnp.float32,
        )
    return running.reshape(row_count, mel_count, width_in)


def standardize(before, total_sum, total_square, pixel_total):
    average = total_sum / pixel_total
    variance = total_square / pixel_total - average * average
    inv_std = lax.rsqrt(variance + 1e-05)
    return ((before - average) * inv_std, inv_std)


def gathered(
    features,
    lengths,
    conv1_weight,
    norm1_gain,
    norm1_bias,
    conv2_weight,
    norm2_gain,
    norm2_bias,
    out_grad,
):
    tm_devices = lax.axis_size("tm")
    frames_dev = features.shape[1]
    mel_count = features.shape[2]
    frame_total = frames_dev * tm_devices
    clip_count = lengths.shape[1] // 3
    valid_mask = frame_valid(lengths[0], frame_total, clip_count).astype(jnp.float32)[:, None, None]
    valid_low = valid_mask.astype(jnp.bfloat16)

    def fetch_frames():
        return lax.all_gather(features, "tm", axis=1, tiled=True)[0] * valid_low

    def fetch_units(local_units):
        return lax.all_gather(local_units, "tm", axis=2, tiled=True)

    masked = fetch_frames()
    weight_one, weight_two = (
        lax.all_gather(conv1_weight, "batch", axis=2, tiled=True),
        lax.all_gather(conv2_weight, "batch", axis=2, tiled=True),
    )
    pre_one = convolve(masked, weight_one)
    local_total = jnp.sum(lengths.astype(jnp.float32)) * mel_count
    sum_one, square_one, pixel_total = lax.psum(
        (
            jnp.sum(pre_one * valid_mask, axis=(0, 1)),
            jnp.sum(pre_one * pre_one * valid_mask, axis=(0, 1)),
            local_total,
        ),
        "batch",
    )
    scaled_one, rstd_one = standardize(pre_one, sum_one, square_one, pixel_total)
    before_one = norm1_gain * scaled_one + norm1_bias
    hidden = (valid_mask * jax.nn.silu(before_one)).astype(jnp.bfloat16)
    hidden_all = fetch_units(hidden)
    pre_two = convolve(hidden_all, weight_two)
    sum_two, square_two = lax.psum(
        (
            jnp.sum(pre_two * valid_mask, axis=(0, 1)),
            jnp.sum(pre_two * pre_two * valid_mask, axis=(0, 1)),
        ),
        "batch",
    )
    scaled_two, rstd_two = standardize(pre_two, sum_two, square_two, pixel_total)
    before_two = norm2_gain * scaled_two + norm2_bias
    output_local = (valid_mask * jax.nn.silu(before_two)).astype(jnp.bfloat16)
    block_out = lax.all_to_all(output_local[None], "tm", split_axis=1, concat_axis=3, tiled=True)
    grad_local = lax.all_to_all(out_grad, "tm", split_axis=3, concat_axis=1, tiled=True)[0]
    delta_two = grad_local.astype(jnp.float32) * valid_mask * silu_slope(before_two)
    gain2_grad, bias2_grad = lax.psum(
        (jnp.sum(delta_two * scaled_two, axis=(0, 1)), jnp.sum(delta_two, axis=(0, 1))), "batch"
    )
    grad_two = (
        valid_mask
        * norm2_gain
        * rstd_two
        * (delta_two - (bias2_grad + scaled_two * gain2_grad) / pixel_total)
    ).astype(jnp.bfloat16)
    units_again = fetch_units(hidden)
    frames_again = fetch_frames()
    conv2_local = weight_grad(units_again, grad_two)
    padded_two = jnp.pad(grad_two.reshape(frame_total, -1), ((1, 1), (0, 0)))
    partial_terms = transposed(padded_two, weight_two, frame_total, mel_count)
    hidden_grad = lax.psum_scatter(
        partial_terms.astype(jnp.bfloat16), "tm", scatter_dimension=2, tiled=True
    ).astype(jnp.float32)
    delta_one = hidden_grad * valid_mask * silu_slope(before_one)
    gain1_grad, bias1_grad = lax.psum(
        (jnp.sum(delta_one * scaled_one, axis=(0, 1)), jnp.sum(delta_one, axis=(0, 1))), "batch"
    )
    grad_one = (
        valid_mask
        * norm1_gain
        * rstd_one
        * (delta_one - (bias1_grad + scaled_one * gain1_grad) / pixel_total)
    ).astype(jnp.bfloat16)
    conv1_local = weight_grad(frames_again, grad_one)
    conv1_grad, conv2_grad = (
        lax.psum_scatter(
            conv1_local.astype(jnp.bfloat16), "batch", scatter_dimension=2, tiled=True
        ).astype(jnp.float32),
        lax.psum_scatter(
            conv2_local.astype(jnp.bfloat16), "batch", scatter_dimension=2, tiled=True
        ).astype(jnp.float32),
    )
    padded_one = jnp.pad(grad_one.reshape(frame_total, -1), ((1, 1), (0, 0)))
    input_dev = lax.psum_scatter(
        transposed(padded_one, weight_one, frames_dev * lax.axis_size("tm"), mel_count).astype(
            jnp.bfloat16
        ),
        "tm",
        scatter_dimension=0,
        tiled=True,
    ).astype(jnp.float32)
    own_mask = lax.dynamic_slice_in_dim(
        valid_mask, lax.axis_index("tm") * frames_dev, frames_dev, 0
    )
    input_grad = (input_dev * own_mask).astype(jnp.bfloat16)[None]
    return (
        block_out,
        input_grad,
        conv1_grad,
        gain1_grad,
        bias1_grad,
        conv2_grad,
        gain2_grad,
        bias2_grad,
    )


NT = (((1,), (1,)), ((), ()))
NN = (((1,), (0,)), ((), ()))
TN = (((0,), (0,)), ((), ()))
CHIPS, PLANES, MELS = 4, 4, 2


def mxu(a, b, dims):
    return lax.dot_general(a, b, dims, preferred_element_type=f32)


def vmem(mib):
    return pltpu.CompilerParams(vmem_limit_bytes=mib << 20)


def same(*shape):
    return pl.BlockSpec(shape, lambda *_: (0,) * len(shape))


def rolled(value, shift):
    shift %= value.shape[0]
    return pltpu.roll(value, shift, 0) if shift else value


def taps1_kernel(pos, w, out):
    def half(tap, rx):
        low, high = w[0, tap, :64, :], w[0, tap, 64:, :]
        return jnp.where(pos[2] == rx, low, high)

    for rx in range(2):
        for mo in range(MELS):
            for mi in range(MELS):
                row = rx * 128 + mo * 64
                out[0, row : row + 64, mi * 128 : mi * 128 + 128] = half(mi - mo + 1, rx)


def taps1(pos, w):
    spec = pltpu.PrefetchScalarGridSpec(
        num_scalar_prefetch=1,
        grid=(3, 4),
        in_specs=[
            pl.BlockSpec(
                (1, 3, 128, 128),
                lambda a, t, p: (2 * (p[1] ^ (t % 2)) + (p[0] ^ (t // 2)), a, 0, 0),
            )
        ],
        out_specs=pl.BlockSpec((1, 256, 256), lambda a, t, p: (a, 0, t)),
    )
    return pl.pallas_call(
        taps1_kernel, grid_spec=spec, out_shape=jax.ShapeDtypeStruct((3, 256, 1024), bf16)
    )(pos, w)


def taps2_kernel(pos, w, out):
    part = w.shape[1]
    low = lax.broadcasted_iota(jnp.int32, (part, 128), 1) < 64
    straight, turned = [], []
    for tap in range(3):
        value = w[tap].astype(f32)
        other = pltpu.roll(value, 64, 1)
        straight.append(jnp.where(pos[2] == 0, value, other))
        turned.append(jnp.where(pos[2] == 0, other, value))
    for mo in range(MELS):
        first, second = 1 - mo, 2 - mo
        rows = slice(mo * part, (mo + 1) * part)
        out[0, rows, :128] = jnp.where(low, straight[first], turned[second]).astype(bf16)
        out[0, rows, 128:] = jnp.where(low, turned[first], straight[second]).astype(bf16)


def taps2(pos, w):
    part = w.shape[1]
    spec = pltpu.PrefetchScalarGridSpec(
        num_scalar_prefetch=1,
        grid=(3, 4),
        in_specs=[
            pl.BlockSpec(
                (3, part, 128),
                lambda a, t, p: (a, 0, 2 * (p[0] ^ (t // 2)) + (p[1] ^ (t % 2))),
            )
        ],
        out_specs=pl.BlockSpec((1, MELS * part, 256), lambda a, t, p: (a, 0, t)),
    )
    return pl.pallas_call(
        taps2_kernel, grid_spec=spec, out_shape=jax.ShapeDtypeStruct((3, 2 * part, 1024), bf16)
    )(pos, w)


def conv_kernel(pieces, splits, *refs):
    xs, w, outs = refs[:pieces], refs[pieces], refs[pieces + 1 :]
    total = None
    for a in (1, 0, 2):
        z, start = None, 0
        for x in xs:
            width = x.shape[1]
            term = mxu(x[...], w[a, :, start : start + width], NT)
            z, start = term if z is None else z + term, start + width
        z = rolled(z, 1 - a)
        total = z if total is None else total + z
    start = 0
    for out in outs:
        out[...] = total[:, start : start + out.shape[1]].astype(out.dtype)
        start += out.shape[1]


def conv(xs, w, kinds, tile):
    rows, (_, width, depth) = xs[0].shape[0], w.shape
    lanes = tile // len(kinds)
    outs = [jax.ShapeDtypeStruct((rows, width // len(kinds)), kind) for kind in kinds]
    flops = 2 * 3 * rows * width * depth
    return pl.pallas_call(
        functools.partial(conv_kernel, len(xs), len(kinds)),
        grid=(width // tile,),
        in_specs=[same(*x.shape) for x in xs]
        + [pl.BlockSpec((3, tile, depth), lambda i: (0, i, 0))],
        out_specs=[pl.BlockSpec((rows, lanes), lambda i: (0, i)) for _ in kinds],
        out_shape=outs,
        compiler_params=vmem(32),
        cost_estimate=pl.CostEstimate(
            flops=flops, bytes_accessed=2 * rows * depth + 6 * width * depth, transcendentals=0
        ),
    )(*xs, w)


def spread_rows(dst, at, value, width, lane):
    rows, lanes = value.shape
    wide = value.astype(f32)
    for a in range(3):
        moved = value if a == 1 else rolled(wide, a - 1).astype(bf16)
        dst[at : at + rows, a * width + lane : a * width + lane + lanes] = moved


def conv_t_kernel(pieces, *refs):
    dys, w = refs[:pieces], refs[pieces]
    keep, send, moved = refs[pieces + 1 :]
    width = moved.shape[1] // 3
    step = pl.program_id(0)

    @pl.when(step == 0)
    def _():
        lane = 0
        for dy in dys:
            spread_rows(moved, 0, dy[...], width, lane)
            lane += dy.shape[1]

    value = mxu(moved[...], w[...].reshape(3 * width, w.shape[2]), NN)

    @pl.when(step == 0)
    def _():
        send[...] = value.astype(send.dtype)

    @pl.when(step == 1)
    def _():
        keep[...] = value.astype(keep.dtype)


def conv_t(dys, w):
    rows, (_, width, depth) = dys[0].shape[0], w.shape
    half = depth // 2
    return pl.pallas_call(
        functools.partial(conv_t_kernel, len(dys)),
        grid=(2,),
        in_specs=[same(*dy.shape) for dy in dys]
        + [pl.BlockSpec((3, width, half), lambda i: (0, 0, 1 - i))],
        out_specs=[same(rows, half), same(rows, half)],
        out_shape=[
            jax.ShapeDtypeStruct((rows, half), f32),
            jax.ShapeDtypeStruct((rows, half), bf16),
        ],
        scratch_shapes=[pltpu.VMEM((rows, 3 * width), bf16)],
        compiler_params=vmem(32),
        cost_estimate=pl.CostEstimate(
            flops=6 * rows * width * depth,
            bytes_accessed=6 * rows * half + 6 * width * depth,
            transcendentals=0,
        ),
    )(*dys, w)


def grad2_place(pos, out, a, prod):
    part = prod.shape[0] // 2
    low = lax.broadcasted_iota(jnp.int32, (part, 128), 1) < 64

    def pick(mo, mi):
        block = prod[mo * part : (mo + 1) * part]
        u, v = block[:, :128], block[:, 128:]
        u, v = jnp.where(pos[2] == 0, u, v), jnp.where(pos[2] == 0, v, u)
        if mi == 0:
            return jnp.where(low, u, pltpu.roll(v, 64, 1))
        return jnp.where(low, pltpu.roll(u, 64, 1), v)

    out[3 * a] = pick(1, 0)
    out[3 * a + 1] = pick(0, 0) + pick(1, 1)
    out[3 * a + 2] = pick(0, 1)


def grad1_place(pos, out, a, prod):
    def pick(rx, mo, mi):
        return prod[rx * 128 + mo * 64 :][:64, mi * 128 : mi * 128 + 128]

    for tap in range(3):
        both = []
        for rx in range(2):
            terms = [pick(rx, mo, mo + tap - 1) for mo in range(MELS) if 0 <= mo + tap - 1 < MELS]
            both.append(functools.reduce(lambda x, y: x + y, terms))
        low = jnp.where(pos[2] == 0, both[0], both[1])
        high = jnp.where(pos[2] == 0, both[1], both[0])
        out[0, 3 * a + tap, :64, :] = low.astype(bf16)
        out[0, 3 * a + tap, 64:, :] = high.astype(bf16)


def grad_kernel(place, groups, pieces, columns, pos, *refs):
    dys = refs[: groups * pieces]
    xs = refs[groups * pieces : -3]
    out, moved, x = refs[-3:]
    width = moved.shape[1] // 3
    step = pl.program_id(0)
    rows = dys[0].shape[0]
    per_group = len(xs) // groups
    steps_each = 4 // per_group

    @pl.when(step == 0)
    def _():
        for r in range(groups):
            lane = 0
            for dy in dys[r * pieces : (r + 1) * pieces]:
                spread_rows(moved, r * rows, dy[...], width, lane)
                lane += dy.shape[1]

    for k in range(per_group):

        @pl.when(step // steps_each == k)
        def _():
            for r in range(groups):
                x[r * rows : (r + 1) * rows, :] = xs[r * per_group + k][...]

    for a in range(3):
        place(pos, out, a, mxu(moved[:, a * width : (a + 1) * width], x[...], TN))


def weight_grad_own(pos, dys, xs, place, out_shape, out_spec):
    groups, pieces, per_group = len(dys), len(dys[0]), len(xs[0])
    rows = dys[0][0].shape[0]
    width = sum(dy.shape[1] for dy in dys[0])
    steps_each = 4 // per_group

    def column(k):
        return lambda t, p: (0, jnp.clip(t - k * steps_each, 0, steps_each - 1))

    spec = pltpu.PrefetchScalarGridSpec(
        num_scalar_prefetch=1,
        grid=(4,),
        in_specs=[same(*dy.shape) for group in dys for dy in group]
        + [pl.BlockSpec((rows, 256), column(k)) for _ in xs for k in range(per_group)],
        out_specs=out_spec,
        scratch_shapes=[
            pltpu.VMEM((groups * rows, 3 * width), bf16),
            pltpu.VMEM((groups * rows, 256), bf16),
        ],
    )
    return pl.pallas_call(
        functools.partial(grad_kernel, place, groups, pieces, 256),
        grid_spec=spec,
        out_shape=out_shape,
        compiler_params=vmem(56),
        cost_estimate=pl.CostEstimate(
            flops=6 * groups * rows * width * 1024,
            bytes_accessed=2 * groups * rows * (width + 1024),
            transcendentals=0,
        ),
    )(pos, *[dy for group in dys for dy in group], *[x for group in xs for x in group])


def stationary(
    features,
    lengths,
    conv1_weight,
    norm1_gain,
    norm1_bias,
    conv2_weight,
    norm2_gain,
    norm2_bias,
    out_grad,
):
    n = 2 * CHIPS
    me, plane = lax.axis_index("tm"), lax.axis_index("batch")
    core, chip = me % 2, me // 2
    py, px = chip // 2, chip % 2
    pos = jnp.stack([core, py, px]).astype(jnp.int32)
    own_frames, _, width1 = features.shape[1:]
    frames = own_frames * n
    part = conv2_weight.shape[0]
    block = part // CHIPS
    clip_count = lengths.shape[1] // 3
    same_core = [[c + 2 * p for p in range(CHIPS)] for c in range(2)]
    groups = range(PLANES)
    X, Y = 2, 4

    def swap(x, bits):
        return lax.ppermute(x, "tm", [(i, i ^ bits) for i in range(n)])

    def along(x, shift):
        return lax.ppermute(x, "batch", [(z, (z + shift) % PLANES) for z in groups])

    def route(x, pairs):
        flat = [(a * PLANES + b, c * PLANES + d) for (a, b), (c, d) in pairs]
        return lax.ppermute(x, ("tm", "batch"), flat)

    def plane_sum(x):
        got = [
            lax.ppermute(x, "batch", [(z, z ^ s) for z in groups]) for s in range(1, PLANES)
        ]
        return (x + got[0]) + (got[1] + got[2])

    def gather_chips(x, x_first):
        lanes = x.shape[1]
        if x_first:
            pair = jnp.concatenate([x, swap(x, X)], axis=1)
            return jnp.concatenate([pair, swap(pair, Y)], axis=1)
        other = swap(x, Y)
        far = swap(jnp.concatenate([x, other], axis=1), X)
        return jnp.concatenate([x, far[:, :lanes], other, far[:, lanes:]], axis=1)

    def scatter_chips(x, x_first):
        lanes = x.shape[1] // 4
        parts = [x[:, k * lanes : (k + 1) * lanes] for k in range(4)]
        if x_first:
            keep, send = [parts[0], parts[2]], [parts[1], parts[3]]
        else:
            keep, send = [parts[0], parts[1]], [parts[2], parts[3]]
        got = swap(jnp.concatenate(send, axis=1).astype(bf16), X if x_first else Y)
        low = keep[0] + got[:, :lanes].astype(f32)
        high = (keep[1] + got[:, lanes:].astype(f32)).astype(bf16)
        return low + swap(high, Y if x_first else X).astype(f32)

    w1 = conv1_weight.transpose(1, 0, 2)
    w1 = w1.reshape(9, 2, part // 2, 2, conv1_weight.shape[2] // 2).transpose(1, 3, 0, 2, 4)
    w1 = w1.reshape(CHIPS, 9, part // 2, conv1_weight.shape[2] // 2)
    w1 = lax.all_to_all(w1, "tm", 0, 0, tiled=True, axis_index_groups=same_core)
    w1 = lax.all_to_all(w1, "batch", 0, 0, tiled=True)
    weights1 = taps1(pos, w1)
    weights2 = taps2(pos, conv2_weight.transpose(1, 0, 2))

    group_lengths = [lengths] + [along(lengths, s) for s in range(1, PLANES)]
    count = sum(jnp.sum(x.astype(f32)) for x in group_lengths) * MELS
    mask = [frame_valid(x[0], frames, clip_count).astype(f32)[:, None] for x in group_lengths]
    here_valid = lax.dynamic_slice_in_dim(
        mask[0].astype(bf16), me * own_frames, own_frames, 0
    )

    own_norm = jnp.stack([norm1_gain, norm1_bias]).reshape(2, CHIPS, block)

    def norm_block(k):
        return lax.dynamic_index_in_dim(own_norm, k, 1, keepdims=False)

    both1 = jnp.where(chip == plane, norm_block(chip), 0.0)
    for s in range(1, CHIPS):
        both1 += route(
            norm_block(plane ^ s),
            [((2 * j + c, j), (2 * (j ^ s) + c, j)) for j in groups for c in range(2)],
        )
    gain1, bias1 = both1[0], both1[1]

    lanes1 = width1 // n
    masked = features[0] * here_valid[:, :, None]
    masked = masked.reshape(own_frames, MELS, 2, 2, 2, lanes1).transpose(2, 4, 3, 0, 1, 5)
    masked = masked.reshape(frames, MELS * lanes1)
    mine = [lax.all_to_all(masked, "tm", 0, 0, tiled=True)]
    for _ in range(PLANES - 1):
        mine.append(along(mine[-1], 1))
    inputs = []
    for x in mine:
        near = swap(x, Y)
        inputs.append([x, near, swap(x, 1), swap(near, 1)])

    pre1 = []
    for x in inputs:
        keep, send = conv(x, weights1, (f32, bf16), 256)
        pre1.append(keep + swap(send, X).astype(f32))

    def per_channel(x):
        return jnp.sum(x.reshape(MELS, -1), axis=0)

    def per_lane(x):
        return jnp.tile(x, MELS)[None]

    def rows_sum(x):
        return jnp.sum(x, axis=0)

    def norm_stats(total, square_total):
        average = total / count
        variance = square_total / count - average * average
        return average, lax.rsqrt(variance + 1e-05)

    sums = sum(rows_sum(x * v) for x, v in zip(pre1, mask))
    squares = sum(rows_sum(x * x * v) for x, v in zip(pre1, mask))
    mean1, rstd1 = norm_stats(per_channel(sums), per_channel(squares))
    xhat1 = [(x - per_lane(mean1)) * per_lane(rstd1) for x in pre1]
    z1 = [per_lane(gain1) * x + per_lane(bias1) for x in xhat1]
    act1 = [(v * jax.nn.silu(z)).astype(bf16) for v, z in zip(mask, z1)]

    hidden = [None] * PLANES
    total = None
    for r in (1, 2, 3, 0):
        half = gather_chips(act1[r], r % 2 == 1)
        hidden[r] = [half, swap(half, 1)]
        (term,) = conv(hidden[r], weights2, (bf16 if r == 1 else f32,), 512)
        total = term if r == 1 else term + along(total.astype(bf16), 1).astype(f32)
    pre2, v0 = total, mask[0]

    sums2 = jnp.stack([rows_sum(pre2 * v0), rows_sum(pre2 * pre2 * v0)])
    sums2 = plane_sum(sums2.reshape(2, MELS, part).sum(axis=1))
    mean2, rstd2 = norm_stats(sums2[0], sums2[1])
    xhat2 = (pre2 - per_lane(mean2)) * per_lane(rstd2)
    z2 = per_lane(norm2_gain) * xhat2 + per_lane(norm2_bias)

    grad_in = out_grad[0].reshape(own_frames, MELS, n, part).transpose(2, 0, 1, 3)
    grad_in = lax.all_to_all(grad_in, "tm", 0, 0, tiled=True).reshape(frames, MELS * part)
    dz2 = grad_in.astype(f32) * v0 * silu_slope(z2)
    grads2 = jnp.stack([rows_sum(dz2), rows_sum(dz2 * xhat2)])
    grads2 = plane_sum(grads2.reshape(2, MELS, part).sum(axis=1))
    bias2_grad, gain2_grad = grads2[0], grads2[1]
    dpre2 = (
        v0
        * per_lane(norm2_gain * rstd2)
        * (dz2 - (per_lane(bias2_grad) + xhat2 * per_lane(gain2_grad)) / count)
    ).astype(bf16)

    dpre2, z2_later = lax.optimization_barrier((dpre2, z2))
    out_local = (v0 * jax.nn.silu(z2_later)).astype(bf16)
    block_out = lax.all_to_all(
        out_local.reshape(n, own_frames, MELS, part), "tm", 0, 0, tiled=True
    )
    block_out = block_out.transpose(1, 2, 0, 3).reshape(1, own_frames, MELS, n * part)

    grad2 = [dpre2]
    for _ in range(PLANES - 1):
        grad2.append(along(grad2[-1], 1))
    dact1 = []
    for r in groups:
        keep, send = conv_t([grad2[r]], weights2)
        dact1.append(scatter_chips(keep + swap(send, 1).astype(f32), r % 2 == 1))

    dz1 = [d * v * silu_slope(z) for d, v, z in zip(dact1, mask, z1)]
    bias1_sum = per_channel(sum(rows_sum(d) for d in dz1))
    gain1_sum = per_channel(sum(rows_sum(d * x) for d, x in zip(dz1, xhat1)))
    dpre1 = [
        (
            v
            * per_lane(gain1 * rstd1)
            * (d - (per_lane(bias1_sum) + x * per_lane(gain1_sum)) / count)
        ).astype(bf16)
        for v, d, x in zip(mask, dz1, xhat1)
    ]
    pairs1, total = [None] * PLANES, None
    for r in (1, 2, 3, 0):
        pairs1[r] = [dpre1[r], swap(dpre1[r], X)]
        keep, send = conv_t(pairs1[r], weights1)
        half = keep + swap(send, 1).astype(f32)
        lanes = half.shape[1] // 2
        term = half[:, :lanes] + swap(half[:, lanes:].astype(bf16), Y).astype(f32)
        total = term if r == 1 else term + along(total.astype(bf16), 1).astype(f32)
    dx = total.astype(bf16).reshape(n, own_frames, MELS * lanes1)
    dx = lax.all_to_all(dx, "tm", 0, 0, tiled=True)
    dx = dx.reshape(2, 2, 2, own_frames, MELS, lanes1).transpose(3, 4, 0, 2, 1, 5)
    input_grad = dx.reshape(1, own_frames, MELS, width1) * here_valid[None, :, :, None]

    grad1 = weight_grad_own(
        pos,
        pairs1,
        inputs,
        grad1_place,
        jax.ShapeDtypeStruct((PLANES, 9, part // 2, 128), bf16),
        pl.BlockSpec(
            (1, 9, part // 2, 128),
            lambda t, p: (2 * (p[1] ^ (t % 2)) + (p[0] ^ (t // 2)), 0, 0, 0),
        ),
    )
    grad1 = lax.all_to_all(grad1, "batch", 0, 0, tiled=True)
    grad1_sent = lax.all_to_all(grad1, "tm", 0, 0, tiled=True, axis_index_groups=same_core)
    conv1_grad = grad1_sent.reshape(2, 2, 9, part // 2, -1).transpose(2, 0, 3, 1, 4)
    conv1_grad = conv1_grad.reshape(9, part, -1).astype(f32).transpose(1, 0, 2)

    conv2_grad = weight_grad_own(
        pos,
        [[g] for g in grad2],
        hidden,
        grad2_place,
        jax.ShapeDtypeStruct((9, part, conv2_weight.shape[2]), f32),
        pl.BlockSpec(
            (9, part, 128),
            lambda t, p: (0, 0, 2 * (p[0] ^ (t // 2)) + (p[1] ^ (t % 2))),
        ),
    ).transpose(1, 0, 2)

    mine1 = jnp.stack([gain1_sum, bias1_sum])
    parts1 = [mine1] + [
        route(mine1, [((2 * (j ^ s) + c, j), (2 * j + c, j)) for j in groups for c in range(2)])
        for s in range(1, CHIPS)
    ]
    whole1 = jnp.stack(parts1, axis=1).reshape(2, 2, 2, block)
    whole1 = jnp.where(plane // 2 == 1, jnp.flip(whole1, 1), whole1)
    whole1 = jnp.where(plane % 2 == 1, jnp.flip(whole1, 2), whole1).reshape(2, part)
    grads1 = jnp.where(chip == plane, whole1, 0.0)
    for s in range(1, PLANES):
        grads1 += route(
            whole1,
            [((2 * j + c, j), (2 * j + c, (j + s) % PLANES)) for j in groups for c in range(2)],
        )
    gain1_grad, bias1_grad = grads1[0], grads1[1]

    return (
        block_out,
        input_grad,
        conv1_grad,
        gain1_grad,
        bias1_grad,
        conv2_grad,
        gain2_grad,
        bias2_grad,
    )


def solution(mesh):
    return jax.shard_map(
        stationary if dict(mesh.shape) == {"tm": 8, "batch": 4} else gathered,
        mesh=mesh,
        in_specs=(
            P("batch", "tm", None, None),
            P("batch", None),
            P("tm", None, "batch"),
            P("tm"),
            P("tm"),
            P("tm", None, "batch"),
            P("tm"),
            P("tm"),
            P("batch", "tm", None, None),
        ),
        out_specs=(
            P("batch", "tm", None, None),
            P("batch", "tm", None, None),
            P("tm", None, "batch"),
            P("tm"),
            P("tm"),
            P("tm", None, "batch"),
            P("tm"),
            P("tm"),
        ),
        check_vma=False,
    )
```

```python
import functools

import jax
import jax.numpy as jnp
from jax import lax
from jax.experimental import pallas as pl
from jax.experimental.pallas import tpu as pltpu
from jax.sharding import PartitionSpec as P

f32, bf16 = jnp.float32, jnp.bfloat16


def frame_valid(lengths_row, frame_total, clip_count):
    frame_ids = jnp.arange(frame_total, dtype=jnp.int32)
    first_end = 16 * clip_count
    second_end = 48 * clip_count
    clip_index = jnp.where(
        frame_ids < first_end,
        frame_ids // 16,
        jnp.where(
            frame_ids < second_end,
            clip_count + (frame_ids - first_end) // 32,
            2 * clip_count + (frame_ids - second_end) // 64,
        ),
    )
    offset = jnp.where(
        frame_ids < first_end,
        frame_ids % 16,
        jnp.where(
            frame_ids < second_end, (frame_ids - first_end) % 32, (frame_ids - second_end) % 64
        ),
    )
    clip_ids = jnp.arange(3 * clip_count, dtype=jnp.int32)
    picked = jnp.where(
        clip_index[:, None] == clip_ids[None, :], lengths_row[None, :], jnp.zeros((), jnp.int32)
    )
    length_here = jnp.sum(picked, axis=1)
    return offset < length_here


def silu_slope(value):
    sigma = jax.nn.sigmoid(value)
    return sigma * (1.0 + value * (1.0 - sigma))


def tap_weights(weight, tap_row, mel_count):
    row_blocks = []
    for mel_out in range(mel_count):
        col_blocks = []
        for mel_in in range(mel_count):
            offset = mel_in - mel_out + 1
            col_blocks.append(weight[:, 3 * tap_row + offset, :])
        row_blocks.append(jnp.concatenate(col_blocks, axis=1))
    return jnp.concatenate(row_blocks, axis=0)


def convolve(source, weight):
    frame_total, mel_count, width_in = source.shape
    width_out = weight.shape[0]
    flat_rows = jnp.pad(source.reshape(frame_total, mel_count * width_in), ((1, 1), (0, 0)))
    running = jnp.zeros((frame_total, mel_count * width_out), jnp.float32)
    for tap_row in range(3):
        running = running + lax.dot_general(
            flat_rows[tap_row : tap_row + frame_total],
            tap_weights(weight, tap_row, mel_count),
            (((1,), (1,)), ((), ())),
            preferred_element_type=jnp.float32,
        )
    return running.reshape(frame_total, mel_count, width_out)


def weight_grad(source, grad):
    frame_total, mel_count, width_in = source.shape
    width_out = grad.shape[2]
    flat_rows = jnp.pad(source.reshape(frame_total, mel_count * width_in), ((1, 1), (0, 0)))
    grad_flat = grad.reshape(frame_total, mel_count * width_out)
    tap_list = []
    for tap_row in range(3):
        product = lax.dot_general(
            grad_flat,
            flat_rows[tap_row : tap_row + frame_total],
            (((0,), (0,)), ((), ())),
            preferred_element_type=jnp.float32,
        )
        product = product.reshape(mel_count, width_out, mel_count, width_in)
        for offset in range(3):
            summed = jnp.zeros((width_out, width_in), jnp.float32)
            for mel_out in range(mel_count):
                mel_in = mel_out + offset - 1
                if 0 <= mel_in < mel_count:
                    summed = summed + product[mel_out, :, mel_in, :]
            tap_list.append(summed)
    return jnp.stack(tap_list, axis=1)


def transposed(grad_padded, weight, row_count, mel_count):
    width_in = weight.shape[2]
    running = jnp.zeros((row_count, mel_count * width_in), jnp.float32)
    for tap_row in range(3):
        running = running + jnp.dot(
            grad_padded[2 - tap_row : 2 - tap_row + row_count],
            tap_weights(weight, tap_row, mel_count),
            preferred_element_type=jnp.float32,
        )
    return running.reshape(row_count, mel_count, width_in)


def standardize(before, total_sum, total_square, pixel_total):
    average = total_sum / pixel_total
    variance = total_square / pixel_total - average * average
    inv_std = lax.rsqrt(variance + 1e-05)
    return ((before - average) * inv_std, inv_std)


def gathered(
    features,
    lengths,
    conv1_weight,
    norm1_gain,
    norm1_bias,
    conv2_weight,
    norm2_gain,
    norm2_bias,
    out_grad,
):
    tm_devices = lax.axis_size("tm")
    frames_dev = features.shape[1]
    mel_count = features.shape[2]
    frame_total = frames_dev * tm_devices
    clip_count = lengths.shape[1] // 3
    valid_mask = frame_valid(lengths[0], frame_total, clip_count).astype(jnp.float32)[:, None, None]
    valid_low = valid_mask.astype(jnp.bfloat16)

    def fetch_frames():
        return lax.all_gather(features, "tm", axis=1, tiled=True)[0] * valid_low

    def fetch_units(local_units):
        return lax.all_gather(local_units, "tm", axis=2, tiled=True)

    masked = fetch_frames()
    weight_one, weight_two = (
        lax.all_gather(conv1_weight, "batch", axis=2, tiled=True),
        lax.all_gather(conv2_weight, "batch", axis=2, tiled=True),
    )
    pre_one = convolve(masked, weight_one)
    local_total = jnp.sum(lengths.astype(jnp.float32)) * mel_count
    sum_one, square_one, pixel_total = lax.psum(
        (
            jnp.sum(pre_one * valid_mask, axis=(0, 1)),
            jnp.sum(pre_one * pre_one * valid_mask, axis=(0, 1)),
            local_total,
        ),
        "batch",
    )
    scaled_one, rstd_one = standardize(pre_one, sum_one, square_one, pixel_total)
    before_one = norm1_gain * scaled_one + norm1_bias
    hidden = (valid_mask * jax.nn.silu(before_one)).astype(jnp.bfloat16)
    hidden_all = fetch_units(hidden)
    pre_two = convolve(hidden_all, weight_two)
    sum_two, square_two = lax.psum(
        (
            jnp.sum(pre_two * valid_mask, axis=(0, 1)),
            jnp.sum(pre_two * pre_two * valid_mask, axis=(0, 1)),
        ),
        "batch",
    )
    scaled_two, rstd_two = standardize(pre_two, sum_two, square_two, pixel_total)
    before_two = norm2_gain * scaled_two + norm2_bias
    output_local = (valid_mask * jax.nn.silu(before_two)).astype(jnp.bfloat16)
    block_out = lax.all_to_all(output_local[None], "tm", split_axis=1, concat_axis=3, tiled=True)
    grad_local = lax.all_to_all(out_grad, "tm", split_axis=3, concat_axis=1, tiled=True)[0]
    delta_two = grad_local.astype(jnp.float32) * valid_mask * silu_slope(before_two)
    gain2_grad, bias2_grad = lax.psum(
        (jnp.sum(delta_two * scaled_two, axis=(0, 1)), jnp.sum(delta_two, axis=(0, 1))), "batch"
    )
    grad_two = (
        valid_mask
        * norm2_gain
        * rstd_two
        * (delta_two - (bias2_grad + scaled_two * gain2_grad) / pixel_total)
    ).astype(jnp.bfloat16)
    units_again = fetch_units(hidden)
    frames_again = fetch_frames()
    conv2_local = weight_grad(units_again, grad_two)
    padded_two = jnp.pad(grad_two.reshape(frame_total, -1), ((1, 1), (0, 0)))
    partial_terms = transposed(padded_two, weight_two, frame_total, mel_count)
    hidden_grad = lax.psum_scatter(
        partial_terms.astype(jnp.bfloat16), "tm", scatter_dimension=2, tiled=True
    ).astype(jnp.float32)
    delta_one = hidden_grad * valid_mask * silu_slope(before_one)
    gain1_grad, bias1_grad = lax.psum(
        (jnp.sum(delta_one * scaled_one, axis=(0, 1)), jnp.sum(delta_one, axis=(0, 1))), "batch"
    )
    grad_one = (
        valid_mask
        * norm1_gain
        * rstd_one
        * (delta_one - (bias1_grad + scaled_one * gain1_grad) / pixel_total)
    ).astype(jnp.bfloat16)
    conv1_local = weight_grad(frames_again, grad_one)
    conv1_grad, conv2_grad = (
        lax.psum_scatter(
            conv1_local.astype(jnp.bfloat16), "batch", scatter_dimension=2, tiled=True
        ).astype(jnp.float32),
        lax.psum_scatter(
            conv2_local.astype(jnp.bfloat16), "batch", scatter_dimension=2, tiled=True
        ).astype(jnp.float32),
    )
    padded_one = jnp.pad(grad_one.reshape(frame_total, -1), ((1, 1), (0, 0)))
    input_dev = lax.psum_scatter(
        transposed(padded_one, weight_one, frames_dev * lax.axis_size("tm"), mel_count).astype(
            jnp.bfloat16
        ),
        "tm",
        scatter_dimension=0,
        tiled=True,
    ).astype(jnp.float32)
    own_mask = lax.dynamic_slice_in_dim(
        valid_mask, lax.axis_index("tm") * frames_dev, frames_dev, 0
    )
    input_grad = (input_dev * own_mask).astype(jnp.bfloat16)[None]
    return (
        block_out,
        input_grad,
        conv1_grad,
        gain1_grad,
        bias1_grad,
        conv2_grad,
        gain2_grad,
        bias2_grad,
    )


NT = (((1,), (1,)), ((), ()))
NN = (((1,), (0,)), ((), ()))
TN = (((0,), (0,)), ((), ()))
CHIPS, PLANES, MELS = 4, 4, 2


def mxu(a, b, dims):
    return lax.dot_general(a, b, dims, preferred_element_type=f32)


def vmem(mib):
    return pltpu.CompilerParams(vmem_limit_bytes=mib << 20)


def same(*shape):
    return pl.BlockSpec(shape, lambda *_: (0,) * len(shape))


def cost(flops, bytes_accessed):
    return pl.CostEstimate(flops=flops, bytes_accessed=bytes_accessed, transcendentals=0)


def rolled(value, shift):
    shift %= value.shape[0]
    return pltpu.roll(value, shift, 0) if shift else value


def taps1_kernel(pos, own, other, out):
    for t in range(4):
        source = 2 * (pos[1] ^ (t // 2)) + t % 2
        for rx in range(2):
            for tap in range(9):
                value = jnp.where(
                    pos[0] ^ pos[2] == rx, own[source, tap], other[source, tap]
                )
                a, b = tap // 3, tap % 3
                for mo in range(MELS):
                    mi = mo + b - 1
                    if 0 <= mi < MELS:
                        row, lane = rx * 256 + mo * 128, t * 256 + mi * 128
                        out[a, row : row + 128, lane : lane + 128] = value


def taps1(pos, own, other):
    spec = pltpu.PrefetchScalarGridSpec(
        num_scalar_prefetch=1,
        grid=(1,),
        in_specs=[same(*own.shape), same(*own.shape)],
        out_specs=same(3, 512, 1024),
    )
    return pl.pallas_call(
        taps1_kernel,
        grid_spec=spec,
        out_shape=jax.ShapeDtypeStruct((3, 512, 1024), bf16),
        compiler_params=vmem(24),
    )(pos, own, other)


def taps2_kernel(pos, own, other, out):
    part = own.shape[1]
    for core, w in enumerate((own, other)):
        for a in range(3):
            for mo in range(MELS):
                row = (core * MELS + mo) * part
                for mi in range(MELS):
                    lane = mi * 128
                    out[a, row : row + part, lane : lane + 128] = w[3 * a + mi - mo + 1]


def taps2(pos, own, other):
    part = own.shape[1]
    source = pl.BlockSpec(
        (9, part, 128), lambda t, p: (0, 0, 2 * (p[2] ^ (t % 2)) + (p[1] ^ (t // 2)))
    )
    spec = pltpu.PrefetchScalarGridSpec(
        num_scalar_prefetch=1,
        grid=(4,),
        in_specs=[source, source],
        out_specs=pl.BlockSpec((3, 4 * part, 256), lambda t, p: (0, 0, t)),
    )
    return pl.pallas_call(
        taps2_kernel,
        grid_spec=spec,
        out_shape=jax.ShapeDtypeStruct((3, 4 * part, 1024), bf16),
        compiler_params=vmem(24),
    )(pos, own, other)


def quarters_kernel(pos, *refs):
    quads, out = refs[:4], refs[4]
    taps, half, lanes = quads[0].shape
    for k in range(4):
        row = pl.multiple_of((pos[1] ^ (k // 2)) * half, half)
        lane = pl.multiple_of((pos[2] ^ (k % 2)) * lanes, lanes)
        out[:, pl.ds(row, half), pl.ds(lane, lanes)] = quads[k][...].astype(out.dtype)


def from_quarters(pos, quads):
    taps, half, lanes = quads[0].shape
    spec = pltpu.PrefetchScalarGridSpec(
        num_scalar_prefetch=1,
        grid=(3,),
        in_specs=[pl.BlockSpec((taps // 3, half, lanes), lambda i, p: (i, 0, 0))] * 4,
        out_specs=pl.BlockSpec((taps // 3, 2 * half, 2 * lanes), lambda i, p: (i, 0, 0)),
    )
    return pl.pallas_call(
        quarters_kernel,
        grid_spec=spec,
        out_shape=jax.ShapeDtypeStruct((taps, 2 * half, 2 * lanes), f32),
    )(pos, *quads)


def conv_kernel(pieces, *refs):
    xs, w, outs = refs[:pieces], refs[pieces], refs[pieces + 1 :]
    total = None
    for a in (1, 0, 2):
        z, start = None, 0
        for x in xs:
            width = x.shape[1]
            term = mxu(x[...], w[a, :, start : start + width], NT)
            z, start = term if z is None else z + term, start + width
        z = rolled(z, 1 - a)
        total = z if total is None else total + z
    start = 0
    for out in outs:
        out[...] = total[:, start : start + out.shape[1]].astype(out.dtype)
        start += out.shape[1]


def conv(xs, w, kinds, tile):
    rows, (_, width, depth) = xs[0].shape[0], w.shape
    lanes = tile // len(kinds)
    return pl.pallas_call(
        functools.partial(conv_kernel, len(xs)),
        grid=(width // tile,),
        in_specs=[same(*x.shape) for x in xs]
        + [pl.BlockSpec((3, tile, depth), lambda i: (0, i, 0))],
        out_specs=[pl.BlockSpec((rows, lanes), lambda i: (0, i)) for _ in kinds],
        out_shape=[jax.ShapeDtypeStruct((rows, width // len(kinds)), kind) for kind in kinds],
        compiler_params=vmem(32),
        cost_estimate=cost(6 * rows * width * depth, 2 * rows * depth + 6 * width * depth),
    )(*xs, w)


def spread_rows(dst, at, value, width, lane):
    rows, lanes = value.shape
    wide = value.astype(f32)
    for a in range(3):
        moved = value if a == 1 else rolled(wide, a - 1).astype(bf16)
        dst[at : at + rows, a * width + lane : a * width + lane + lanes] = moved


def conv_t_kernel(pieces, *refs):
    dys, w = refs[:pieces], refs[pieces]
    outs, moved = refs[pieces + 1 : -1], refs[-1]
    width = moved.shape[1] // 3
    step = pl.program_id(0)

    @pl.when(step == 0)
    def _():
        lane = 0
        for dy in dys:
            spread_rows(moved, 0, dy[...], width, lane)
            lane += dy.shape[1]

    value = mxu(moved[...], w[...].reshape(3 * width, w.shape[2]), NN)
    for k, out in enumerate(outs):

        @pl.when(step == k)
        def _():
            out[...] = value.astype(out.dtype)


def conv_t(dys, w, blocks):
    rows, (_, width, depth) = dys[0].shape[0], w.shape
    lanes = depth // blocks
    return pl.pallas_call(
        functools.partial(conv_t_kernel, len(dys)),
        grid=(blocks,),
        in_specs=[same(*dy.shape) for dy in dys]
        + [pl.BlockSpec((3, width, lanes), lambda i: (0, 0, i))],
        out_specs=[same(rows, lanes)] * blocks,
        out_shape=[
            jax.ShapeDtypeStruct((rows, lanes), bf16 if k else f32) for k in range(blocks)
        ],
        scratch_shapes=[pltpu.VMEM((rows, 3 * width), bf16)],
        compiler_params=vmem(32),
        cost_estimate=cost(6 * rows * width * depth, 3 * rows * depth + 6 * width * depth),
    )(*dys, w)


def grad2_place(pos, own, send, a, prod):
    part = prod.shape[0] // 4
    for core, out in enumerate((own, send)):
        first = prod[2 * core * part : (2 * core + 1) * part]
        second = prod[(2 * core + 1) * part : (2 * core + 2) * part]
        out[3 * a] = second[:, :128].astype(out.dtype)
        out[3 * a + 1] = (first[:, :128] + second[:, 128:]).astype(out.dtype)
        out[3 * a + 2] = first[:, 128:].astype(out.dtype)


def grad1_place(pos, own, send, a, prod):
    taps = []
    for rx in range(2):
        first, second = prod[rx * 256 : rx * 256 + 128], prod[rx * 256 + 128 :][:128]
        taps.append([second[:, :128], first[:, :128] + second[:, 128:], first[:, 128:]])
    for b in range(3):
        mine = pos[0] == pos[2]
        own[0, 3 * a + b] = jnp.where(mine, taps[0][b], taps[1][b])
        send[0, 3 * a + b] = jnp.where(mine, taps[1][b], taps[0][b]).astype(bf16)


def grad_kernel(place, groups, pieces, pos, *refs):
    dys = refs[: groups * pieces]
    xs = refs[groups * pieces : -4]
    own, send, moved, x = refs[-4:]
    width = moved.shape[1] // 3
    step = pl.program_id(0)
    rows = dys[0].shape[0]
    per_group = len(xs) // groups
    steps_each = 4 // per_group

    @pl.when(step == 0)
    def _():
        for r in range(groups):
            lane = 0
            for dy in dys[r * pieces : (r + 1) * pieces]:
                spread_rows(moved, r * rows, dy[...], width, lane)
                lane += dy.shape[1]

    for k in range(per_group):

        @pl.when(step // steps_each == k)
        def _():
            for r in range(groups):
                x[r * rows : (r + 1) * rows, :] = xs[r * per_group + k][...]

    for a in range(3):
        place(pos, own, send, a, mxu(moved[:, a * width : (a + 1) * width], x[...], TN))


def weight_grad_own(pos, dys, xs, place, shape, out_spec):
    groups, pieces, per_group = len(dys), len(dys[0]), len(xs[0])
    rows = dys[0][0].shape[0]
    width = sum(dy.shape[1] for dy in dys[0])
    steps_each = 4 // per_group

    def column(k):
        return lambda t, p: (0, jnp.clip(t - k * steps_each, 0, steps_each - 1))

    spec = pltpu.PrefetchScalarGridSpec(
        num_scalar_prefetch=1,
        grid=(4,),
        in_specs=[same(*dy.shape) for group in dys for dy in group]
        + [pl.BlockSpec((rows, 256), column(k)) for _ in xs for k in range(per_group)],
        out_specs=[out_spec, out_spec],
        scratch_shapes=[
            pltpu.VMEM((groups * rows, 3 * width), bf16),
            pltpu.VMEM((groups * rows, 256), bf16),
        ],
    )
    args = [dy for group in dys for dy in group] + [x for group in xs for x in group]
    return pl.pallas_call(
        functools.partial(grad_kernel, place, groups, pieces),
        grid_spec=spec,
        out_shape=[jax.ShapeDtypeStruct(shape, f32), jax.ShapeDtypeStruct(shape, bf16)],
        compiler_params=vmem(56),
        cost_estimate=cost(
            6 * groups * rows * width * 1024, 2 * groups * rows * (width + 1024)
        ),
    )(pos, *args)


def clip_places(lengths_row, half_rows):
    clips = lengths_row.shape[0]
    each = clips // 3

    def rank(axis):
        clip = lax.broadcasted_iota(jnp.int32, (clips, clips), axis)
        kind, place = clip // each, clip % each
        late = place >= each // 2
        long = jnp.where(late, place + 2 * each, place)
        middle = jnp.where(late, place + each + each // 2, place + each // 2)
        return jnp.where(kind == 2, long, jnp.where(kind == 1, middle, place + each))

    size = lengths_row[None, :] + 1
    before = jnp.sum(jnp.where(rank(1) < rank(0), size, 0), axis=1)
    late = before + lengths_row + 1 > half_rows
    taken = jnp.sum(jnp.where(late, 0, lengths_row + 1))
    return late.astype(jnp.int32), jnp.where(late, before - taken, before)


def halves_fit(lengths_row, half_rows):
    late, _ = clip_places(lengths_row, half_rows)
    return jnp.sum(late * (lengths_row + 1)) <= half_rows


def row_valid(lengths_row, core, half_rows):
    half, start = clip_places(lengths_row, half_rows)
    length = jnp.where(half == core, lengths_row, 0)[None, :]
    row = lax.broadcasted_iota(jnp.int32, (half_rows, lengths_row.shape[0]), 0)
    inside = (row >= start[None, :]) & (row < start[None, :] + length)
    return jnp.sum(inside.astype(f32), axis=1, keepdims=True)


def row_picker(lengths_row, core, half_rows, frames):
    clips = lengths_row.shape[0]
    clip = lax.broadcasted_iota(jnp.int32, (frames, clips), 1)
    frame = lax.broadcasted_iota(jnp.int32, (frames, clips), 0)
    each = clips // 3
    padded = jnp.where(clip < each, 16, jnp.where(clip < 2 * each, 32, 64))
    base = jnp.where(
        clip < each, 0, jnp.where(clip < 2 * each, 16 * each, 48 * each)
    ) + padded * (clip % each)
    offset = frame - base
    inside = (offset >= 0) & (offset < lengths_row[None, :])
    half, start = clip_places(lengths_row, half_rows)
    place = jnp.where(half == core, start, start + half_rows)
    target = jnp.sum(jnp.where(inside, place[None, :] + offset + 1, 0), axis=1)
    row = lax.broadcasted_iota(jnp.int32, (2 * half_rows, frames), 0)
    return (row + 1 == target[None, :]).astype(bf16)


def after(value, *others):
    return lax.optimization_barrier((value, *others))[0]


def stationary(
    features,
    lengths,
    conv1_weight,
    norm1_gain,
    norm1_bias,
    conv2_weight,
    norm2_gain,
    norm2_bias,
    out_grad,
):
    n = 2 * CHIPS
    own_frames, _, width1 = features.shape[1:]
    frames, lanes1 = own_frames * n, width1 // n

    sent = features[0].reshape(own_frames, MELS, 2, 2, 2, lanes1).transpose(2, 4, 3, 0, 1, 5)
    sent = sent.reshape(frames, MELS * lanes1)
    mine = lax.all_to_all(sent, "tm", 0, 0, tiled=True)
    every = [lengths[0]] + [
        lax.ppermute(lengths, "batch", [(z, (z + s) % PLANES) for z in range(PLANES)])[0]
        for s in range(1, PLANES)
    ]
    part, wide = conv1_weight.shape[0], conv1_weight.shape[2]
    quarters = conv1_weight.transpose(1, 0, 2).reshape(9, 2, part // 2, 2, wide // 2)
    quarters = quarters.transpose(1, 3, 0, 2, 4).reshape(CHIPS, 9, part // 2, wide // 2)
    half_rows = frames * 3 // 7
    fits = functools.reduce(jnp.logical_and, [halves_fit(x, half_rows) for x in every])
    return lax.cond(
        fits,
        functools.partial(on_rows, half_rows),
        functools.partial(on_rows, frames // 2),
        mine,
        jnp.stack(every),
        quarters,
        norm1_gain,
        norm1_bias,
        conv2_weight,
        norm2_gain,
        norm2_bias,
        out_grad,
    )


def on_rows(
    rows,
    mine,
    every,
    w1,
    norm1_gain,
    norm1_bias,
    conv2_weight,
    norm2_gain,
    norm2_bias,
    out_grad,
):
    n = 2 * CHIPS
    me, plane = lax.axis_index("tm"), lax.axis_index("batch")
    core, chip = me % 2, me // 2
    py, px = chip // 2, chip % 2
    pos = jnp.stack([core, py, px]).astype(jnp.int32)
    frames, lanes1 = mine.shape[0], mine.shape[1] // MELS
    own_frames, width1 = frames // n, n * lanes1
    part = conv2_weight.shape[0]
    half = part // 2
    same_core = [[c + 2 * p for p in range(CHIPS)] for c in range(2)]
    groups = range(PLANES)
    X, Y = 2, 4

    def swap(x, bits):
        return lax.ppermute(x, "tm", [(i, i ^ bits) for i in range(n)])

    def along(x, shift):
        return lax.ppermute(x, "batch", [(z, (z + shift) % PLANES) for z in groups])

    def route(x, pairs):
        flat = [(a * PLANES + b, c * PLANES + d) for (a, b), (c, d) in pairs]
        return lax.ppermute(x, ("tm", "batch"), flat)

    def plane_sum(x):
        got = [
            lax.ppermute(x, "batch", [(z, z ^ s) for z in groups]) for s in range(1, PLANES)
        ]
        return (x + got[0]) + (got[1] + got[2])

    def per_channel(x):
        return jnp.sum(x.reshape(MELS, -1), axis=0)

    def per_lane(x):
        return jnp.tile(x, MELS)[None]

    def rows_sum(x):
        return jnp.sum(x, axis=0)

    picker = row_picker(every[0], core, rows, frames)
    mask = [row_valid(every[r], core, rows) for r in groups]
    count = jnp.sum(every.astype(f32)) * MELS
    packed = mxu(picker, mine, NN).astype(bf16)
    other = swap(packed[rows:], 1)
    first = jnp.where(core == 0, packed[:rows], other)
    second = jnp.where(core == 0, other, packed[:rows])
    mine = [jnp.concatenate([first, second], axis=1)]

    w1 = lax.all_to_all(w1, "tm", 0, 0, tiled=True, axis_index_groups=same_core)
    w2 = conv2_weight.transpose(1, 0, 2)
    w2_other = swap(after(w2, mine[0]), 1)

    def norm_of_block(own_norm):
        both = 0.0
        for y in range(2):
            for c in range(2):
                both += route(
                    own_norm[:, y],
                    [((2 * j + x, j), (4 * y + 2 * x + c, j)) for j in groups for x in range(2)],
                )
        return both

    own_norm = jnp.stack([norm1_gain, norm1_bias]).reshape(2, 2, half)
    nears, both1, weights2 = [], None, None
    for r in groups:
        x = mine[r]
        ahead = along(x, 1) if r < PLANES - 1 else None
        nears.append(swap(x, Y))
        done = [nears[r]]
        if r == 1:
            w1 = lax.all_to_all(after(w1, x), "batch", 0, 0, tiled=True)
            weights2 = taps2(pos, w2, after(w2_other, x))
            done.append(weights2)
        if r == 2:
            both1 = norm_of_block(after(own_norm, x))
            done.append(both1)
        if ahead is not None:
            mine.append(after(ahead, *done))
    gain1, bias1 = both1[0], both1[1]

    w1 = after(w1, mine[3])
    weights1 = taps1(pos, w1, swap(w1, 1))
    inputs, pre1, send = [], [], None
    for r in groups:
        inputs.append([mine[r], nears[r] if r < 3 else after(nears[r], send)])
        xs = inputs[r] if r == 0 else [after(mine[r], send), inputs[r][1]]
        keep, send = conv(xs, weights1, (f32, bf16), 512)
        pre1.append(keep + swap(send, X).astype(f32))

    def norm_stats(total, square_total):
        average = total / count
        variance = square_total / count - average * average
        return average, lax.rsqrt(variance + 1e-05)

    def chip_sum(x):
        return x + swap(x, 1)

    sums = jnp.stack(
        [
            per_channel(sum(rows_sum(x * v) for x, v in zip(pre1, mask))),
            per_channel(sum(rows_sum(x * x * v) for x, v in zip(pre1, mask))),
        ]
    )
    sums = chip_sum(sums)
    mean1, rstd1 = norm_stats(sums[0], sums[1])
    xhat1 = [(x - per_lane(mean1)) * per_lane(rstd1) for x in pre1]
    z1 = [per_lane(gain1) * x + per_lane(bias1) for x in xhat1]
    act1 = [(v * jax.nn.silu(z)).astype(bf16) for v, z in zip(mask, z1)]

    hidden = [None] * PLANES
    payload, term, got, grad_in = None, None, None, None
    for r in (1, 2, 3, 0):
        x = act1[r] if r == 1 else after(act1[r], *got)
        got = [swap(x, X), swap(x, Y), swap(x, X + Y)]
        if r != 1:
            got[2] = after(got[2], term)
        hidden[r] = [x, *got]
        moved = None if r == 1 else along(payload, 1)
        (term,) = conv(hidden[r], weights2, (bf16 if r == 1 else f32,), 512)
        if r == 1:
            payload = term
            continue
        if r == 0:
            grad_in = mxu(picker, grad_in.reshape(frames, MELS * part), NN).astype(bf16)
            grad_in = jnp.concatenate([grad_in[:rows], swap(grad_in[rows:], 1)], axis=1)
            moved = after(moved, grad_in)
        total = term + after(moved, term).astype(f32)
        payload = total.astype(bf16)
        if r == 2:
            grad_in = after(out_grad, payload)[0].reshape(own_frames, MELS, n, part)
            grad_in = grad_in.transpose(2, 0, 1, 3)
            grad_in = lax.all_to_all(grad_in, "tm", 0, 0, tiled=True)
    pre2, v0 = total, mask[0]

    def all_rows(x, y):
        sums = jnp.stack([rows_sum(x), rows_sum(y)]).reshape(2, 2, MELS, part).sum(axis=2)
        return plane_sum(sums + swap(jnp.flip(sums, 1), 1))

    def lanes2(x):
        return jnp.broadcast_to(x[:, None, :], (2, MELS, part)).reshape(1, -1)

    norm2 = jnp.stack([norm2_gain, norm2_bias])
    norm2 = jnp.stack([norm2, swap(after(norm2, act1[1]), 1)], axis=1)
    sums2 = all_rows(pre2 * v0, pre2 * pre2 * v0)
    mean2, rstd2 = norm_stats(sums2[0], sums2[1])
    xhat2 = (pre2 - lanes2(mean2)) * lanes2(rstd2)
    z2 = lanes2(norm2[0]) * xhat2 + lanes2(norm2[1])
    dz2 = grad_in.astype(f32) * v0 * silu_slope(z2)
    grads2 = all_rows(dz2, dz2 * xhat2)
    bias2_grad, gain2_grad = grads2[0, 0], grads2[1, 0]
    dpre2 = (
        v0
        * lanes2(norm2[0] * rstd2)
        * (dz2 - (lanes2(grads2[0]) + xhat2 * lanes2(grads2[1])) / count)
    ).astype(bf16)

    grad2 = [dpre2]
    dact1, block_out = [], None
    for r in groups:
        ahead = along(grad2[r], 1) if r < PLANES - 1 else None
        keep, *sends = conv_t([grad2[r]], weights2, CHIPS)
        got = [swap(v, bits) for v, bits in zip(sends, (X, Y, X + Y))]
        done = list(got)
        if r == 0:
            out_local = (v0 * jax.nn.silu(after(z2, keep))).astype(bf16)
            lanes = MELS * part
            out_local = jnp.concatenate(
                [out_local[:, :lanes], swap(out_local[:, lanes:], 1)], axis=0
            )
            out_local = mxu(picker, out_local, TN).astype(bf16)
            out_local = out_local.reshape(n, own_frames, MELS, part)
            done.append(out_local)
        if r == 1:
            block_out = lax.all_to_all(after(out_local, keep), "tm", 0, 0, tiled=True)
        if r == 2:
            block_out = block_out.transpose(1, 2, 0, 3)
            block_out = block_out.reshape(1, own_frames, MELS, n * part)
            done.append(block_out)
        dact1.append(
            (keep + got[0].astype(f32)) + (got[1].astype(f32) + got[2].astype(f32))
        )
        if ahead is not None:
            ahead, *rest = lax.optimization_barrier((ahead, *done))
            if r == 0:
                out_local = rest[-1]
            if r == 2:
                block_out = rest[-1]
            grad2.append(ahead)

    dz1 = [d * v * silu_slope(z) for d, v, z in zip(dact1, mask, z1)]
    sums = jnp.stack(
        [
            per_channel(sum(rows_sum(d) for d in dz1)),
            per_channel(sum(rows_sum(d * x) for d, x in zip(dz1, xhat1))),
        ]
    )
    grads1 = chip_sum(sums)
    dpre1 = [
        (
            v
            * per_lane(gain1 * rstd1)
            * (d - (per_lane(grads1[0]) + x * per_lane(grads1[1])) / count)
        ).astype(bf16)
        for v, d, x in zip(mask, dz1, xhat1)
    ]
    order = (1, 2, 3, 0)
    pairs1, terms = [None] * PLANES, {}
    for k, r in enumerate(order):
        x = dpre1[r] if k == 0 else after(dpre1[r], pairs1[1][1])
        pairs1[r] = [x, swap(x, X)]
    send = None
    for k, r in enumerate(order):
        x, near = pairs1[r]
        if k > 0:
            near = after(near, send)
        keep, send = conv_t([x, near], weights1, 2)
        terms[r] = keep, send

    def dx_term(r):
        return terms[r][0] + swap(terms[r][1], Y).astype(f32)

    first = dx_term(1).astype(bf16)
    pairs1[1][0] = after(pairs1[1][0], first, send)
    grad1_own, grad1_send = weight_grad_own(
        pos,
        [pairs1[r] for r in order],
        [inputs[r] for r in order],
        grad1_place,
        (PLANES, 9, half, 128),
        pl.BlockSpec(
            (1, 9, half, 128), lambda t, p: (2 * (p[1] ^ (t // 2)) + t % 2, 0, 0, 0)
        ),
    )
    grad1 = (grad1_own + swap(grad1_send, 1).astype(f32)).astype(bf16)
    second = (dx_term(2) + after(along(first, 1), grad1).astype(f32)).astype(bf16)
    moved = along(second, 1)
    grad1_planes = lax.all_to_all(after(grad1, second), "batch", 0, 0, tiled=True)
    grad2_own, grad2_send = weight_grad_own(
        pos,
        [[after(grad2[0], second)]] + [[g] for g in grad2[1:]],
        hidden,
        grad2_place,
        (9, part, conv2_weight.shape[2]),
        pl.BlockSpec(
            (9, part, 128), lambda t, p: (0, 0, 2 * (p[2] ^ (t % 2)) + (p[1] ^ (t // 2)))
        ),
    )
    third = (dx_term(3) + after(moved, grad2_send).astype(f32)).astype(bf16)
    moved = along(third, 1)
    conv2_grad = grad2_own + swap(after(grad2_send, third), 1).astype(f32)
    dx = (dx_term(0) + after(moved, conv2_grad).astype(f32)).astype(bf16)
    conv2_grad = conv2_grad.transpose(1, 0, 2)
    low, high = dx[:, : MELS * lanes1], dx[:, MELS * lanes1 :]
    other = swap(jnp.where(core == 0, high, low), 1)
    dx = jnp.concatenate([jnp.where(core == 0, low, high), other], axis=0)
    dx = mxu(picker, dx, TN).astype(bf16)

    def quarter(k):
        return lax.dynamic_index_in_dim(grad1_planes, chip ^ k, 0, keepdims=False)

    quads = [quarter(0)] + [swap(quarter(k), 2 * k) for k in range(1, CHIPS)]
    dx = lax.all_to_all(dx.reshape(n, own_frames, MELS * lanes1), "tm", 0, 0, tiled=True)
    dx = dx.reshape(2, 2, 2, own_frames, MELS, lanes1).transpose(3, 4, 0, 2, 1, 5)
    input_grad = dx.reshape(1, own_frames, MELS, width1)
    conv1_grad = from_quarters(pos, quads).transpose(1, 0, 2)

    grads1 = after(grads1, grad2_send)
    whole1 = jnp.concatenate(
        [
            route(
                grads1,
                [((4 * y + 2 * x, j), (2 * j + x, j)) for j in groups for x in range(2)],
            )
            for y in range(2)
        ],
        axis=1,
    )
    mine1 = jnp.where(chip == plane, whole1, 0.0)
    for s in range(1, PLANES):
        mine1 += route(
            whole1,
            [((2 * j + c, j), (2 * j + c, (j + s) % PLANES)) for j in groups for c in range(2)],
        )
    bias1_grad, gain1_grad = mine1[0], mine1[1]

    return (
        block_out,
        input_grad,
        conv1_grad,
        gain1_grad,
        bias1_grad,
        conv2_grad,
        gain2_grad,
        bias2_grad,
    )


def solution(mesh):
    return jax.shard_map(
        stationary if dict(mesh.shape) == {"tm": 8, "batch": 4} else gathered,
        mesh=mesh,
        in_specs=(
            P("batch", "tm", None, None),
            P("batch", None),
            P("tm", None, "batch"),
            P("tm"),
            P("tm"),
            P("tm", None, "batch"),
            P("tm"),
            P("tm"),
            P("batch", "tm", None, None),
        ),
        out_specs=(
            P("batch", "tm", None, None),
            P("batch", "tm", None, None),
            P("tm", None, "batch"),
            P("tm"),
            P("tm"),
            P("tm", None, "batch"),
            P("tm"),
            P("tm"),
        ),
        check_vma=False,
    )
```

```python
import functools

import jax
import jax.numpy as jnp
from jax import lax
from jax.experimental import pallas as pl
from jax.experimental.pallas import tpu as pltpu
from jax.sharding import PartitionSpec as P

f32, bf16 = jnp.float32, jnp.bfloat16


def frame_valid(lengths_row, frame_total, clip_count):
    frame_ids = jnp.arange(frame_total, dtype=jnp.int32)
    first_end = 16 * clip_count
    second_end = 48 * clip_count
    clip_index = jnp.where(
        frame_ids < first_end,
        frame_ids // 16,
        jnp.where(
            frame_ids < second_end,
            clip_count + (frame_ids - first_end) // 32,
            2 * clip_count + (frame_ids - second_end) // 64,
        ),
    )
    offset = jnp.where(
        frame_ids < first_end,
        frame_ids % 16,
        jnp.where(
            frame_ids < second_end, (frame_ids - first_end) % 32, (frame_ids - second_end) % 64
        ),
    )
    clip_ids = jnp.arange(3 * clip_count, dtype=jnp.int32)
    picked = jnp.where(
        clip_index[:, None] == clip_ids[None, :], lengths_row[None, :], jnp.zeros((), jnp.int32)
    )
    length_here = jnp.sum(picked, axis=1)
    return offset < length_here


def silu_slope(value):
    sigma = jax.nn.sigmoid(value)
    return sigma * (1.0 + value * (1.0 - sigma))


def tap_weights(weight, tap_row, mel_count):
    row_blocks = []
    for mel_out in range(mel_count):
        col_blocks = []
        for mel_in in range(mel_count):
            offset = mel_in - mel_out + 1
            col_blocks.append(weight[:, 3 * tap_row + offset, :])
        row_blocks.append(jnp.concatenate(col_blocks, axis=1))
    return jnp.concatenate(row_blocks, axis=0)


def convolve(source, weight):
    frame_total, mel_count, width_in = source.shape
    width_out = weight.shape[0]
    flat_rows = jnp.pad(source.reshape(frame_total, mel_count * width_in), ((1, 1), (0, 0)))
    running = jnp.zeros((frame_total, mel_count * width_out), jnp.float32)
    for tap_row in range(3):
        running = running + lax.dot_general(
            flat_rows[tap_row : tap_row + frame_total],
            tap_weights(weight, tap_row, mel_count),
            (((1,), (1,)), ((), ())),
            preferred_element_type=jnp.float32,
        )
    return running.reshape(frame_total, mel_count, width_out)


def weight_grad(source, grad):
    frame_total, mel_count, width_in = source.shape
    width_out = grad.shape[2]
    flat_rows = jnp.pad(source.reshape(frame_total, mel_count * width_in), ((1, 1), (0, 0)))
    grad_flat = grad.reshape(frame_total, mel_count * width_out)
    tap_list = []
    for tap_row in range(3):
        product = lax.dot_general(
            grad_flat,
            flat_rows[tap_row : tap_row + frame_total],
            (((0,), (0,)), ((), ())),
            preferred_element_type=jnp.float32,
        )
        product = product.reshape(mel_count, width_out, mel_count, width_in)
        for offset in range(3):
            summed = jnp.zeros((width_out, width_in), jnp.float32)
            for mel_out in range(mel_count):
                mel_in = mel_out + offset - 1
                if 0 <= mel_in < mel_count:
                    summed = summed + product[mel_out, :, mel_in, :]
            tap_list.append(summed)
    return jnp.stack(tap_list, axis=1)


def transposed(grad_padded, weight, row_count, mel_count):
    width_in = weight.shape[2]
    running = jnp.zeros((row_count, mel_count * width_in), jnp.float32)
    for tap_row in range(3):
        running = running + jnp.dot(
            grad_padded[2 - tap_row : 2 - tap_row + row_count],
            tap_weights(weight, tap_row, mel_count),
            preferred_element_type=jnp.float32,
        )
    return running.reshape(row_count, mel_count, width_in)


def standardize(before, total_sum, total_square, pixel_total):
    average = total_sum / pixel_total
    variance = total_square / pixel_total - average * average
    inv_std = lax.rsqrt(variance + 1e-05)
    return ((before - average) * inv_std, inv_std)


def gathered(
    features,
    lengths,
    conv1_weight,
    norm1_gain,
    norm1_bias,
    conv2_weight,
    norm2_gain,
    norm2_bias,
    out_grad,
):
    tm_devices = lax.axis_size("tm")
    frames_dev = features.shape[1]
    mel_count = features.shape[2]
    frame_total = frames_dev * tm_devices
    clip_count = lengths.shape[1] // 3
    valid_mask = frame_valid(lengths[0], frame_total, clip_count).astype(jnp.float32)[:, None, None]
    valid_low = valid_mask.astype(jnp.bfloat16)

    def fetch_frames():
        return lax.all_gather(features, "tm", axis=1, tiled=True)[0] * valid_low

    def fetch_units(local_units):
        return lax.all_gather(local_units, "tm", axis=2, tiled=True)

    masked = fetch_frames()
    weight_one, weight_two = (
        lax.all_gather(conv1_weight, "batch", axis=2, tiled=True),
        lax.all_gather(conv2_weight, "batch", axis=2, tiled=True),
    )
    pre_one = convolve(masked, weight_one)
    local_total = jnp.sum(lengths.astype(jnp.float32)) * mel_count
    sum_one, square_one, pixel_total = lax.psum(
        (
            jnp.sum(pre_one * valid_mask, axis=(0, 1)),
            jnp.sum(pre_one * pre_one * valid_mask, axis=(0, 1)),
            local_total,
        ),
        "batch",
    )
    scaled_one, rstd_one = standardize(pre_one, sum_one, square_one, pixel_total)
    before_one = norm1_gain * scaled_one + norm1_bias
    hidden = (valid_mask * jax.nn.silu(before_one)).astype(jnp.bfloat16)
    hidden_all = fetch_units(hidden)
    pre_two = convolve(hidden_all, weight_two)
    sum_two, square_two = lax.psum(
        (
            jnp.sum(pre_two * valid_mask, axis=(0, 1)),
            jnp.sum(pre_two * pre_two * valid_mask, axis=(0, 1)),
        ),
        "batch",
    )
    scaled_two, rstd_two = standardize(pre_two, sum_two, square_two, pixel_total)
    before_two = norm2_gain * scaled_two + norm2_bias
    output_local = (valid_mask * jax.nn.silu(before_two)).astype(jnp.bfloat16)
    block_out = lax.all_to_all(output_local[None], "tm", split_axis=1, concat_axis=3, tiled=True)
    grad_local = lax.all_to_all(out_grad, "tm", split_axis=3, concat_axis=1, tiled=True)[0]
    delta_two = grad_local.astype(jnp.float32) * valid_mask * silu_slope(before_two)
    gain2_grad, bias2_grad = lax.psum(
        (jnp.sum(delta_two * scaled_two, axis=(0, 1)), jnp.sum(delta_two, axis=(0, 1))), "batch"
    )
    grad_two = (
        valid_mask
        * norm2_gain
        * rstd_two
        * (delta_two - (bias2_grad + scaled_two * gain2_grad) / pixel_total)
    ).astype(jnp.bfloat16)
    units_again = fetch_units(hidden)
    frames_again = fetch_frames()
    conv2_local = weight_grad(units_again, grad_two)
    padded_two = jnp.pad(grad_two.reshape(frame_total, -1), ((1, 1), (0, 0)))
    partial_terms = transposed(padded_two, weight_two, frame_total, mel_count)
    hidden_grad = lax.psum_scatter(
        partial_terms.astype(jnp.bfloat16), "tm", scatter_dimension=2, tiled=True
    ).astype(jnp.float32)
    delta_one = hidden_grad * valid_mask * silu_slope(before_one)
    gain1_grad, bias1_grad = lax.psum(
        (jnp.sum(delta_one * scaled_one, axis=(0, 1)), jnp.sum(delta_one, axis=(0, 1))), "batch"
    )
    grad_one = (
        valid_mask
        * norm1_gain
        * rstd_one
        * (delta_one - (bias1_grad + scaled_one * gain1_grad) / pixel_total)
    ).astype(jnp.bfloat16)
    conv1_local = weight_grad(frames_again, grad_one)
    conv1_grad, conv2_grad = (
        lax.psum_scatter(
            conv1_local.astype(jnp.bfloat16), "batch", scatter_dimension=2, tiled=True
        ).astype(jnp.float32),
        lax.psum_scatter(
            conv2_local.astype(jnp.bfloat16), "batch", scatter_dimension=2, tiled=True
        ).astype(jnp.float32),
    )
    padded_one = jnp.pad(grad_one.reshape(frame_total, -1), ((1, 1), (0, 0)))
    input_dev = lax.psum_scatter(
        transposed(padded_one, weight_one, frames_dev * lax.axis_size("tm"), mel_count).astype(
            jnp.bfloat16
        ),
        "tm",
        scatter_dimension=0,
        tiled=True,
    ).astype(jnp.float32)
    own_mask = lax.dynamic_slice_in_dim(
        valid_mask, lax.axis_index("tm") * frames_dev, frames_dev, 0
    )
    input_grad = (input_dev * own_mask).astype(jnp.bfloat16)[None]
    return (
        block_out,
        input_grad,
        conv1_grad,
        gain1_grad,
        bias1_grad,
        conv2_grad,
        gain2_grad,
        bias2_grad,
    )


NT = (((1,), (1,)), ((), ()))
NN = (((1,), (0,)), ((), ()))
TN = (((0,), (0,)), ((), ()))
CHIPS, PLANES, MELS = 4, 4, 2


def mxu(a, b, dims):
    return lax.dot_general(a, b, dims, preferred_element_type=f32)


def vmem(mib):
    return pltpu.CompilerParams(vmem_limit_bytes=mib << 20)


def same(*shape):
    return pl.BlockSpec(shape, lambda *_: (0,) * len(shape))


def cost(flops, bytes_accessed):
    return pl.CostEstimate(flops=flops, bytes_accessed=bytes_accessed, transcendentals=0)


def rolled(value, shift):
    shift %= value.shape[0]
    return pltpu.roll(value, shift, 0) if shift else value


def taps1_kernel(pos, own, other, out):
    for t in range(4):
        source = 2 * (pos[1] ^ (t // 2)) + t % 2
        for rx in range(2):
            for tap in range(9):
                value = jnp.where(
                    pos[0] ^ pos[2] == rx, own[source, tap], other[source, tap]
                )
                a, b = tap // 3, tap % 3
                for mo in range(MELS):
                    mi = mo + b - 1
                    if 0 <= mi < MELS:
                        row, lane = rx * 256 + mo * 128, t * 256 + mi * 128
                        out[a, row : row + 128, lane : lane + 128] = value


def taps1(pos, own, other):
    spec = pltpu.PrefetchScalarGridSpec(
        num_scalar_prefetch=1,
        grid=(1,),
        in_specs=[same(*own.shape), same(*own.shape)],
        out_specs=same(3, 512, 1024),
    )
    return pl.pallas_call(
        taps1_kernel,
        grid_spec=spec,
        out_shape=jax.ShapeDtypeStruct((3, 512, 1024), bf16),
        compiler_params=vmem(24),
    )(pos, own, other)


def taps2_kernel(pos, own, other, out):
    part = own.shape[1]
    for core, w in enumerate((own, other)):
        for a in range(3):
            for mo in range(MELS):
                row = (core * MELS + mo) * part
                for mi in range(MELS):
                    lane = mi * 128
                    out[a, row : row + part, lane : lane + 128] = w[3 * a + mi - mo + 1]


def taps2(pos, own, other):
    part = own.shape[1]
    source = pl.BlockSpec(
        (9, part, 128), lambda t, p: (0, 0, 2 * (p[2] ^ (t % 2)) + (p[1] ^ (t // 2)))
    )
    spec = pltpu.PrefetchScalarGridSpec(
        num_scalar_prefetch=1,
        grid=(4,),
        in_specs=[source, source],
        out_specs=pl.BlockSpec((3, 4 * part, 256), lambda t, p: (0, 0, t)),
    )
    return pl.pallas_call(
        taps2_kernel,
        grid_spec=spec,
        out_shape=jax.ShapeDtypeStruct((3, 4 * part, 1024), bf16),
        compiler_params=vmem(24),
    )(pos, own, other)


def to_quarters_kernel(pos, w, *outs):
    half, lanes = outs[0].shape[1:]
    for k, out in enumerate(outs):
        row = pl.multiple_of((pos[1] ^ (k // 2)) * half, half)
        lane = pl.multiple_of((pos[2] ^ (k % 2)) * lanes, lanes)
        out[...] = w[:, pl.ds(row, half), pl.ds(lane, lanes)]


def to_quarters(pos, w):
    taps, o, c = w.shape
    spec = pltpu.PrefetchScalarGridSpec(
        num_scalar_prefetch=1,
        grid=(1,),
        in_specs=[same(*w.shape)],
        out_specs=[same(taps, o // 2, c // 2)] * 4,
    )
    return pl.pallas_call(
        to_quarters_kernel,
        grid_spec=spec,
        out_shape=[jax.ShapeDtypeStruct((taps, o // 2, c // 2), w.dtype)] * 4,
        compiler_params=vmem(16),
    )(pos, w)


def by_chip_kernel(pos, *refs):
    for k in range(4):
        refs[4][2 * (pos[1] ^ (k // 2)) + (pos[2] ^ (k % 2))] = refs[k][...]


def by_chip(pos, pieces):
    shape = pieces[0].shape
    spec = pltpu.PrefetchScalarGridSpec(
        num_scalar_prefetch=1,
        grid=(1,),
        in_specs=[same(*shape)] * 4,
        out_specs=same(4, *shape),
    )
    return pl.pallas_call(
        by_chip_kernel,
        grid_spec=spec,
        out_shape=jax.ShapeDtypeStruct((4, *shape), pieces[0].dtype),
        compiler_params=vmem(16),
    )(pos, *pieces)


def quarters_kernel(quads, out):
    half, lanes = quads.shape[2:]
    for k in range(4):
        row, lane = (k // 2) * half, (k % 2) * lanes
        out[:, row : row + half, lane : lane + lanes] = quads[k].astype(out.dtype)


def from_quarters(quads):
    _, taps, half, lanes = quads.shape
    return pl.pallas_call(
        quarters_kernel,
        grid=(1,),
        in_specs=[same(*quads.shape)],
        out_specs=same(taps, 2 * half, 2 * lanes),
        out_shape=jax.ShapeDtypeStruct((taps, 2 * half, 2 * lanes), f32),
        compiler_params=vmem(16),
    )(quads)


def conv_kernel(pieces, *refs):
    xs, w, outs = refs[:pieces], refs[pieces], refs[pieces + 1 :]
    total = None
    for a in (1, 0, 2):
        z, start = None, 0
        for x in xs:
            width = x.shape[1]
            term = mxu(x[...], w[a, :, start : start + width], NT)
            z, start = term if z is None else z + term, start + width
        z = rolled(z, 1 - a)
        total = z if total is None else total + z
    start = 0
    for out in outs:
        out[...] = total[:, start : start + out.shape[1]].astype(out.dtype)
        start += out.shape[1]


def conv(xs, w, kinds, tile):
    rows, (_, width, depth) = xs[0].shape[0], w.shape
    lanes = tile // len(kinds)
    return pl.pallas_call(
        functools.partial(conv_kernel, len(xs)),
        grid=(width // tile,),
        in_specs=[same(*x.shape) for x in xs]
        + [pl.BlockSpec((3, tile, depth), lambda i: (0, i, 0))],
        out_specs=[pl.BlockSpec((rows, lanes), lambda i: (0, i)) for _ in kinds],
        out_shape=[jax.ShapeDtypeStruct((rows, width // len(kinds)), kind) for kind in kinds],
        compiler_params=vmem(16),
        cost_estimate=cost(6 * rows * width * depth, 2 * rows * depth + 6 * width * depth),
    )(*xs, w)


def spread_rows(dst, at, value, width, lane):
    rows, lanes = value.shape
    wide = value.astype(f32)
    for a in range(3):
        moved = value if a == 1 else rolled(wide, a - 1).astype(bf16)
        dst[at : at + rows, a * width + lane : a * width + lane + lanes] = moved


def conv_t_kernel(pieces, *refs):
    dys, w = refs[:pieces], refs[pieces]
    outs, moved = refs[pieces + 1 : -1], refs[-1]
    width = moved.shape[1] // 3
    step = pl.program_id(0)

    @pl.when(step == 0)
    def _():
        lane = 0
        for dy in dys:
            spread_rows(moved, 0, dy[...], width, lane)
            lane += dy.shape[1]

    value = mxu(moved[...], w[...].reshape(3 * width, w.shape[2]), NN)
    for k, out in enumerate(outs):

        @pl.when(step == k)
        def _():
            out[...] = value.astype(out.dtype)


def conv_t(dys, w, blocks):
    rows, (_, width, depth) = dys[0].shape[0], w.shape
    lanes = depth // blocks
    return pl.pallas_call(
        functools.partial(conv_t_kernel, len(dys)),
        grid=(blocks,),
        in_specs=[same(*dy.shape) for dy in dys]
        + [pl.BlockSpec((3, width, lanes), lambda i: (0, 0, i))],
        out_specs=[same(rows, lanes)] * blocks,
        out_shape=[
            jax.ShapeDtypeStruct((rows, lanes), bf16 if k else f32) for k in range(blocks)
        ],
        scratch_shapes=[pltpu.VMEM((rows, 3 * width), bf16)],
        compiler_params=vmem(16),
        cost_estimate=cost(6 * rows * width * depth, 3 * rows * depth + 6 * width * depth),
    )(*dys, w)


def to_lanes_kernel(pos, x, *outs):
    width = x.shape[2]
    for k, out in enumerate(outs):

        @pl.when(pl.program_id(0) == k)
        def _():
            for m in range(MELS):
                out[:, m * width : (m + 1) * width] = x[:, m, :]


def to_lanes(pos, x, count):
    rows, _, lanes = x.shape
    width = lanes // count
    spec = pltpu.PrefetchScalarGridSpec(
        num_scalar_prefetch=1,
        grid=(count,),
        in_specs=[pl.BlockSpec((rows, MELS, width), lambda i, p: (0, 0, p[3] ^ i))],
        out_specs=[same(rows, MELS * width)] * count,
    )
    return pl.pallas_call(
        to_lanes_kernel,
        grid_spec=spec,
        out_shape=[jax.ShapeDtypeStruct((rows, MELS * width), x.dtype)] * count,
    )(pos, x)


def from_lanes_kernel(pos, *refs):
    out = refs[-1]
    width = out.shape[2]
    for k, x in enumerate(refs[:-1]):

        @pl.when(pl.program_id(0) == k)
        def _():
            for m in range(MELS):
                out[:, m, :] = x[:, m * width : (m + 1) * width]


def from_lanes(pos, pieces):
    count = len(pieces)
    rows, lanes = pieces[0].shape
    width = lanes // MELS
    spec = pltpu.PrefetchScalarGridSpec(
        num_scalar_prefetch=1,
        grid=(count,),
        in_specs=[same(rows, lanes)] * count,
        out_specs=pl.BlockSpec((rows, MELS, width), lambda i, p: (0, 0, p[3] ^ i)),
    )
    return pl.pallas_call(
        from_lanes_kernel,
        grid_spec=spec,
        out_shape=jax.ShapeDtypeStruct((rows, MELS, count * width), pieces[0].dtype),
    )(pos, *pieces)


def row_sums(x, y):
    row = lax.broadcasted_iota(jnp.int32, (8, x.shape[1]), 0)
    first = jnp.sum(x, axis=0, keepdims=True)
    second = jnp.sum(y, axis=0, keepdims=True)
    return jnp.where(row == 0, first, jnp.where(row == 1, second, 0.0))


def mel_sums(parts):
    total = (parts[0][...] + parts[1][...]) + (parts[2][...] + parts[3][...])
    part = total.shape[1] // 4
    cores = [
        total[:, 2 * c * part : (2 * c + 1) * part]
        + total[:, (2 * c + 1) * part : (2 * c + 2) * part]
        for c in range(2)
    ]
    return jnp.concatenate([cores[0], cores[0], cores[1], cores[1]], axis=1)


def norm2_kernel(term, moved, mask, pre, sums):
    value = term[...] + moved[...].astype(f32)
    pre[...] = value
    sums[...] = row_sums(value * mask[...], value * value * mask[...])


def back2_kernel(pre, mask, grad, norm, count, t0, t1, t2, t3, xhat, dz, act, scale, sums):
    total = mel_sums((t0, t1, t2, t3)) / count[0, 0]
    average = total[0:1]
    rstd = lax.rsqrt(total[1:2] - average * average + 1e-05)
    gain, bias = norm[0:1], norm[1:2]
    scaled = (pre[...] - average) * rstd
    z = gain * scaled + bias
    sigma = 1.0 / (1.0 + jnp.exp(-z))
    act[...] = (mask[...] * (z * sigma)).astype(bf16)
    delta = grad[...].astype(f32) * mask[...] * (sigma * (1.0 + z * (1.0 - sigma)))
    xhat[...] = scaled
    dz[...] = delta
    scale[...] = jnp.broadcast_to(gain * rstd, scale.shape)
    sums[...] = row_sums(delta, delta * scaled)


def dpre2_kernel(xhat, dz, mask, scale, count, t0, t1, t2, t3, dpre, grads):
    total = mel_sums((t0, t1, t2, t3))
    grads[...] = total
    mean = total / count[0, 0]
    value = dz[...] - (mean[0:1] + xhat[...] * mean[1:2])
    dpre[...] = (mask[...] * scale[0:1] * value).astype(bf16)


def lanes_kernel(body, args, kinds):
    rows, lanes = args[0].shape
    shapes = [(8, lanes) if kind is None else (rows, lanes) for kind in kinds]
    return pl.pallas_call(
        body,
        grid=(1,),
        in_specs=[
            pl.BlockSpec(memory_space=pltpu.MemorySpace.SMEM)
            if x.shape == (1, 1)
            else same(*x.shape)
            for x in args
        ],
        out_specs=[same(*shape) for shape in shapes],
        out_shape=[
            jax.ShapeDtypeStruct(shape, kind or f32) for shape, kind in zip(shapes, kinds)
        ],
        compiler_params=vmem(24),
    )(*args)


def conv_t3_kernel(*refs):
    dys, w, outs, moved = refs[:6], refs[6], refs[7:13], refs[13]
    rows, width = dys[0].shape[0], moved.shape[1] // 3
    step = pl.program_id(0)

    @pl.when(step == 0)
    def _():
        for r in range(3):
            for k in range(2):
                dy = dys[2 * r + k]
                spread_rows(moved, r * rows, dy[...], width, k * dy.shape[1])

    value = mxu(moved[...], w[...].reshape(3 * width, w.shape[2]), NN)
    for k in range(2):

        @pl.when(step == k)
        def _():
            for r in range(3):
                out = outs[2 * r + k]
                out[...] = value[r * rows : (r + 1) * rows].astype(out.dtype)


def conv_t3(pairs, w):
    rows, (_, width, depth) = pairs[0][0].shape[0], w.shape
    lanes = depth // 2
    flat = [dy for pair in pairs for dy in pair]
    out = pl.pallas_call(
        conv_t3_kernel,
        grid=(2,),
        in_specs=[same(*dy.shape) for dy in flat]
        + [pl.BlockSpec((3, width, lanes), lambda i: (0, 0, i))],
        out_specs=[same(rows, lanes)] * 6,
        out_shape=[jax.ShapeDtypeStruct((rows, lanes), kind) for kind in (f32, bf16) * 3],
        scratch_shapes=[pltpu.VMEM((3 * rows, 3 * width), bf16)],
        compiler_params=vmem(24),
        cost_estimate=cost(18 * rows * width * depth, 9 * rows * depth + 6 * width * depth),
    )(*flat, w)
    return [out[2 * r : 2 * r + 2] for r in range(3)]


def grad2_place(pos, own, send, a, prod):
    part = prod.shape[0] // 4
    for core, out in enumerate((own, send)):
        first = prod[2 * core * part : (2 * core + 1) * part]
        second = prod[(2 * core + 1) * part : (2 * core + 2) * part]
        out[3 * a] = second[:, :128].astype(out.dtype)
        out[3 * a + 1] = (first[:, :128] + second[:, 128:]).astype(out.dtype)
        out[3 * a + 2] = first[:, 128:].astype(out.dtype)


def grad1_place(pos, own, send, a, prod):
    taps = []
    for rx in range(2):
        first, second = prod[rx * 256 : rx * 256 + 128], prod[rx * 256 + 128 :][:128]
        taps.append([second[:, :128], first[:, :128] + second[:, 128:], first[:, 128:]])
    for b in range(3):
        mine = pos[0] == pos[2]
        own[0, 3 * a + b] = jnp.where(mine, taps[0][b], taps[1][b])
        send[0, 3 * a + b] = jnp.where(mine, taps[1][b], taps[0][b]).astype(bf16)


def grad_kernel(place, groups, pieces, pos, *refs):
    dys = refs[: groups * pieces]
    xs = refs[groups * pieces : -4]
    own, send, moved, x = refs[-4:]
    width = moved.shape[1] // 3
    step = pl.program_id(0)
    rows = dys[0].shape[0]
    per_group = len(xs) // groups
    steps_each = 4 // per_group

    @pl.when(step == 0)
    def _():
        for r in range(groups):
            lane = 0
            for dy in dys[r * pieces : (r + 1) * pieces]:
                spread_rows(moved, r * rows, dy[...], width, lane)
                lane += dy.shape[1]

    for k in range(per_group):

        @pl.when(step // steps_each == k)
        def _():
            for r in range(groups):
                x[r * rows : (r + 1) * rows, :] = xs[r * per_group + k][...]

    for a in range(3):
        place(pos, own, send, a, mxu(moved[:, a * width : (a + 1) * width], x[...], TN))


def weight_grad_own(pos, dys, xs, place, shape, out_spec, grant):
    groups, pieces, per_group = len(dys), len(dys[0]), len(xs[0])
    rows = dys[0][0].shape[0]
    width = sum(dy.shape[1] for dy in dys[0])
    steps_each = 4 // per_group

    def column(k):
        return lambda t, p: (0, jnp.clip(t - k * steps_each, 0, steps_each - 1))

    spec = pltpu.PrefetchScalarGridSpec(
        num_scalar_prefetch=1,
        grid=(4,),
        in_specs=[same(*dy.shape) for group in dys for dy in group]
        + [pl.BlockSpec((rows, 256), column(k)) for _ in xs for k in range(per_group)],
        out_specs=[out_spec, out_spec],
        scratch_shapes=[
            pltpu.VMEM((groups * rows, 3 * width), bf16),
            pltpu.VMEM((groups * rows, 256), bf16),
        ],
    )
    args = [dy for group in dys for dy in group] + [x for group in xs for x in group]
    return pl.pallas_call(
        functools.partial(grad_kernel, place, groups, pieces),
        grid_spec=spec,
        out_shape=[jax.ShapeDtypeStruct(shape, f32), jax.ShapeDtypeStruct(shape, bf16)],
        compiler_params=vmem(grant),
        cost_estimate=cost(0, 0),
    )(pos, *args)


def clip_places(lengths, half_rows):
    clips = lengths.shape[1]
    each = clips // 3

    def rank(axis):
        clip = lax.broadcasted_iota(jnp.int32, (1, clips, clips), axis)
        kind, place = clip // each, clip % each
        late = place >= each // 2
        long = jnp.where(late, place + 2 * each, place)
        middle = jnp.where(late, place + each + each // 2, place + each // 2)
        return jnp.where(kind == 2, long, jnp.where(kind == 1, middle, place + each))

    size = lengths + 1
    before = jnp.sum(jnp.where(rank(2) < rank(1), size[:, None, :], 0), axis=2)
    late = (before + size > half_rows).astype(jnp.int32)
    taken = jnp.sum((1 - late) * size, axis=1, keepdims=True)
    fits = jnp.max(jnp.sum(late * size, axis=1)) <= half_rows
    return late, before - late * taken, fits


def frame_clips(lengths_row, frames, outward):
    clips = lengths_row.shape[0]
    clip = lax.broadcasted_iota(jnp.int32, (frames, clips), 1)
    frame = lax.broadcasted_iota(jnp.int32, (frames, clips), 0)
    if outward:
        device, own = outward
        frame = ((frame // own) ^ device) * own + frame % own
    each = clips // 3
    padded = jnp.where(clip < each, 16, jnp.where(clip < 2 * each, 32, 64))
    base = jnp.where(
        clip < each, 0, jnp.where(clip < 2 * each, 16 * each, 48 * each)
    ) + padded * (clip % each)
    offset = frame - base
    return jnp.where((offset >= 0) & (offset < lengths_row[None, :]), offset, -1)


def row_masks(lengths, late, start, core, rows):
    length = jnp.where(late == core, lengths, 0)[None]
    row = lax.broadcasted_iota(jnp.int32, (rows, *lengths.shape), 0)
    inside = (row >= start[None]) & (row < start[None] + length)
    return jnp.sum(inside.astype(f32), axis=2)


def after(value, *others):
    return lax.optimization_barrier((value, *others))[0]


def stationary(
    features,
    lengths,
    conv1_weight,
    norm1_gain,
    norm1_bias,
    conv2_weight,
    norm2_gain,
    norm2_bias,
    out_grad,
):
    n = 2 * CHIPS
    own_frames, _, width1 = features.shape[1:]
    frames, lanes1 = own_frames * n, width1 // n

    sent = features[0].reshape(own_frames, MELS, 2, 2, 2, lanes1).transpose(2, 4, 3, 0, 1, 5)
    sent, lengths = lax.optimization_barrier((sent.reshape(frames, MELS * lanes1), lengths))
    mine = lax.all_to_all(sent, "tm", 0, 0, tiled=True)
    every = jnp.concatenate(
        [lengths]
        + [
            lax.ppermute(lengths, "batch", [(z, (z + s) % PLANES) for z in range(PLANES)])
            for s in range(1, PLANES)
        ]
    )
    me = lax.axis_index("tm")
    pos = jnp.stack([me % 2, me // 4, me // 2 % 2, me]).astype(jnp.int32)
    quarters = to_quarters(pos, conv1_weight.transpose(1, 0, 2))
    w2 = conv2_weight.transpose(1, 0, 2)
    norm2 = jnp.stack([norm2_gain, norm2_bias])
    flip = [(i, i ^ 1) for i in range(n)]
    w2_other, norm2_other = lax.ppermute(w2, "tm", flip), lax.ppermute(norm2, "tm", flip)
    norm2 = jnp.concatenate([norm2, norm2, norm2_other, norm2_other], axis=1)
    count = jnp.sum(every.astype(f32)).reshape(1, 1) * MELS
    orders = [
        frame_clips(lengths[0], frames, None),
        frame_clips(lengths[0], frames, (me, own_frames)),
    ]
    core = lax.axis_index("tm") % 2

    def places(half_rows):
        late, start, fits = clip_places(every, half_rows)
        row = jnp.where(late[0] == core, start[0], start[0] + half_rows)
        targets = [jnp.max(jnp.where(x >= 0, row[None, :] + x, -1), axis=1) for x in orders]
        return late, start, *targets, fits

    *packed, fits = places(frames * 3 // 7)
    *loose, _ = places(frames // 2)
    chosen = [jnp.where(fits, x, y) for x, y in zip(packed, loose)]
    return lax.cond(
        fits,
        functools.partial(on_rows, frames * 3 // 7),
        functools.partial(on_rows, frames // 2),
        mine,
        every,
        chosen,
        quarters,
        norm1_gain,
        norm1_bias,
        w2,
        w2_other,
        norm2,
        out_grad[0],
        count,
        pos,
    )


def on_rows(
    rows,
    mine,
    every,
    places,
    w1,
    norm1_gain,
    norm1_bias,
    w2,
    w2_other,
    norm2,
    out_grad,
    count,
    pos,
):
    n = 2 * CHIPS
    me, plane = lax.axis_index("tm"), lax.axis_index("batch")
    core, chip = me % 2, me // 2
    py, px = chip // 2, chip % 2
    frames, lanes1 = mine.shape[0], mine.shape[1] // MELS
    own_frames, width1 = frames // n, n * lanes1
    part = w2.shape[1]
    half = part // 2
    same_core = [[c + 2 * p for p in range(CHIPS)] for c in range(2)]
    groups = range(PLANES)
    X, Y = 2, 4

    def swap(x, bits):
        return lax.ppermute(x, "tm", [(i, i ^ bits) for i in range(n)])

    def along(x, shift):
        return lax.ppermute(x, "batch", [(z, (z + shift) % PLANES) for z in groups])

    def route(x, pairs):
        flat = [(a * PLANES + b, c * PLANES + d) for (a, b), (c, d) in pairs]
        return lax.ppermute(x, ("tm", "batch"), flat)

    def plane_sum(x):
        got = [
            lax.ppermute(x, "batch", [(z, z ^ s) for z in groups]) for s in range(1, PLANES)
        ]
        return (x + got[0]) + (got[1] + got[2])

    def per_channel(x):
        return jnp.sum(x.reshape(MELS, -1), axis=0)

    def per_lane(x):
        return jnp.tile(x, MELS)[None]

    def rows_sum(x):
        return jnp.sum(x, axis=0)

    late, start, target, outward = places
    picker = lax.broadcasted_iota(jnp.int32, (2 * rows, frames), 0) == target[None, :]
    picker = picker.astype(bf16)
    packed = mxu(picker, mine, NN).astype(bf16)
    other = swap(packed[rows:], 1)
    first = jnp.where(core == 0, packed[:rows], other)
    second = jnp.where(core == 0, other, packed[:rows])
    mine = [jnp.concatenate([first, second], axis=1)]
    outward = lax.broadcasted_iota(jnp.int32, (2 * rows, frames), 0) == outward[None, :]
    outward = outward.astype(bf16)

    def norm_of_block(own_norm):
        both = 0.0
        for y in range(2):
            for c in range(2):
                both += route(
                    own_norm[:, y],
                    [((2 * j + x, j), (4 * y + 2 * x + c, j)) for j in groups for x in range(2)],
                )
        return both

    own_norm = jnp.stack([norm1_gain, norm1_bias]).reshape(2, 2, half)
    nears, both1, weights2, mask = [], None, None, None
    for r in groups:
        x = mine[r]
        ahead = along(x, 1) if r < PLANES - 1 else None
        nears.append(swap(x, Y))
        if r == 0:
            w1 = [w1[0]] + [swap(w1[k], 2 * k) for k in range(1, CHIPS)]
            mask = row_masks(every, after(late, x), start, core, rows)
            mask = [mask[:, k : k + 1] for k in groups]
            ahead, *mask = lax.optimization_barrier((ahead, *mask))
        if r == 1:
            w1 = by_chip(pos, [after(w1[0], x)] + w1[1:])
            w1 = lax.all_to_all(w1, "batch", 0, 0, tiled=True)
            weights2 = taps2(pos, w2, after(w2_other, x))
            grad_in = list(to_lanes(pos, after(out_grad, x), n))
            sent = [swap(grad_in[k], k) for k in (1, 2, 3, 4, 5)]
            ahead, nears[0], nears[1], _, *sent = lax.optimization_barrier(
                (ahead, nears[0], nears[1], weights2, *sent)
            )
            grad_in[1:6] = sent
        if r == 2:
            both1 = norm_of_block(after(own_norm, x))
            sent = [swap(after(grad_in[k], x), k) for k in (6, 7)]
            ahead, nears[2], both1, *sent = lax.optimization_barrier(
                (ahead, nears[2], both1, *sent)
            )
            grad_in[6:] = sent
        if ahead is not None:
            mine.append(ahead)
    gain1, bias1 = both1[0], both1[1]

    w1_other = swap(after(w1, mine[3]), 1)
    weights1 = taps1(pos, w1, w1_other)
    inputs, pre1, send = [], [], None
    for r in groups:
        near = nears[r]
        if r == 3:
            near = after(near, send)
        inputs.append([mine[r], near])
        xs = inputs[r] if r == 0 else [after(mine[r], send), inputs[r][1]]
        keep, send = conv(xs, weights1, (f32, bf16), 512)
        pre1.append(keep + swap(send, X).astype(f32))

    def norm_stats(total, square_total):
        average = total / count[0, 0]
        variance = square_total / count[0, 0] - average * average
        return average, lax.rsqrt(variance + 1e-05)

    def chip_sum(x):
        return x + swap(x, 1)

    sums = jnp.stack(
        [
            per_channel(sum(rows_sum(x * v) for x, v in zip(pre1, mask))),
            per_channel(sum(rows_sum(x * x * v) for x, v in zip(pre1, mask))),
        ]
    )
    sums = chip_sum(sums)
    mean1, rstd1 = norm_stats(sums[0], sums[1])
    xhat1 = [(x - per_lane(mean1)) * per_lane(rstd1) for x in pre1]
    z1 = [per_lane(gain1) * x + per_lane(bias1) for x in xhat1]
    act1 = [(v * jax.nn.silu(z)).astype(bf16) for v, z in zip(mask, z1)]

    hidden = [None] * PLANES
    payload, term, got = None, None, None
    for r in (1, 2, 3, 0):
        x = act1[r] if r == 1 else after(act1[r], *got)
        got = [swap(x, X), swap(x, Y), swap(x, X + Y)]
        if r != 1:
            got[2] = after(got[2], term)
        hidden[r] = [x, *got]
        moved = None if r == 1 else along(payload, 1)
        (term,) = conv(hidden[r], weights2, (bf16 if r == 1 else f32,), 512)
        if r == 1:
            payload = term
        elif r != 0:
            payload = (term + after(moved, term).astype(f32)).astype(bf16)
        else:
            grad_in = jnp.concatenate(grad_in, axis=0)
            grad_in = mxu(outward, after(grad_in, payload), NN).astype(bf16)
            grad_in = jnp.concatenate([grad_in[:rows], swap(grad_in[rows:], 1)], axis=1)
            moved, grad_in, _ = lax.optimization_barrier((moved, grad_in, term))

    lanes2 = 2 * MELS * part

    def to_planes(sums):
        got = swap(sums, 1)
        turned = jnp.concatenate([got[:, lanes2 // 2 :], got[:, : lanes2 // 2]], axis=1)
        sums = sums + turned
        return [sums] + [
            lax.ppermute(sums, "batch", [(z, z ^ s) for z in groups]) for s in range(1, PLANES)
        ]

    v0 = mask[0]
    pre2, sums = lanes_kernel(norm2_kernel, [term, moved, v0], [f32, None])
    xhat2, dz2, out_local, scale2, sums = lanes_kernel(
        back2_kernel,
        [pre2, v0, grad_in, norm2, count, *to_planes(sums)],
        [f32, f32, bf16, None, None],
    )
    dpre2, grads2 = lanes_kernel(
        dpre2_kernel, [xhat2, dz2, v0, scale2, count, *to_planes(sums)], [bf16, None]
    )

    grad2 = [dpre2]
    dact1 = []
    for r in groups:
        ahead = along(grad2[r], 1) if r < PLANES - 1 else None
        keep, *sends = conv_t([grad2[r]], weights2, CHIPS)
        got = [swap(v, bits) for v, bits in zip(sends, (X, Y, X + Y))]
        dact1.append(
            (keep + got[0].astype(f32)) + (got[1].astype(f32) + got[2].astype(f32))
        )
        if ahead is not None:
            grad2.append(after(ahead, *got))

    dz1 = [d * v * silu_slope(z) for d, v, z in zip(dact1, mask, z1)]
    sums = jnp.stack(
        [
            per_channel(sum(rows_sum(d) for d in dz1)),
            per_channel(sum(rows_sum(d * x) for d, x in zip(dz1, xhat1))),
        ]
    )
    grads1 = chip_sum(sums)
    dpre1 = [
        (
            v
            * per_lane(gain1 * rstd1)
            * (d - (per_lane(grads1[0]) + x * per_lane(grads1[1])) / count[0, 0])
        ).astype(bf16)
        for v, d, x in zip(mask, dz1, xhat1)
    ]
    order = (1, 2, 3, 0)
    pairs1, terms, nears = [None] * PLANES, {}, {}
    pairs1[1] = [dpre1[1], swap(dpre1[1], X)]
    later = jnp.concatenate([dpre1[r] for r in order[1:]], axis=0)
    later_near = swap(after(later, pairs1[1][1]), X)
    terms[1] = conv_t(pairs1[1], weights1, 2)
    first = (terms[1][0] + swap(terms[1][1], Y).astype(f32)).astype(bf16)
    out_local = after(out_local, terms[1][1])
    out_local = jnp.concatenate(
        [out_local[:, : lanes2 // 2], swap(out_local[:, lanes2 // 2 :], 1)], axis=0
    )
    out_local = mxu(outward, out_local, TN).astype(bf16)
    out_local = after(out_local, first).reshape(n, own_frames, MELS * part)
    out_pieces = [out_local[k] for k in range(n)]
    sent = [swap(out_pieces[k], k) for k in (1, 2, 3)]
    later_near, *sent = lax.optimization_barrier((later_near, *sent))
    out_pieces[1:4] = sent
    for k, r in enumerate(order[1:]):
        pairs1[r] = [dpre1[r], later_near[k * rows : (k + 1) * rows]]
    terms[2], terms[3], terms[0] = conv_t3([pairs1[r] for r in order[1:]], weights1)
    for r in order[1:]:
        nears[r] = swap(terms[r][1], Y)

    moved = along(first, 1)
    grad1_own, grad1_send = weight_grad_own(
        pos,
        [pairs1[r] for r in order],
        [inputs[r] for r in order],
        grad1_place,
        (PLANES, 9, half, 128),
        pl.BlockSpec(
            (1, 9, half, 128), lambda t, p: (2 * (p[1] ^ (t // 2)) + t % 2, 0, 0, 0)
        ),
        36,
    )
    grad1_send, moved, nears[2] = lax.optimization_barrier((grad1_send, moved, nears[2]))
    second = ((terms[2][0] + nears[2].astype(f32)) + moved.astype(f32)).astype(bf16)
    moved = along(second, 1)
    grad1 = (grad1_own + swap(grad1_send, 1).astype(f32)).astype(bf16)
    grad1_planes = lax.all_to_all(grad1, "batch", 0, 0, tiled=True)
    grad2_first = after(grad2[0], grad1)
    sent = [swap(after(out_pieces[k], grad1), k) for k in (4, 5)]
    grad2_own, grad2_send = weight_grad_own(
        pos,
        [[grad2_first]] + [[g] for g in grad2[1:]],
        hidden,
        grad2_place,
        w2.shape,
        pl.BlockSpec(
            (9, part, 128), lambda t, p: (0, 0, 2 * (p[2] ^ (t % 2)) + (p[1] ^ (t // 2)))
        ),
        60,
    )
    grads1 = after(grads1, grad2_send)
    whole1 = jnp.concatenate(
        [
            route(
                grads1,
                [((4 * y + 2 * x, j), (2 * j + x, j)) for j in groups for x in range(2)],
            )
            for y in range(2)
        ],
        axis=1,
    )
    grad2_send, nears[0], *sent = lax.optimization_barrier((grad2_send, nears[0], *sent))
    sent += [swap(after(out_pieces[k], grad2_send), k) for k in (6, 7)]
    moved, nears[3], grad2_send, grad1_planes, whole1, *sent = lax.optimization_barrier(
        (moved, nears[3], grad2_send, grad1_planes, whole1, *sent)
    )
    out_pieces[4:] = sent
    third = ((terms[3][0] + nears[3].astype(f32)) + moved.astype(f32)).astype(bf16)
    whole1, grad1_planes = after(whole1, third), after(grad1_planes, third)
    moved = along(third, 1)
    grad2_got = swap(grad2_send, 1)

    grad1_chips = lax.all_to_all(
        grad1_planes, "tm", 0, 0, tiled=True, axis_index_groups=same_core
    )
    mine1 = jnp.where(chip == plane, whole1, 0.0)
    for s in range(1, PLANES):
        mine1 += route(
            whole1,
            [((2 * j + c, j), (2 * j + c, (j + s) % PLANES)) for j in groups for c in range(2)],
        )

    moved, grad2_got, mine1 = lax.optimization_barrier((moved, grad2_got, mine1))
    bias1_grad, gain1_grad = mine1[0], mine1[1]
    moved, grad1_chips = lax.optimization_barrier((moved, grad1_chips))
    dx = ((terms[0][0] + nears[0].astype(f32)) + moved.astype(f32)).astype(bf16)
    low, high = dx[:, : MELS * lanes1], dx[:, MELS * lanes1 :]
    other = swap(jnp.where(core == 0, high, low), 1)
    dx = jnp.concatenate([jnp.where(core == 0, low, high), other], axis=0)
    dx = mxu(picker, dx, TN).astype(bf16)
    dx, grad2_got, grad1_chips, out_pieces[0] = lax.optimization_barrier(
        (dx, grad2_got, grad1_chips, out_pieces[0])
    )

    dx = lax.all_to_all(dx.reshape(n, own_frames, MELS * lanes1), "tm", 0, 0, tiled=True)
    dx = dx.reshape(2, 2, 2, own_frames, MELS, lanes1).transpose(3, 4, 0, 2, 1, 5)
    input_grad = dx.reshape(1, own_frames, MELS, width1)
    conv1_grad = from_quarters(grad1_chips).transpose(1, 0, 2)
    block_out = from_lanes(pos, out_pieces)[None]
    conv2_grad = (grad2_own + grad2_got.astype(f32)).transpose(1, 0, 2)

    return (
        block_out,
        input_grad,
        conv1_grad,
        gain1_grad,
        bias1_grad,
        conv2_grad,
        grads2[1, :part],
        grads2[0, :part],
    )


def solution(mesh):
    return jax.shard_map(
        stationary if dict(mesh.shape) == {"tm": 8, "batch": 4} else gathered,
        mesh=mesh,
        in_specs=(
            P("batch", "tm", None, None),
            P("batch", None),
            P("tm", None, "batch"),
            P("tm"),
            P("tm"),
            P("tm", None, "batch"),
            P("tm"),
            P("tm"),
            P("batch", "tm", None, None),
        ),
        out_specs=(
            P("batch", "tm", None, None),
            P("batch", "tm", None, None),
            P("tm", None, "batch"),
            P("tm"),
            P("tm"),
            P("tm", None, "batch"),
            P("tm"),
            P("tm"),
        ),
        check_vma=False,
    )
```

```python
import functools

import jax
import jax.numpy as jnp
from jax import lax
from jax.experimental import pallas as pl
from jax.experimental.pallas import tpu as pltpu
from jax.sharding import PartitionSpec as P

f32, bf16 = jnp.float32, jnp.bfloat16


def frame_valid(lengths_row, frame_total, clip_count):
    frame_ids = jnp.arange(frame_total, dtype=jnp.int32)
    first_end = 16 * clip_count
    second_end = 48 * clip_count
    clip_index = jnp.where(
        frame_ids < first_end,
        frame_ids // 16,
        jnp.where(
            frame_ids < second_end,
            clip_count + (frame_ids - first_end) // 32,
            2 * clip_count + (frame_ids - second_end) // 64,
        ),
    )
    offset = jnp.where(
        frame_ids < first_end,
        frame_ids % 16,
        jnp.where(
            frame_ids < second_end, (frame_ids - first_end) % 32, (frame_ids - second_end) % 64
        ),
    )
    clip_ids = jnp.arange(3 * clip_count, dtype=jnp.int32)
    picked = jnp.where(
        clip_index[:, None] == clip_ids[None, :], lengths_row[None, :], jnp.zeros((), jnp.int32)
    )
    length_here = jnp.sum(picked, axis=1)
    return offset < length_here


def silu_slope(value):
    sigma = jax.nn.sigmoid(value)
    return sigma * (1.0 + value * (1.0 - sigma))


def tap_weights(weight, tap_row, mel_count):
    row_blocks = []
    for mel_out in range(mel_count):
        col_blocks = []
        for mel_in in range(mel_count):
            offset = mel_in - mel_out + 1
            col_blocks.append(weight[:, 3 * tap_row + offset, :])
        row_blocks.append(jnp.concatenate(col_blocks, axis=1))
    return jnp.concatenate(row_blocks, axis=0)


def convolve(source, weight):
    frame_total, mel_count, width_in = source.shape
    width_out = weight.shape[0]
    flat_rows = jnp.pad(source.reshape(frame_total, mel_count * width_in), ((1, 1), (0, 0)))
    running = jnp.zeros((frame_total, mel_count * width_out), jnp.float32)
    for tap_row in range(3):
        running = running + lax.dot_general(
            flat_rows[tap_row : tap_row + frame_total],
            tap_weights(weight, tap_row, mel_count),
            (((1,), (1,)), ((), ())),
            preferred_element_type=jnp.float32,
        )
    return running.reshape(frame_total, mel_count, width_out)


def weight_grad(source, grad):
    frame_total, mel_count, width_in = source.shape
    width_out = grad.shape[2]
    flat_rows = jnp.pad(source.reshape(frame_total, mel_count * width_in), ((1, 1), (0, 0)))
    grad_flat = grad.reshape(frame_total, mel_count * width_out)
    tap_list = []
    for tap_row in range(3):
        product = lax.dot_general(
            grad_flat,
            flat_rows[tap_row : tap_row + frame_total],
            (((0,), (0,)), ((), ())),
            preferred_element_type=jnp.float32,
        )
        product = product.reshape(mel_count, width_out, mel_count, width_in)
        for offset in range(3):
            summed = jnp.zeros((width_out, width_in), jnp.float32)
            for mel_out in range(mel_count):
                mel_in = mel_out + offset - 1
                if 0 <= mel_in < mel_count:
                    summed = summed + product[mel_out, :, mel_in, :]
            tap_list.append(summed)
    return jnp.stack(tap_list, axis=1)


def transposed(grad_padded, weight, row_count, mel_count):
    width_in = weight.shape[2]
    running = jnp.zeros((row_count, mel_count * width_in), jnp.float32)
    for tap_row in range(3):
        running = running + jnp.dot(
            grad_padded[2 - tap_row : 2 - tap_row + row_count],
            tap_weights(weight, tap_row, mel_count),
            preferred_element_type=jnp.float32,
        )
    return running.reshape(row_count, mel_count, width_in)


def standardize(before, total_sum, total_square, pixel_total):
    average = total_sum / pixel_total
    variance = total_square / pixel_total - average * average
    inv_std = lax.rsqrt(variance + 1e-05)
    return ((before - average) * inv_std, inv_std)


def gathered(
    features,
    lengths,
    conv1_weight,
    norm1_gain,
    norm1_bias,
    conv2_weight,
    norm2_gain,
    norm2_bias,
    out_grad,
):
    tm_devices = lax.axis_size("tm")
    frames_dev = features.shape[1]
    mel_count = features.shape[2]
    frame_total = frames_dev * tm_devices
    clip_count = lengths.shape[1] // 3
    valid_mask = frame_valid(lengths[0], frame_total, clip_count).astype(jnp.float32)[:, None, None]
    valid_low = valid_mask.astype(jnp.bfloat16)

    def fetch_frames():
        return lax.all_gather(features, "tm", axis=1, tiled=True)[0] * valid_low

    def fetch_units(local_units):
        return lax.all_gather(local_units, "tm", axis=2, tiled=True)

    masked = fetch_frames()
    weight_one, weight_two = (
        lax.all_gather(conv1_weight, "batch", axis=2, tiled=True),
        lax.all_gather(conv2_weight, "batch", axis=2, tiled=True),
    )
    pre_one = convolve(masked, weight_one)
    local_total = jnp.sum(lengths.astype(jnp.float32)) * mel_count
    sum_one, square_one, pixel_total = lax.psum(
        (
            jnp.sum(pre_one * valid_mask, axis=(0, 1)),
            jnp.sum(pre_one * pre_one * valid_mask, axis=(0, 1)),
            local_total,
        ),
        "batch",
    )
    scaled_one, rstd_one = standardize(pre_one, sum_one, square_one, pixel_total)
    before_one = norm1_gain * scaled_one + norm1_bias
    hidden = (valid_mask * jax.nn.silu(before_one)).astype(jnp.bfloat16)
    hidden_all = fetch_units(hidden)
    pre_two = convolve(hidden_all, weight_two)
    sum_two, square_two = lax.psum(
        (
            jnp.sum(pre_two * valid_mask, axis=(0, 1)),
            jnp.sum(pre_two * pre_two * valid_mask, axis=(0, 1)),
        ),
        "batch",
    )
    scaled_two, rstd_two = standardize(pre_two, sum_two, square_two, pixel_total)
    before_two = norm2_gain * scaled_two + norm2_bias
    output_local = (valid_mask * jax.nn.silu(before_two)).astype(jnp.bfloat16)
    block_out = lax.all_to_all(output_local[None], "tm", split_axis=1, concat_axis=3, tiled=True)
    grad_local = lax.all_to_all(out_grad, "tm", split_axis=3, concat_axis=1, tiled=True)[0]
    delta_two = grad_local.astype(jnp.float32) * valid_mask * silu_slope(before_two)
    gain2_grad, bias2_grad = lax.psum(
        (jnp.sum(delta_two * scaled_two, axis=(0, 1)), jnp.sum(delta_two, axis=(0, 1))), "batch"
    )
    grad_two = (
        valid_mask
        * norm2_gain
        * rstd_two
        * (delta_two - (bias2_grad + scaled_two * gain2_grad) / pixel_total)
    ).astype(jnp.bfloat16)
    units_again = fetch_units(hidden)
    frames_again = fetch_frames()
    conv2_local = weight_grad(units_again, grad_two)
    padded_two = jnp.pad(grad_two.reshape(frame_total, -1), ((1, 1), (0, 0)))
    partial_terms = transposed(padded_two, weight_two, frame_total, mel_count)
    hidden_grad = lax.psum_scatter(
        partial_terms.astype(jnp.bfloat16), "tm", scatter_dimension=2, tiled=True
    ).astype(jnp.float32)
    delta_one = hidden_grad * valid_mask * silu_slope(before_one)
    gain1_grad, bias1_grad = lax.psum(
        (jnp.sum(delta_one * scaled_one, axis=(0, 1)), jnp.sum(delta_one, axis=(0, 1))), "batch"
    )
    grad_one = (
        valid_mask
        * norm1_gain
        * rstd_one
        * (delta_one - (bias1_grad + scaled_one * gain1_grad) / pixel_total)
    ).astype(jnp.bfloat16)
    conv1_local = weight_grad(frames_again, grad_one)
    conv1_grad, conv2_grad = (
        lax.psum_scatter(
            conv1_local.astype(jnp.bfloat16), "batch", scatter_dimension=2, tiled=True
        ).astype(jnp.float32),
        lax.psum_scatter(
            conv2_local.astype(jnp.bfloat16), "batch", scatter_dimension=2, tiled=True
        ).astype(jnp.float32),
    )
    padded_one = jnp.pad(grad_one.reshape(frame_total, -1), ((1, 1), (0, 0)))
    input_dev = lax.psum_scatter(
        transposed(padded_one, weight_one, frames_dev * lax.axis_size("tm"), mel_count).astype(
            jnp.bfloat16
        ),
        "tm",
        scatter_dimension=0,
        tiled=True,
    ).astype(jnp.float32)
    own_mask = lax.dynamic_slice_in_dim(
        valid_mask, lax.axis_index("tm") * frames_dev, frames_dev, 0
    )
    input_grad = (input_dev * own_mask).astype(jnp.bfloat16)[None]
    return (
        block_out,
        input_grad,
        conv1_grad,
        gain1_grad,
        bias1_grad,
        conv2_grad,
        gain2_grad,
        bias2_grad,
    )


NT = (((1,), (1,)), ((), ()))
NN = (((1,), (0,)), ((), ()))
TN = (((0,), (0,)), ((), ()))
CHIPS, PLANES, MELS = 4, 4, 2


def mxu(a, b, dims):
    return lax.dot_general(a, b, dims, preferred_element_type=f32)


def vmem(mib):
    return pltpu.CompilerParams(vmem_limit_bytes=mib << 20)


def same(*shape):
    return pl.BlockSpec(shape, lambda *_: (0,) * len(shape))


def cost(flops, bytes_accessed):
    return pl.CostEstimate(flops=flops, bytes_accessed=bytes_accessed, transcendentals=0)


def rolled(value, shift):
    shift %= value.shape[0]
    return pltpu.roll(value, shift, 0) if shift else value


def taps1_kernel(pos, own, other, out):
    for t in range(4):
        source = 2 * (pos[1] ^ (t // 2)) + t % 2
        for rx in range(2):
            for tap in range(9):
                value = jnp.where(
                    pos[0] ^ pos[2] == rx, own[source, tap], other[source, tap]
                )
                a, b = tap // 3, tap % 3
                for mo in range(MELS):
                    mi = mo + b - 1
                    if 0 <= mi < MELS:
                        row, lane = rx * 256 + mo * 128, t * 256 + mi * 128
                        out[a, row : row + 128, lane : lane + 128] = value


def taps1(pos, own, other):
    spec = pltpu.PrefetchScalarGridSpec(
        num_scalar_prefetch=1,
        grid=(1,),
        in_specs=[same(*own.shape), same(*own.shape)],
        out_specs=same(3, 512, 1024),
    )
    return pl.pallas_call(
        taps1_kernel,
        grid_spec=spec,
        out_shape=jax.ShapeDtypeStruct((3, 512, 1024), bf16),
        compiler_params=vmem(24),
    )(pos, own, other)


def taps2_kernel(pos, own, other, out):
    part = own.shape[1]
    for core, w in enumerate((own, other)):
        for a in range(3):
            for mo in range(MELS):
                row = (core * MELS + mo) * part
                for mi in range(MELS):
                    lane = mi * 128
                    out[a, row : row + part, lane : lane + 128] = w[3 * a + mi - mo + 1]


def taps2(pos, own, other):
    part = own.shape[1]
    source = pl.BlockSpec(
        (9, part, 128), lambda t, p: (0, 0, 2 * (p[2] ^ (t % 2)) + (p[1] ^ (t // 2)))
    )
    spec = pltpu.PrefetchScalarGridSpec(
        num_scalar_prefetch=1,
        grid=(4,),
        in_specs=[source, source],
        out_specs=pl.BlockSpec((3, 4 * part, 256), lambda t, p: (0, 0, t)),
    )
    return pl.pallas_call(
        taps2_kernel,
        grid_spec=spec,
        out_shape=jax.ShapeDtypeStruct((3, 4 * part, 1024), bf16),
        compiler_params=vmem(24),
    )(pos, own, other)


def to_quarters_kernel(pos, w, *outs):
    half, lanes = outs[0].shape[1:]
    for k, out in enumerate(outs):
        row = pl.multiple_of((pos[1] ^ (k // 2)) * half, half)
        lane = pl.multiple_of((pos[2] ^ (k % 2)) * lanes, lanes)
        out[...] = w[:, pl.ds(row, half), pl.ds(lane, lanes)]


def to_quarters(pos, w):
    taps, o, c = w.shape
    spec = pltpu.PrefetchScalarGridSpec(
        num_scalar_prefetch=1,
        grid=(1,),
        in_specs=[same(*w.shape)],
        out_specs=[same(taps, o // 2, c // 2)] * 4,
    )
    return pl.pallas_call(
        to_quarters_kernel,
        grid_spec=spec,
        out_shape=[jax.ShapeDtypeStruct((taps, o // 2, c // 2), w.dtype)] * 4,
        compiler_params=vmem(16),
    )(pos, w)


def by_chip_kernel(pos, *refs):
    for k in range(4):
        refs[4][2 * (pos[1] ^ (k // 2)) + (pos[2] ^ (k % 2))] = refs[k][...]


def by_chip(pos, pieces):
    shape = pieces[0].shape
    spec = pltpu.PrefetchScalarGridSpec(
        num_scalar_prefetch=1,
        grid=(1,),
        in_specs=[same(*shape)] * 4,
        out_specs=same(4, *shape),
    )
    return pl.pallas_call(
        by_chip_kernel,
        grid_spec=spec,
        out_shape=jax.ShapeDtypeStruct((4, *shape), pieces[0].dtype),
        compiler_params=vmem(16),
    )(pos, *pieces)


def quarters_kernel(pos, *refs):
    quads, out = refs[:4], refs[4]
    taps, half, lanes = quads[0].shape
    for k in range(4):
        row = pl.multiple_of((pos[1] ^ (k // 2)) * half, half)
        lane = pl.multiple_of((pos[2] ^ (k % 2)) * lanes, lanes)
        out[:, pl.ds(row, half), pl.ds(lane, lanes)] = quads[k][...].astype(out.dtype)


def from_quarters(pos, quads):
    taps, half, lanes = quads[0].shape
    spec = pltpu.PrefetchScalarGridSpec(
        num_scalar_prefetch=1,
        grid=(1,),
        in_specs=[same(*quads[0].shape)] * 4,
        out_specs=same(taps, 2 * half, 2 * lanes),
    )
    return pl.pallas_call(
        quarters_kernel,
        grid_spec=spec,
        out_shape=jax.ShapeDtypeStruct((taps, 2 * half, 2 * lanes), f32),
        compiler_params=vmem(16),
    )(pos, *quads)


def conv_kernel(pieces, *refs):
    xs, w, outs = refs[:pieces], refs[pieces], refs[pieces + 1 :]
    total = None
    for a in (1, 0, 2):
        z, start = None, 0
        for x in xs:
            width = x.shape[1]
            term = mxu(x[...], w[a, :, start : start + width], NT)
            z, start = term if z is None else z + term, start + width
        z = rolled(z, 1 - a)
        total = z if total is None else total + z
    start = 0
    for out in outs:
        out[...] = total[:, start : start + out.shape[1]].astype(out.dtype)
        start += out.shape[1]


def conv(xs, w, kinds, tile):
    rows, (_, width, depth) = xs[0].shape[0], w.shape
    lanes = tile // len(kinds)
    return pl.pallas_call(
        functools.partial(conv_kernel, len(xs)),
        grid=(width // tile,),
        in_specs=[same(*x.shape) for x in xs]
        + [pl.BlockSpec((3, tile, depth), lambda i: (0, i, 0))],
        out_specs=[pl.BlockSpec((rows, lanes), lambda i: (0, i)) for _ in kinds],
        out_shape=[jax.ShapeDtypeStruct((rows, width // len(kinds)), kind) for kind in kinds],
        compiler_params=vmem(16),
        cost_estimate=cost(6 * rows * width * depth, 2 * rows * depth + 6 * width * depth),
    )(*xs, w)


def spread_rows(dst, at, value, width, lane):
    rows, lanes = value.shape
    wide = value.astype(f32)
    for a in range(3):
        moved = value if a == 1 else rolled(wide, a - 1).astype(bf16)
        dst[at : at + rows, a * width + lane : a * width + lane + lanes] = moved


def conv_t_kernel(pieces, *refs):
    dys, w = refs[:pieces], refs[pieces]
    outs, moved = refs[pieces + 1 : -1], refs[-1]
    width = moved.shape[1] // 3
    step = pl.program_id(0)

    @pl.when(step == 0)
    def _():
        lane = 0
        for dy in dys:
            spread_rows(moved, 0, dy[...], width, lane)
            lane += dy.shape[1]

    value = mxu(moved[...], w[...].reshape(3 * width, w.shape[2]), NN)
    for k, out in enumerate(outs):

        @pl.when(step == k)
        def _():
            out[...] = value.astype(out.dtype)


def conv_t(dys, w, blocks):
    rows, (_, width, depth) = dys[0].shape[0], w.shape
    lanes = depth // blocks
    return pl.pallas_call(
        functools.partial(conv_t_kernel, len(dys)),
        grid=(blocks,),
        in_specs=[same(*dy.shape) for dy in dys]
        + [pl.BlockSpec((3, width, lanes), lambda i: (0, 0, i))],
        out_specs=[same(rows, lanes)] * blocks,
        out_shape=[
            jax.ShapeDtypeStruct((rows, lanes), bf16 if k else f32) for k in range(blocks)
        ],
        scratch_shapes=[pltpu.VMEM((rows, 3 * width), bf16)],
        compiler_params=vmem(16),
        cost_estimate=cost(6 * rows * width * depth, 3 * rows * depth + 6 * width * depth),
    )(*dys, w)


def to_lanes_kernel(pos, x, *outs):
    width = x.shape[2]
    for k, out in enumerate(outs):

        @pl.when(pl.program_id(0) == k)
        def _():
            for m in range(MELS):
                out[:, m * width : (m + 1) * width] = x[:, m, :]


def to_lanes(pos, x, count):
    rows, _, lanes = x.shape
    width = lanes // count
    spec = pltpu.PrefetchScalarGridSpec(
        num_scalar_prefetch=1,
        grid=(count,),
        in_specs=[pl.BlockSpec((rows, MELS, width), lambda i, p: (0, 0, p[3] ^ i))],
        out_specs=[same(rows, MELS * width)] * count,
    )
    return pl.pallas_call(
        to_lanes_kernel,
        grid_spec=spec,
        out_shape=[jax.ShapeDtypeStruct((rows, MELS * width), x.dtype)] * count,
    )(pos, x)


def from_lanes_kernel(pos, *refs):
    out = refs[-1]
    width = out.shape[2]
    for k, x in enumerate(refs[:-1]):

        @pl.when(pl.program_id(0) == k)
        def _():
            for m in range(MELS):
                out[:, m, :] = x[:, m * width : (m + 1) * width]


def from_lanes(pos, pieces):
    count = len(pieces)
    rows, lanes = pieces[0].shape
    width = lanes // MELS
    spec = pltpu.PrefetchScalarGridSpec(
        num_scalar_prefetch=1,
        grid=(count,),
        in_specs=[same(rows, lanes)] * count,
        out_specs=pl.BlockSpec((rows, MELS, width), lambda i, p: (0, 0, p[3] ^ i)),
    )
    return pl.pallas_call(
        from_lanes_kernel,
        grid_spec=spec,
        out_shape=jax.ShapeDtypeStruct((rows, MELS, count * width), pieces[0].dtype),
    )(pos, *pieces)


def row_sums(x, y):
    row = lax.broadcasted_iota(jnp.int32, (8, x.shape[1]), 0)
    first = jnp.sum(x, axis=0, keepdims=True)
    second = jnp.sum(y, axis=0, keepdims=True)
    return jnp.where(row == 0, first, jnp.where(row == 1, second, 0.0))


def mel_sums(parts):
    total = (parts[0][...] + parts[1][...]) + (parts[2][...] + parts[3][...])
    part = total.shape[1] // 4
    cores = [
        total[:, 2 * c * part : (2 * c + 1) * part]
        + total[:, (2 * c + 1) * part : (2 * c + 2) * part]
        for c in range(2)
    ]
    return jnp.concatenate([cores[0], cores[0], cores[1], cores[1]], axis=1)


def norm2_kernel(term, moved, mask, pre, sums):
    value = term[...] + moved[...].astype(f32)
    pre[...] = value
    sums[...] = row_sums(value * mask[...], value * value * mask[...])


def back2_kernel(pre, mask, grad, norm, count, t0, t1, t2, t3, xhat, dz, act, scale, sums):
    total = mel_sums((t0, t1, t2, t3)) / count[0, 0]
    average = total[0:1]
    rstd = lax.rsqrt(total[1:2] - average * average + 1e-05)
    gain, bias = norm[0:1], norm[1:2]
    scaled = (pre[...] - average) * rstd
    z = gain * scaled + bias
    sigma = 1.0 / (1.0 + jnp.exp(-z))
    act[...] = (mask[...] * (z * sigma)).astype(bf16)
    delta = grad[...].astype(f32) * mask[...] * (sigma * (1.0 + z * (1.0 - sigma)))
    xhat[...] = scaled
    dz[...] = delta
    scale[...] = jnp.broadcast_to(gain * rstd, scale.shape)
    sums[...] = row_sums(delta, delta * scaled)


def dpre2_kernel(xhat, dz, mask, scale, count, t0, t1, t2, t3, dpre, grads):
    total = mel_sums((t0, t1, t2, t3))
    grads[...] = total
    mean = total / count[0, 0]
    value = dz[...] - (mean[0:1] + xhat[...] * mean[1:2])
    dpre[...] = (mask[...] * scale[0:1] * value).astype(bf16)


def lanes_kernel(body, args, kinds):
    rows, lanes = args[0].shape
    shapes = [(8, lanes) if kind is None else (rows, lanes) for kind in kinds]
    return pl.pallas_call(
        body,
        grid=(1,),
        in_specs=[
            pl.BlockSpec(memory_space=pltpu.MemorySpace.SMEM)
            if x.shape == (1, 1)
            else same(*x.shape)
            for x in args
        ],
        out_specs=[same(*shape) for shape in shapes],
        out_shape=[
            jax.ShapeDtypeStruct(shape, kind or f32) for shape, kind in zip(shapes, kinds)
        ],
        compiler_params=vmem(24),
    )(*args)


def conv_t3_kernel(*refs):
    dys, w, outs, moved = refs[:6], refs[6], refs[7:13], refs[13]
    rows, width = dys[0].shape[0], moved.shape[1] // 3
    step = pl.program_id(0)

    @pl.when(step == 0)
    def _():
        for r in range(3):
            for k in range(2):
                dy = dys[2 * r + k]
                spread_rows(moved, r * rows, dy[...], width, k * dy.shape[1])

    value = mxu(moved[...], w[...].reshape(3 * width, w.shape[2]), NN)
    for k in range(2):

        @pl.when(step == k)
        def _():
            for r in range(3):
                out = outs[2 * r + k]
                out[...] = value[r * rows : (r + 1) * rows].astype(out.dtype)


def conv_t3(pairs, w):
    rows, (_, width, depth) = pairs[0][0].shape[0], w.shape
    lanes = depth // 2
    flat = [dy for pair in pairs for dy in pair]
    out = pl.pallas_call(
        conv_t3_kernel,
        grid=(2,),
        in_specs=[same(*dy.shape) for dy in flat]
        + [pl.BlockSpec((3, width, lanes), lambda i: (0, 0, i))],
        out_specs=[same(rows, lanes)] * 6,
        out_shape=[jax.ShapeDtypeStruct((rows, lanes), kind) for kind in (f32, bf16) * 3],
        scratch_shapes=[pltpu.VMEM((3 * rows, 3 * width), bf16)],
        compiler_params=vmem(24),
        cost_estimate=cost(18 * rows * width * depth, 9 * rows * depth + 6 * width * depth),
    )(*flat, w)
    return [out[2 * r : 2 * r + 2] for r in range(3)]


def grad2_place(pos, own, send, a, prod):
    part = prod.shape[0] // 4
    for core, out in enumerate((own, send)):
        first = prod[2 * core * part : (2 * core + 1) * part]
        second = prod[(2 * core + 1) * part : (2 * core + 2) * part]
        out[3 * a] = second[:, :128].astype(out.dtype)
        out[3 * a + 1] = (first[:, :128] + second[:, 128:]).astype(out.dtype)
        out[3 * a + 2] = first[:, 128:].astype(out.dtype)


def grad1_place(pos, own, send, a, prod):
    taps = []
    for rx in range(2):
        first, second = prod[rx * 256 : rx * 256 + 128], prod[rx * 256 + 128 :][:128]
        taps.append([second[:, :128], first[:, :128] + second[:, 128:], first[:, 128:]])
    for b in range(3):
        mine = pos[0] == pos[2]
        own[0, 3 * a + b] = jnp.where(mine, taps[0][b], taps[1][b])
        send[0, 3 * a + b] = jnp.where(mine, taps[1][b], taps[0][b]).astype(bf16)


def grad_kernel(place, groups, pieces, pos, *refs):
    dys = refs[: groups * pieces]
    xs = refs[groups * pieces : -4]
    own, send, moved, x = refs[-4:]
    width = moved.shape[1] // 3
    step = pl.program_id(0)
    rows = dys[0].shape[0]
    per_group = len(xs) // groups
    steps_each = 4 // per_group

    @pl.when(step == 0)
    def _():
        for r in range(groups):
            lane = 0
            for dy in dys[r * pieces : (r + 1) * pieces]:
                spread_rows(moved, r * rows, dy[...], width, lane)
                lane += dy.shape[1]

    for k in range(per_group):

        @pl.when(step // steps_each == k)
        def _():
            for r in range(groups):
                x[r * rows : (r + 1) * rows, :] = xs[r * per_group + k][...]

    for a in range(3):
        place(pos, own, send, a, mxu(moved[:, a * width : (a + 1) * width], x[...], TN))


def weight_grad_own(pos, dys, xs, place, shape, out_spec, grant):
    groups, pieces, per_group = len(dys), len(dys[0]), len(xs[0])
    rows = dys[0][0].shape[0]
    width = sum(dy.shape[1] for dy in dys[0])
    steps_each = 4 // per_group

    def column(k):
        return lambda t, p: (0, jnp.clip(t - k * steps_each, 0, steps_each - 1))

    spec = pltpu.PrefetchScalarGridSpec(
        num_scalar_prefetch=1,
        grid=(4,),
        in_specs=[same(*dy.shape) for group in dys for dy in group]
        + [pl.BlockSpec((rows, 256), column(k)) for _ in xs for k in range(per_group)],
        out_specs=[out_spec, out_spec],
        scratch_shapes=[
            pltpu.VMEM((groups * rows, 3 * width), bf16),
            pltpu.VMEM((groups * rows, 256), bf16),
        ],
    )
    args = [dy for group in dys for dy in group] + [x for group in xs for x in group]
    return pl.pallas_call(
        functools.partial(grad_kernel, place, groups, pieces),
        grid_spec=spec,
        out_shape=[jax.ShapeDtypeStruct(shape, f32), jax.ShapeDtypeStruct(shape, bf16)],
        compiler_params=vmem(grant),
        cost_estimate=cost(0, 0),
    )(pos, *args)


def clip_places(lengths, sizes):
    clips = lengths.shape[1]
    each = clips // 3

    def rank(axis):
        clip = lax.broadcasted_iota(jnp.int32, (1, clips, clips), axis)
        kind, place = clip // each, clip % each
        late = place >= each // 2
        long = jnp.where(late, place + 2 * each, place)
        middle = jnp.where(late, place + each + each // 2, place + each // 2)
        return jnp.where(kind == 2, long, jnp.where(kind == 1, middle, place + each))

    sizes = jnp.array(sizes, jnp.int32)[:, None, None]
    size = lengths + 1
    before = jnp.sum(jnp.where(rank(2) < rank(1), size[:, None, :], 0), axis=2)
    late = ((before + size)[None] > sizes).astype(jnp.int32)
    taken = jnp.sum((1 - late) * size[None], axis=2, keepdims=True)
    rest = jnp.sum(late * size[None], axis=2)
    small = jnp.sum((jnp.max(rest, axis=1) > sizes[:, 0, 0]).astype(jnp.int32))
    return late, before[None] - late * taken, small


def frame_clips(lengths_row, frames, outward):
    clips = lengths_row.shape[0]
    clip = lax.broadcasted_iota(jnp.int32, (frames, clips), 1)
    frame = lax.broadcasted_iota(jnp.int32, (frames, clips), 0)
    if outward:
        device, own = outward
        frame = ((frame // own) ^ device) * own + frame % own
    each = clips // 3
    padded = jnp.where(clip < each, 16, jnp.where(clip < 2 * each, 32, 64))
    base = jnp.where(
        clip < each, 0, jnp.where(clip < 2 * each, 16 * each, 48 * each)
    ) + padded * (clip % each)
    offset = frame - base
    return jnp.where((offset >= 0) & (offset < lengths_row[None, :]), offset, -1)


def row_masks(lengths, late, start, core, rows):
    length = jnp.where(late == core, lengths, 0)[None]
    row = lax.broadcasted_iota(jnp.int32, (rows, *lengths.shape), 0)
    inside = (row >= start[None]) & (row < start[None] + length)
    return jnp.sum(inside.astype(f32), axis=2)


def after(value, *others):
    return lax.optimization_barrier((value, *others))[0]


def stationary(
    features,
    lengths,
    conv1_weight,
    norm1_gain,
    norm1_bias,
    conv2_weight,
    norm2_gain,
    norm2_bias,
    out_grad,
):
    n = 2 * CHIPS
    own_frames, _, width1 = features.shape[1:]
    frames, lanes1 = own_frames * n, width1 // n

    sent = features[0].reshape(own_frames, MELS, 2, 2, 2, lanes1).transpose(2, 4, 3, 0, 1, 5)
    sent, lengths = lax.optimization_barrier((sent.reshape(frames, MELS * lanes1), lengths))
    mine = lax.all_to_all(sent, "tm", 0, 0, tiled=True)
    every = jnp.concatenate(
        [lengths]
        + [
            lax.ppermute(lengths, "batch", [(z, (z + s) % PLANES) for z in range(PLANES)])
            for s in range(1, PLANES)
        ]
    )
    me = lax.axis_index("tm")
    pos = jnp.stack([me % 2, me // 4, me // 2 % 2, me]).astype(jnp.int32)
    mine, quarters = lax.optimization_barrier((mine, conv1_weight))
    quarters = to_quarters(pos, quarters.transpose(1, 0, 2))
    w2 = conv2_weight.transpose(1, 0, 2)
    norm2 = jnp.stack([norm2_gain, norm2_bias])
    flip = [(i, i ^ 1) for i in range(n)]
    w2_other, norm2_other = lax.ppermute(w2, "tm", flip), lax.ppermute(norm2, "tm", flip)
    norm2 = jnp.concatenate([norm2, norm2, norm2_other, norm2_other], axis=1)
    count = jnp.sum(every.astype(f32)).reshape(1, 1) * MELS
    orders = [
        frame_clips(lengths[0], frames, None),
        frame_clips(lengths[0], frames, (me, own_frames)),
    ]
    core = lax.axis_index("tm") % 2

    sizes = [frames * 23 // 56, frames * 3 // 7, frames // 2]
    late, start, small = clip_places(every, sizes)
    away = jnp.array(sizes, jnp.int32)[:, None]
    row = jnp.where(late[:, 0] == core, start[:, 0], start[:, 0] + away)
    targets = [
        jnp.max(jnp.where(x[None] >= 0, row[:, None, :] + x[None], -1), axis=2) for x in orders
    ]
    late, start, targets, small = lax.optimization_barrier((late, start, targets, small))
    packings = [(late[k], start[k], *[x[k] for x in targets]) for k in range(len(sizes))]
    return lax.switch(
        small,
        [functools.partial(on_rows, size, k) for k, size in enumerate(sizes)],
        mine,
        every,
        packings,
        quarters,
        norm1_gain,
        norm1_bias,
        w2,
        w2_other,
        norm2,
        out_grad[0],
        count,
        pos,
    )


def on_rows(
    rows,
    size,
    mine,
    every,
    places,
    w1,
    norm1_gain,
    norm1_bias,
    w2,
    w2_other,
    norm2,
    out_grad,
    count,
    pos,
):
    n = 2 * CHIPS
    me, plane = lax.axis_index("tm"), lax.axis_index("batch")
    core, chip = me % 2, me // 2
    py, px = chip // 2, chip % 2
    frames, lanes1 = mine.shape[0], mine.shape[1] // MELS
    own_frames, width1 = frames // n, n * lanes1
    part = w2.shape[1]
    half = part // 2
    same_core = [[c + 2 * p for p in range(CHIPS)] for c in range(2)]
    groups = range(PLANES)
    X, Y = 2, 4

    def swap(x, bits):
        return lax.ppermute(x, "tm", [(i, i ^ bits) for i in range(n)])

    def along(x, shift):
        return lax.ppermute(x, "batch", [(z, (z + shift) % PLANES) for z in groups])

    def route(x, pairs):
        flat = [(a * PLANES + b, c * PLANES + d) for (a, b), (c, d) in pairs]
        return lax.ppermute(x, ("tm", "batch"), flat)

    def plane_sum(x):
        got = [
            lax.ppermute(x, "batch", [(z, z ^ s) for z in groups]) for s in range(1, PLANES)
        ]
        return (x + got[0]) + (got[1] + got[2])

    def per_channel(x):
        return jnp.sum(x.reshape(MELS, -1), axis=0)

    def per_lane(x):
        return jnp.tile(x, MELS)[None]

    def rows_sum(x):
        return jnp.sum(x, axis=0)

    late, start, target, outward = places[size]
    picker = lax.broadcasted_iota(jnp.int32, (2 * rows, frames), 0) == target[None, :]
    picker = picker.astype(bf16)
    packed = mxu(picker, mine, NN).astype(bf16)
    other = swap(packed[rows:], 1)
    first = jnp.where(core == 0, packed[:rows], other)
    second = jnp.where(core == 0, other, packed[:rows])
    mine = [jnp.concatenate([first, second], axis=1)]
    outward = lax.broadcasted_iota(jnp.int32, (2 * rows, frames), 0) == outward[None, :]
    outward = outward.astype(bf16)

    def norm_of_block(own_norm):
        both = 0.0
        for y in range(2):
            for c in range(2):
                both += route(
                    own_norm[:, y],
                    [((2 * j + x, j), (4 * y + 2 * x + c, j)) for j in groups for x in range(2)],
                )
        return both

    own_norm = jnp.stack([norm1_gain, norm1_bias]).reshape(2, 2, half)
    nears, both1, weights2, mask = [], None, None, None
    for r in groups:
        x = mine[r]
        ahead = along(x, 1) if r < PLANES - 1 else None
        nears.append(swap(x, Y))
        if r == 0:
            w1 = [w1[0]] + [swap(after(w1[k], x), 2 * k) for k in range(1, CHIPS)]
            mask = row_masks(every, after(late, x), start, core, rows)
            mask = [mask[:, k : k + 1] for k in groups]
            ahead, *mask = lax.optimization_barrier((ahead, *mask))
        if r == 1:
            w1 = by_chip(pos, [after(w1[0], x)] + w1[1:])
            w1 = lax.all_to_all(w1, "batch", 0, 0, tiled=True)
            weights2 = taps2(pos, w2, after(w2_other, x))
            grad_in = list(to_lanes(pos, after(out_grad, x), n))
            sent = [swap(after(grad_in[k], weights2), k) for k in (1, 2, 3)]
            ahead, nears[0], nears[1], _, *sent = lax.optimization_barrier(
                (ahead, nears[0], nears[1], weights2, *sent)
            )
            grad_in[1:4] = sent
        if r == 2:
            both1 = norm_of_block(after(own_norm, x))
            sent = [swap(after(grad_in[k], x), k) for k in (4, 5, 6, 7)]
            ahead, nears[2], both1, *sent = lax.optimization_barrier(
                (ahead, nears[2], both1, *sent)
            )
            grad_in[4:] = sent
        if ahead is not None:
            mine.append(ahead)
    gain1, bias1 = both1[0], both1[1]

    w1_other = swap(after(w1, mine[3]), 1)
    weights1 = taps1(pos, w1, w1_other)
    inputs, pre1, send = [], [], None
    for r in groups:
        near = nears[r]
        if r == 3:
            near = after(near, send)
        inputs.append([mine[r], near])
        xs = inputs[r] if r == 0 else [after(mine[r], send), inputs[r][1]]
        keep, send = conv(xs, weights1, (f32, bf16), 512)
        pre1.append(keep + swap(send, X).astype(f32))

    def norm_stats(total, square_total):
        average = total / count[0, 0]
        variance = square_total / count[0, 0] - average * average
        return average, lax.rsqrt(variance + 1e-05)

    def chip_sum(x):
        return x + swap(x, 1)

    sums = jnp.stack(
        [
            per_channel(sum(rows_sum(x * v) for x, v in zip(pre1, mask))),
            per_channel(sum(rows_sum(x * x * v) for x, v in zip(pre1, mask))),
        ]
    )
    sums = chip_sum(sums)
    mean1, rstd1 = norm_stats(sums[0], sums[1])
    xhat1 = [(x - per_lane(mean1)) * per_lane(rstd1) for x in pre1]
    z1 = [per_lane(gain1) * x + per_lane(bias1) for x in xhat1]
    act1 = [(v * jax.nn.silu(z)).astype(bf16) for v, z in zip(mask, z1)]

    hidden = [None] * PLANES
    payload, term, got = None, None, None
    for r in (1, 2, 3, 0):
        x = act1[r] if r == 1 else after(act1[r], *got)
        got = [swap(x, X), swap(x, Y), swap(x, X + Y)]
        if r != 1:
            got[2] = after(got[2], term)
        hidden[r] = [x, *got]
        moved = None if r == 1 else along(payload, 1)
        (term,) = conv(hidden[r], weights2, (bf16 if r == 1 else f32,), 512)
        if r == 1:
            payload = term
        elif r != 0:
            payload = (term + after(moved, term).astype(f32)).astype(bf16)
        else:
            grad_in = jnp.concatenate(grad_in, axis=0)
            grad_in = mxu(outward, after(grad_in, payload), NN).astype(bf16)
            grad_in = jnp.concatenate([grad_in[:rows], swap(grad_in[rows:], 1)], axis=1)
            moved, grad_in, _ = lax.optimization_barrier((moved, grad_in, term))

    lanes2 = 2 * MELS * part

    def to_planes(sums):
        got = swap(sums, 1)
        turned = jnp.concatenate([got[:, lanes2 // 2 :], got[:, : lanes2 // 2]], axis=1)
        sums = sums + turned
        return [sums] + [
            lax.ppermute(sums, "batch", [(z, z ^ s) for z in groups]) for s in range(1, PLANES)
        ]

    v0 = mask[0]
    pre2, sums = lanes_kernel(norm2_kernel, [term, moved, v0], [f32, None])
    xhat2, dz2, out_local, scale2, sums = lanes_kernel(
        back2_kernel,
        [pre2, v0, grad_in, norm2, count, *to_planes(sums)],
        [f32, f32, bf16, None, None],
    )
    dpre2, grads2 = lanes_kernel(
        dpre2_kernel, [xhat2, dz2, v0, scale2, count, *to_planes(sums)], [bf16, None]
    )

    grad2 = [dpre2]
    dact1 = []
    for r in groups:
        ahead = along(grad2[r], 1) if r < PLANES - 1 else None
        keep, *sends = conv_t([grad2[r]], weights2, CHIPS)
        got = [swap(v, bits) for v, bits in zip(sends, (X, Y, X + Y))]
        dact1.append(
            (keep + got[0].astype(f32)) + (got[1].astype(f32) + got[2].astype(f32))
        )
        if ahead is not None:
            grad2.append(after(ahead, *got))

    dz1 = [d * v * silu_slope(z) for d, v, z in zip(dact1, mask, z1)]
    sums = jnp.stack(
        [
            per_channel(sum(rows_sum(d) for d in dz1)),
            per_channel(sum(rows_sum(d * x) for d, x in zip(dz1, xhat1))),
        ]
    )
    grads1 = chip_sum(sums)
    dpre1 = [
        (
            v
            * per_lane(gain1 * rstd1)
            * (d - (per_lane(grads1[0]) + x * per_lane(grads1[1])) / count[0, 0])
        ).astype(bf16)
        for v, d, x in zip(mask, dz1, xhat1)
    ]
    order = (1, 2, 3, 0)
    pairs1, terms, nears = [None] * PLANES, {}, {}
    pairs1[1] = [dpre1[1], swap(dpre1[1], X)]
    later = jnp.concatenate([dpre1[r] for r in order[1:]], axis=0)
    later_near = swap(after(later, pairs1[1][1]), X)
    grads1 = after(grads1, dpre1[1])
    whole1 = jnp.concatenate(
        [
            route(
                grads1,
                [((4 * y + 2 * x, j), (2 * j + x, j)) for j in groups for x in range(2)],
            )
            for y in range(2)
        ],
        axis=1,
    )
    pairs1[1][1], whole1 = lax.optimization_barrier((pairs1[1][1], whole1))
    terms[1] = conv_t(pairs1[1], weights1, 2)
    whole1 = after(whole1, terms[1][1])
    mine1 = jnp.where(chip == plane, whole1, 0.0)
    for s in range(1, PLANES):
        mine1 += route(
            whole1,
            [((2 * j + c, j), (2 * j + c, (j + s) % PLANES)) for j in groups for c in range(2)],
        )

    near, mine1 = lax.optimization_barrier((swap(terms[1][1], Y), mine1))
    bias1_grad, gain1_grad = mine1[0], mine1[1]
    first = (terms[1][0] + near.astype(f32)).astype(bf16)
    out_local = after(out_local, terms[1][1])
    out_local = jnp.concatenate(
        [out_local[:, : lanes2 // 2], swap(out_local[:, lanes2 // 2 :], 1)], axis=0
    )
    out_local = mxu(outward, out_local, TN).astype(bf16)
    out_local = after(out_local, first).reshape(n, own_frames, MELS * part)
    out_pieces = [out_local[k] for k in range(n)]
    later_near = after(later_near, first)
    for k, r in enumerate(order[1:]):
        pairs1[r] = [dpre1[r], later_near[k * rows : (k + 1) * rows]]
    terms[2], terms[3], terms[0] = conv_t3([pairs1[r] for r in order[1:]], weights1)
    for r in order[1:]:
        nears[r] = swap(terms[r][1], Y)

    second = ((terms[2][0] + nears[2].astype(f32)) + along(first, 1).astype(f32)).astype(bf16)
    moved = along(second, 1)
    pairs1[1][0] = after(pairs1[1][0], second)
    grad1_own, grad1_send = weight_grad_own(
        pos,
        [pairs1[r] for r in order],
        [inputs[r] for r in order],
        grad1_place,
        (PLANES, 9, half, 128),
        pl.BlockSpec(
            (1, 9, half, 128), lambda t, p: (2 * (p[1] ^ (t // 2)) + t % 2, 0, 0, 0)
        ),
        36,
    )
    grad1_send, moved, nears[3] = lax.optimization_barrier((grad1_send, moved, nears[3]))
    third = ((terms[3][0] + nears[3].astype(f32)) + moved.astype(f32)).astype(bf16)
    moved = along(third, 1)
    grad1 = (grad1_own + swap(grad1_send, 1).astype(f32)).astype(bf16)
    grad1_planes = lax.all_to_all(grad1, "batch", 0, 0, tiled=True)
    grad2_first = after(grad2[0], third, grad1)
    sent = [swap(after(out_pieces[k], grad1), k) for k in (4, 5, 6)]
    grad2_own, grad2_send = weight_grad_own(
        pos,
        [[grad2_first]] + [[g] for g in grad2[1:]],
        hidden,
        grad2_place,
        w2.shape,
        pl.BlockSpec(
            (9, part, 128), lambda t, p: (0, 0, 2 * (p[2] ^ (t % 2)) + (p[1] ^ (t // 2)))
        ),
        60,
    )
    grad2_send, nears[0], *sent = lax.optimization_barrier((grad2_send, nears[0], *sent))
    later = [swap(after(out_pieces[k], grad2_send), k) for k in (7, 1, 2, 3)]
    moved, grad1_planes, *later = lax.optimization_barrier((moved, grad1_planes, *later))
    out_pieces = out_pieces[:1] + later[1:] + sent + later[:1]

    def quarter(k):
        return lax.dynamic_index_in_dim(grad1_planes, chip ^ k, 0, keepdims=False)

    quads = [quarter(0)] + [swap(quarter(k), 2 * k) for k in range(1, CHIPS)]
    grad2_got = swap(after(grad2_send, moved), 1)
    dx = ((terms[0][0] + nears[0].astype(f32)) + moved.astype(f32)).astype(bf16)
    low, high = dx[:, : MELS * lanes1], dx[:, MELS * lanes1 :]
    other = swap(jnp.where(core == 0, high, low), 1)
    dx = jnp.concatenate([jnp.where(core == 0, low, high), other], axis=0)
    dx = mxu(picker, dx, TN).astype(bf16)
    dx, grad2_got, quads[0], *out_pieces = lax.optimization_barrier(
        (dx, grad2_got, quads[0], *out_pieces)
    )

    dx = lax.all_to_all(dx.reshape(n, own_frames, MELS * lanes1), "tm", 0, 0, tiled=True)
    dx = dx.reshape(2, 2, 2, own_frames, MELS, lanes1).transpose(3, 4, 0, 2, 1, 5)
    input_grad = dx.reshape(1, own_frames, MELS, width1)
    conv1_grad = from_quarters(pos, quads).transpose(1, 0, 2)
    block_out = from_lanes(pos, out_pieces)[None]
    conv2_grad = (grad2_own + grad2_got.astype(f32)).transpose(1, 0, 2)

    return (
        block_out,
        input_grad,
        conv1_grad,
        gain1_grad,
        bias1_grad,
        conv2_grad,
        grads2[1, :part],
        grads2[0, :part],
    )


def solution(mesh):
    return jax.shard_map(
        stationary if dict(mesh.shape) == {"tm": 8, "batch": 4} else gathered,
        mesh=mesh,
        in_specs=(
            P("batch", "tm", None, None),
            P("batch", None),
            P("tm", None, "batch"),
            P("tm"),
            P("tm"),
            P("tm", None, "batch"),
            P("tm"),
            P("tm"),
            P("batch", "tm", None, None),
        ),
        out_specs=(
            P("batch", "tm", None, None),
            P("batch", "tm", None, None),
            P("tm", None, "batch"),
            P("tm"),
            P("tm"),
            P("tm", None, "batch"),
            P("tm"),
            P("tm"),
        ),
        check_vma=False,
    )
```

```python
import functools

import jax
import jax.numpy as jnp
from jax import lax
from jax.experimental import pallas as pl
from jax.experimental.pallas import tpu as pltpu
from jax.sharding import PartitionSpec as P

f32, bf16 = jnp.float32, jnp.bfloat16


def frame_valid(lengths_row, frame_total, clip_count):
    frame_ids = jnp.arange(frame_total, dtype=jnp.int32)
    first_end = 16 * clip_count
    second_end = 48 * clip_count
    clip_index = jnp.where(
        frame_ids < first_end,
        frame_ids // 16,
        jnp.where(
            frame_ids < second_end,
            clip_count + (frame_ids - first_end) // 32,
            2 * clip_count + (frame_ids - second_end) // 64,
        ),
    )
    offset = jnp.where(
        frame_ids < first_end,
        frame_ids % 16,
        jnp.where(
            frame_ids < second_end, (frame_ids - first_end) % 32, (frame_ids - second_end) % 64
        ),
    )
    clip_ids = jnp.arange(3 * clip_count, dtype=jnp.int32)
    picked = jnp.where(
        clip_index[:, None] == clip_ids[None, :], lengths_row[None, :], jnp.zeros((), jnp.int32)
    )
    length_here = jnp.sum(picked, axis=1)
    return offset < length_here


def silu_slope(value):
    sigma = jax.nn.sigmoid(value)
    return sigma * (1.0 + value * (1.0 - sigma))


def tap_weights(weight, tap_row, mel_count):
    row_blocks = []
    for mel_out in range(mel_count):
        col_blocks = []
        for mel_in in range(mel_count):
            offset = mel_in - mel_out + 1
            col_blocks.append(weight[:, 3 * tap_row + offset, :])
        row_blocks.append(jnp.concatenate(col_blocks, axis=1))
    return jnp.concatenate(row_blocks, axis=0)


def convolve(source, weight):
    frame_total, mel_count, width_in = source.shape
    width_out = weight.shape[0]
    flat_rows = jnp.pad(source.reshape(frame_total, mel_count * width_in), ((1, 1), (0, 0)))
    running = jnp.zeros((frame_total, mel_count * width_out), jnp.float32)
    for tap_row in range(3):
        running = running + lax.dot_general(
            flat_rows[tap_row : tap_row + frame_total],
            tap_weights(weight, tap_row, mel_count),
            (((1,), (1,)), ((), ())),
            preferred_element_type=jnp.float32,
        )
    return running.reshape(frame_total, mel_count, width_out)


def weight_grad(source, grad):
    frame_total, mel_count, width_in = source.shape
    width_out = grad.shape[2]
    flat_rows = jnp.pad(source.reshape(frame_total, mel_count * width_in), ((1, 1), (0, 0)))
    grad_flat = grad.reshape(frame_total, mel_count * width_out)
    tap_list = []
    for tap_row in range(3):
        product = lax.dot_general(
            grad_flat,
            flat_rows[tap_row : tap_row + frame_total],
            (((0,), (0,)), ((), ())),
            preferred_element_type=jnp.float32,
        )
        product = product.reshape(mel_count, width_out, mel_count, width_in)
        for offset in range(3):
            summed = jnp.zeros((width_out, width_in), jnp.float32)
            for mel_out in range(mel_count):
                mel_in = mel_out + offset - 1
                if 0 <= mel_in < mel_count:
                    summed = summed + product[mel_out, :, mel_in, :]
            tap_list.append(summed)
    return jnp.stack(tap_list, axis=1)


def transposed(grad_padded, weight, row_count, mel_count):
    width_in = weight.shape[2]
    running = jnp.zeros((row_count, mel_count * width_in), jnp.float32)
    for tap_row in range(3):
        running = running + jnp.dot(
            grad_padded[2 - tap_row : 2 - tap_row + row_count],
            tap_weights(weight, tap_row, mel_count),
            preferred_element_type=jnp.float32,
        )
    return running.reshape(row_count, mel_count, width_in)


def standardize(before, total_sum, total_square, pixel_total):
    average = total_sum / pixel_total
    variance = total_square / pixel_total - average * average
    inv_std = lax.rsqrt(variance + 1e-05)
    return ((before - average) * inv_std, inv_std)


def gathered(
    features,
    lengths,
    conv1_weight,
    norm1_gain,
    norm1_bias,
    conv2_weight,
    norm2_gain,
    norm2_bias,
    out_grad,
):
    tm_devices = lax.axis_size("tm")
    frames_dev = features.shape[1]
    mel_count = features.shape[2]
    frame_total = frames_dev * tm_devices
    clip_count = lengths.shape[1] // 3
    valid_mask = frame_valid(lengths[0], frame_total, clip_count).astype(jnp.float32)[:, None, None]
    valid_low = valid_mask.astype(jnp.bfloat16)

    def fetch_frames():
        return lax.all_gather(features, "tm", axis=1, tiled=True)[0] * valid_low

    def fetch_units(local_units):
        return lax.all_gather(local_units, "tm", axis=2, tiled=True)

    masked = fetch_frames()
    weight_one, weight_two = (
        lax.all_gather(conv1_weight, "batch", axis=2, tiled=True),
        lax.all_gather(conv2_weight, "batch", axis=2, tiled=True),
    )
    pre_one = convolve(masked, weight_one)
    local_total = jnp.sum(lengths.astype(jnp.float32)) * mel_count
    sum_one, square_one, pixel_total = lax.psum(
        (
            jnp.sum(pre_one * valid_mask, axis=(0, 1)),
            jnp.sum(pre_one * pre_one * valid_mask, axis=(0, 1)),
            local_total,
        ),
        "batch",
    )
    scaled_one, rstd_one = standardize(pre_one, sum_one, square_one, pixel_total)
    before_one = norm1_gain * scaled_one + norm1_bias
    hidden = (valid_mask * jax.nn.silu(before_one)).astype(jnp.bfloat16)
    hidden_all = fetch_units(hidden)
    pre_two = convolve(hidden_all, weight_two)
    sum_two, square_two = lax.psum(
        (
            jnp.sum(pre_two * valid_mask, axis=(0, 1)),
            jnp.sum(pre_two * pre_two * valid_mask, axis=(0, 1)),
        ),
        "batch",
    )
    scaled_two, rstd_two = standardize(pre_two, sum_two, square_two, pixel_total)
    before_two = norm2_gain * scaled_two + norm2_bias
    output_local = (valid_mask * jax.nn.silu(before_two)).astype(jnp.bfloat16)
    block_out = lax.all_to_all(output_local[None], "tm", split_axis=1, concat_axis=3, tiled=True)
    grad_local = lax.all_to_all(out_grad, "tm", split_axis=3, concat_axis=1, tiled=True)[0]
    delta_two = grad_local.astype(jnp.float32) * valid_mask * silu_slope(before_two)
    gain2_grad, bias2_grad = lax.psum(
        (jnp.sum(delta_two * scaled_two, axis=(0, 1)), jnp.sum(delta_two, axis=(0, 1))), "batch"
    )
    grad_two = (
        valid_mask
        * norm2_gain
        * rstd_two
        * (delta_two - (bias2_grad + scaled_two * gain2_grad) / pixel_total)
    ).astype(jnp.bfloat16)
    units_again = fetch_units(hidden)
    frames_again = fetch_frames()
    conv2_local = weight_grad(units_again, grad_two)
    padded_two = jnp.pad(grad_two.reshape(frame_total, -1), ((1, 1), (0, 0)))
    partial_terms = transposed(padded_two, weight_two, frame_total, mel_count)
    hidden_grad = lax.psum_scatter(
        partial_terms.astype(jnp.bfloat16), "tm", scatter_dimension=2, tiled=True
    ).astype(jnp.float32)
    delta_one = hidden_grad * valid_mask * silu_slope(before_one)
    gain1_grad, bias1_grad = lax.psum(
        (jnp.sum(delta_one * scaled_one, axis=(0, 1)), jnp.sum(delta_one, axis=(0, 1))), "batch"
    )
    grad_one = (
        valid_mask
        * norm1_gain
        * rstd_one
        * (delta_one - (bias1_grad + scaled_one * gain1_grad) / pixel_total)
    ).astype(jnp.bfloat16)
    conv1_local = weight_grad(frames_again, grad_one)
    conv1_grad, conv2_grad = (
        lax.psum_scatter(
            conv1_local.astype(jnp.bfloat16), "batch", scatter_dimension=2, tiled=True
        ).astype(jnp.float32),
        lax.psum_scatter(
            conv2_local.astype(jnp.bfloat16), "batch", scatter_dimension=2, tiled=True
        ).astype(jnp.float32),
    )
    padded_one = jnp.pad(grad_one.reshape(frame_total, -1), ((1, 1), (0, 0)))
    input_dev = lax.psum_scatter(
        transposed(padded_one, weight_one, frames_dev * lax.axis_size("tm"), mel_count).astype(
            jnp.bfloat16
        ),
        "tm",
        scatter_dimension=0,
        tiled=True,
    ).astype(jnp.float32)
    own_mask = lax.dynamic_slice_in_dim(
        valid_mask, lax.axis_index("tm") * frames_dev, frames_dev, 0
    )
    input_grad = (input_dev * own_mask).astype(jnp.bfloat16)[None]
    return (
        block_out,
        input_grad,
        conv1_grad,
        gain1_grad,
        bias1_grad,
        conv2_grad,
        gain2_grad,
        bias2_grad,
    )


NT = (((1,), (1,)), ((), ()))
NN = (((1,), (0,)), ((), ()))
TN = (((0,), (0,)), ((), ()))
CHIPS, PLANES, MELS = 4, 4, 2


def mxu(a, b, dims):
    return lax.dot_general(a, b, dims, preferred_element_type=f32)


def vmem(mib):
    return pltpu.CompilerParams(vmem_limit_bytes=mib << 20)


def same(*shape):
    return pl.BlockSpec(shape, lambda *_: (0,) * len(shape))


def cost(flops, bytes_accessed):
    return pl.CostEstimate(flops=flops, bytes_accessed=bytes_accessed, transcendentals=0)


def rolled(value, shift):
    shift %= value.shape[0]
    return pltpu.roll(value, shift, 0) if shift else value


def taps1_kernel(pos, own, other, out):
    for t in range(4):
        source = 2 * (pos[1] ^ (t // 2)) + t % 2
        for rx in range(2):
            for tap in range(9):
                value = jnp.where(
                    pos[0] ^ pos[2] == rx, own[source, tap], other[source, tap]
                )
                a, b = tap // 3, tap % 3
                for mo in range(MELS):
                    mi = mo + b - 1
                    if 0 <= mi < MELS:
                        row, lane = rx * 256 + mo * 128, t * 256 + mi * 128
                        out[a, row : row + 128, lane : lane + 128] = value


def taps1(pos, own, other):
    spec = pltpu.PrefetchScalarGridSpec(
        num_scalar_prefetch=1,
        grid=(1,),
        in_specs=[same(*own.shape), same(*own.shape)],
        out_specs=same(3, 512, 1024),
    )
    return pl.pallas_call(
        taps1_kernel,
        grid_spec=spec,
        out_shape=jax.ShapeDtypeStruct((3, 512, 1024), bf16),
        compiler_params=vmem(24),
    )(pos, own, other)


def taps2_kernel(pos, own, other, out):
    part = own.shape[1]
    for core, w in enumerate((own, other)):
        for a in range(3):
            for mo in range(MELS):
                row = (core * MELS + mo) * part
                for mi in range(MELS):
                    lane = mi * 128
                    out[a, row : row + part, lane : lane + 128] = w[3 * a + mi - mo + 1]


def taps2(pos, own, other):
    part = own.shape[1]
    source = pl.BlockSpec(
        (9, part, 128), lambda t, p: (0, 0, 2 * (p[2] ^ (t % 2)) + (p[1] ^ (t // 2)))
    )
    spec = pltpu.PrefetchScalarGridSpec(
        num_scalar_prefetch=1,
        grid=(4,),
        in_specs=[source, source],
        out_specs=pl.BlockSpec((3, 4 * part, 256), lambda t, p: (0, 0, t)),
    )
    return pl.pallas_call(
        taps2_kernel,
        grid_spec=spec,
        out_shape=jax.ShapeDtypeStruct((3, 4 * part, 1024), bf16),
        compiler_params=vmem(24),
    )(pos, own, other)


def to_quarters_kernel(pos, w, *outs):
    half, lanes = outs[0].shape[1:]
    for k, out in enumerate(outs):
        row = pl.multiple_of((pos[1] ^ (k // 2)) * half, half)
        lane = pl.multiple_of((pos[2] ^ (k % 2)) * lanes, lanes)
        out[...] = w[:, pl.ds(row, half), pl.ds(lane, lanes)]


def to_quarters(pos, w):
    taps, o, c = w.shape
    spec = pltpu.PrefetchScalarGridSpec(
        num_scalar_prefetch=1,
        grid=(1,),
        in_specs=[same(*w.shape)],
        out_specs=[same(taps, o // 2, c // 2)] * 4,
    )
    return pl.pallas_call(
        to_quarters_kernel,
        grid_spec=spec,
        out_shape=[jax.ShapeDtypeStruct((taps, o // 2, c // 2), w.dtype)] * 4,
        compiler_params=vmem(16),
    )(pos, w)


def by_chip_kernel(pos, *refs):
    for k in range(4):
        refs[4][2 * (pos[1] ^ (k // 2)) + (pos[2] ^ (k % 2))] = refs[k][...]


def by_chip(pos, pieces):
    shape = pieces[0].shape
    spec = pltpu.PrefetchScalarGridSpec(
        num_scalar_prefetch=1,
        grid=(1,),
        in_specs=[same(*shape)] * 4,
        out_specs=same(4, *shape),
    )
    return pl.pallas_call(
        by_chip_kernel,
        grid_spec=spec,
        out_shape=jax.ShapeDtypeStruct((4, *shape), pieces[0].dtype),
        compiler_params=vmem(16),
    )(pos, *pieces)


def quarters_kernel(pos, *refs):
    quads, out = refs[:4], refs[4]
    taps, half, lanes = quads[0].shape
    for k in range(4):
        row = pl.multiple_of((pos[1] ^ (k // 2)) * half, half)
        lane = pl.multiple_of((pos[2] ^ (k % 2)) * lanes, lanes)
        out[:, pl.ds(row, half), pl.ds(lane, lanes)] = quads[k][...].astype(out.dtype)


def from_quarters(pos, quads):
    taps, half, lanes = quads[0].shape
    spec = pltpu.PrefetchScalarGridSpec(
        num_scalar_prefetch=1,
        grid=(1,),
        in_specs=[same(*quads[0].shape)] * 4,
        out_specs=same(taps, 2 * half, 2 * lanes),
    )
    return pl.pallas_call(
        quarters_kernel,
        grid_spec=spec,
        out_shape=jax.ShapeDtypeStruct((taps, 2 * half, 2 * lanes), f32),
        compiler_params=vmem(16),
    )(pos, *quads)


def conv_kernel(pieces, *refs):
    xs, w, outs = refs[:pieces], refs[pieces], refs[pieces + 1 :]
    total = None
    for a in (1, 0, 2):
        z, start = None, 0
        for x in xs:
            width = x.shape[1]
            term = mxu(x[...], w[a, :, start : start + width], NT)
            z, start = term if z is None else z + term, start + width
        z = rolled(z, 1 - a)
        total = z if total is None else total + z
    start = 0
    for out in outs:
        out[...] = total[:, start : start + out.shape[1]].astype(out.dtype)
        start += out.shape[1]


def conv(xs, w, kinds, tile):
    rows, (_, width, depth) = xs[0].shape[0], w.shape
    lanes = tile // len(kinds)
    return pl.pallas_call(
        functools.partial(conv_kernel, len(xs)),
        grid=(width // tile,),
        in_specs=[same(*x.shape) for x in xs]
        + [pl.BlockSpec((3, tile, depth), lambda i: (0, i, 0))],
        out_specs=[pl.BlockSpec((rows, lanes), lambda i: (0, i)) for _ in kinds],
        out_shape=[jax.ShapeDtypeStruct((rows, width // len(kinds)), kind) for kind in kinds],
        compiler_params=vmem(16),
        cost_estimate=cost(6 * rows * width * depth, 2 * rows * depth + 6 * width * depth),
    )(*xs, w)


def spread_rows(dst, at, value, width, lane):
    rows, lanes = value.shape
    wide = value.astype(f32)
    for a in range(3):
        moved = value if a == 1 else rolled(wide, a - 1).astype(bf16)
        dst[at : at + rows, a * width + lane : a * width + lane + lanes] = moved


def conv_t_kernel(pieces, *refs):
    dys, w = refs[:pieces], refs[pieces]
    outs, moved = refs[pieces + 1 : -1], refs[-1]
    width = moved.shape[1] // 3
    step = pl.program_id(0)

    @pl.when(step == 0)
    def _():
        lane = 0
        for dy in dys:
            spread_rows(moved, 0, dy[...], width, lane)
            lane += dy.shape[1]

    value = mxu(moved[...], w[...].reshape(3 * width, w.shape[2]), NN)
    for k, out in enumerate(outs):

        @pl.when(step == k)
        def _():
            out[...] = value.astype(out.dtype)


def conv_t(dys, w, blocks):
    rows, (_, width, depth) = dys[0].shape[0], w.shape
    lanes = depth // blocks
    return pl.pallas_call(
        functools.partial(conv_t_kernel, len(dys)),
        grid=(blocks,),
        in_specs=[same(*dy.shape) for dy in dys]
        + [pl.BlockSpec((3, width, lanes), lambda i: (0, 0, i))],
        out_specs=[same(rows, lanes)] * blocks,
        out_shape=[
            jax.ShapeDtypeStruct((rows, lanes), bf16 if k else f32) for k in range(blocks)
        ],
        scratch_shapes=[pltpu.VMEM((rows, 3 * width), bf16)],
        compiler_params=vmem(16),
        cost_estimate=cost(6 * rows * width * depth, 3 * rows * depth + 6 * width * depth),
    )(*dys, w)


def to_lanes_kernel(pos, x, *outs):
    width = x.shape[2]
    for k, out in enumerate(outs):

        @pl.when(pl.program_id(0) == k)
        def _():
            for m in range(MELS):
                out[:, m * width : (m + 1) * width] = x[:, m, :]


def to_lanes(pos, x, count):
    rows, _, lanes = x.shape
    width = lanes // count
    spec = pltpu.PrefetchScalarGridSpec(
        num_scalar_prefetch=1,
        grid=(count,),
        in_specs=[pl.BlockSpec((rows, MELS, width), lambda i, p: (0, 0, p[3] ^ i))],
        out_specs=[same(rows, MELS * width)] * count,
    )
    return pl.pallas_call(
        to_lanes_kernel,
        grid_spec=spec,
        out_shape=[jax.ShapeDtypeStruct((rows, MELS * width), x.dtype)] * count,
    )(pos, x)


def from_lanes_kernel(pos, *refs):
    out = refs[-1]
    width = out.shape[2]
    for k, x in enumerate(refs[:-1]):

        @pl.when(pl.program_id(0) == k)
        def _():
            for m in range(MELS):
                out[:, m, :] = x[:, m * width : (m + 1) * width]


def from_lanes(pos, pieces):
    count = len(pieces)
    rows, lanes = pieces[0].shape
    width = lanes // MELS
    spec = pltpu.PrefetchScalarGridSpec(
        num_scalar_prefetch=1,
        grid=(count,),
        in_specs=[same(rows, lanes)] * count,
        out_specs=pl.BlockSpec((rows, MELS, width), lambda i, p: (0, 0, p[3] ^ i)),
    )
    return pl.pallas_call(
        from_lanes_kernel,
        grid_spec=spec,
        out_shape=jax.ShapeDtypeStruct((rows, MELS, count * width), pieces[0].dtype),
    )(pos, *pieces)


def row_sums(x, y):
    row = lax.broadcasted_iota(jnp.int32, (8, x.shape[1]), 0)
    first = jnp.sum(x, axis=0, keepdims=True)
    second = jnp.sum(y, axis=0, keepdims=True)
    return jnp.where(row == 0, first, jnp.where(row == 1, second, 0.0))


def mel_sums(parts):
    total = (parts[0][...] + parts[1][...]) + (parts[2][...] + parts[3][...])
    part = total.shape[1] // 4
    cores = [
        total[:, 2 * c * part : (2 * c + 1) * part]
        + total[:, (2 * c + 1) * part : (2 * c + 2) * part]
        for c in range(2)
    ]
    return jnp.concatenate([cores[0], cores[0], cores[1], cores[1]], axis=1)


def norm2_kernel(term, moved, mask, pre, sums):
    value = term[...] + moved[...].astype(f32)
    pre[...] = value
    sums[...] = row_sums(value * mask[...], value * value * mask[...])


def back2_kernel(pre, mask, grad, norm, count, t0, t1, t2, t3, xhat, dz, act, scale, sums):
    total = mel_sums((t0, t1, t2, t3)) / count[0, 0]
    average = total[0:1]
    rstd = lax.rsqrt(total[1:2] - average * average + 1e-05)
    gain, bias = norm[0:1], norm[1:2]
    scaled = (pre[...] - average) * rstd
    z = gain * scaled + bias
    sigma = 1.0 / (1.0 + jnp.exp(-z))
    act[...] = (mask[...] * (z * sigma)).astype(bf16)
    delta = grad[...].astype(f32) * mask[...] * (sigma * (1.0 + z * (1.0 - sigma)))
    xhat[...] = scaled
    dz[...] = delta
    scale[...] = jnp.broadcast_to(gain * rstd, scale.shape)
    sums[...] = row_sums(delta, delta * scaled)


def dpre2_kernel(xhat, dz, mask, scale, count, t0, t1, t2, t3, dpre, grads):
    total = mel_sums((t0, t1, t2, t3))
    grads[...] = total
    mean = total / count[0, 0]
    value = dz[...] - (mean[0:1] + xhat[...] * mean[1:2])
    dpre[...] = (mask[...] * scale[0:1] * value).astype(bf16)


def lanes_kernel(body, args, kinds):
    rows, lanes = args[0].shape
    shapes = [(8, lanes) if kind is None else (rows, lanes) for kind in kinds]
    return pl.pallas_call(
        body,
        grid=(1,),
        in_specs=[
            pl.BlockSpec(memory_space=pltpu.MemorySpace.SMEM)
            if x.shape == (1, 1)
            else same(*x.shape)
            for x in args
        ],
        out_specs=[same(*shape) for shape in shapes],
        out_shape=[
            jax.ShapeDtypeStruct(shape, kind or f32) for shape, kind in zip(shapes, kinds)
        ],
        compiler_params=vmem(24),
    )(*args)


def grad2_place(pos, own, send, a, prod):
    part = prod.shape[0] // 4
    for core, out in enumerate((own, send)):
        first = prod[2 * core * part : (2 * core + 1) * part]
        second = prod[(2 * core + 1) * part : (2 * core + 2) * part]
        out[3 * a] = second[:, :128].astype(out.dtype)
        out[3 * a + 1] = (first[:, :128] + second[:, 128:]).astype(out.dtype)
        out[3 * a + 2] = first[:, 128:].astype(out.dtype)


def grad1_place(pos, own, send, a, prod):
    taps = []
    for rx in range(2):
        first, second = prod[rx * 256 : rx * 256 + 128], prod[rx * 256 + 128 :][:128]
        taps.append([second[:, :128], first[:, :128] + second[:, 128:], first[:, 128:]])
    for b in range(3):
        mine = pos[0] == pos[2]
        own[0, 3 * a + b] = jnp.where(mine, taps[0][b], taps[1][b])
        send[0, 3 * a + b] = jnp.where(mine, taps[1][b], taps[0][b]).astype(bf16)


def grad_kernel(place, groups, pieces, pos, *refs):
    dys = refs[: groups * pieces]
    xs = refs[groups * pieces : -4]
    own, send, moved, x = refs[-4:]
    width = moved.shape[1] // 3
    step = pl.program_id(0)
    rows = dys[0].shape[0]
    per_group = len(xs) // groups
    steps_each = 4 // per_group

    @pl.when(step == 0)
    def _():
        for r in range(groups):
            lane = 0
            for dy in dys[r * pieces : (r + 1) * pieces]:
                spread_rows(moved, r * rows, dy[...], width, lane)
                lane += dy.shape[1]

    for k in range(per_group):

        @pl.when(step // steps_each == k)
        def _():
            for r in range(groups):
                x[r * rows : (r + 1) * rows, :] = xs[r * per_group + k][...]

    for a in range(3):
        place(pos, own, send, a, mxu(moved[:, a * width : (a + 1) * width], x[...], TN))


def weight_grad_own(pos, dys, xs, place, shape, out_spec, grant):
    groups, pieces, per_group = len(dys), len(dys[0]), len(xs[0])
    rows = dys[0][0].shape[0]
    width = sum(dy.shape[1] for dy in dys[0])
    steps_each = 4 // per_group

    def column(k):
        return lambda t, p: (0, jnp.clip(t - k * steps_each, 0, steps_each - 1))

    spec = pltpu.PrefetchScalarGridSpec(
        num_scalar_prefetch=1,
        grid=(4,),
        in_specs=[same(*dy.shape) for group in dys for dy in group]
        + [pl.BlockSpec((rows, 256), column(k)) for _ in xs for k in range(per_group)],
        out_specs=[out_spec, out_spec],
        scratch_shapes=[
            pltpu.VMEM((groups * rows, 3 * width), bf16),
            pltpu.VMEM((groups * rows, 256), bf16),
        ],
    )
    args = [dy for group in dys for dy in group] + [x for group in xs for x in group]
    return pl.pallas_call(
        functools.partial(grad_kernel, place, groups, pieces),
        grid_spec=spec,
        out_shape=[jax.ShapeDtypeStruct(shape, f32), jax.ShapeDtypeStruct(shape, bf16)],
        compiler_params=vmem(grant),
        cost_estimate=cost(0, 0),
    )(pos, *args)


def clip_places(lengths, sizes):
    clips = lengths.shape[1]
    each = clips // 3

    def rank(axis):
        clip = lax.broadcasted_iota(jnp.int32, (1, clips, clips), axis)
        kind, place = clip // each, clip % each
        late = place >= each // 2
        long = jnp.where(late, place + 2 * each, place)
        middle = jnp.where(late, place + each + each // 2, place + each // 2)
        return jnp.where(kind == 2, long, jnp.where(kind == 1, middle, place + each))

    sizes = jnp.array(sizes, jnp.int32)[:, None, None]
    size = lengths + 1
    before = jnp.sum(jnp.where(rank(2) < rank(1), size[:, None, :], 0), axis=2)
    late = ((before + size)[None] > sizes).astype(jnp.int32)
    taken = jnp.sum((1 - late) * size[None], axis=2, keepdims=True)
    rest = jnp.sum(late * size[None], axis=2)
    small = jnp.sum((jnp.max(rest, axis=1) > sizes[:, 0, 0]).astype(jnp.int32))
    return late, before[None] - late * taken, small


def frame_clips(lengths_row, frames, outward):
    clips = lengths_row.shape[0]
    clip = lax.broadcasted_iota(jnp.int32, (frames, clips), 1)
    frame = lax.broadcasted_iota(jnp.int32, (frames, clips), 0)
    if outward:
        device, own = outward
        frame = ((frame // own) ^ device) * own + frame % own
    each = clips // 3
    padded = jnp.where(clip < each, 16, jnp.where(clip < 2 * each, 32, 64))
    base = jnp.where(
        clip < each, 0, jnp.where(clip < 2 * each, 16 * each, 48 * each)
    ) + padded * (clip % each)
    offset = frame - base
    return jnp.where((offset >= 0) & (offset < lengths_row[None, :]), offset, -1)


def row_masks(lengths, late, start, core, rows):
    length = jnp.where(late == core, lengths, 0)[None]
    row = lax.broadcasted_iota(jnp.int32, (rows, *lengths.shape), 0)
    inside = (row >= start[None]) & (row < start[None] + length)
    return jnp.sum(inside.astype(f32), axis=2)


def after(value, *others):
    return lax.optimization_barrier((value, *others))[0]


def stationary(
    features,
    lengths,
    conv1_weight,
    norm1_gain,
    norm1_bias,
    conv2_weight,
    norm2_gain,
    norm2_bias,
    out_grad,
):
    n = 2 * CHIPS
    own_frames, _, width1 = features.shape[1:]
    frames, lanes1 = own_frames * n, width1 // n

    sent = features[0].reshape(own_frames, MELS, 2, 2, 2, lanes1).transpose(2, 4, 3, 0, 1, 5)
    sent, lengths = lax.optimization_barrier((sent.reshape(frames, MELS * lanes1), lengths))
    mine = lax.all_to_all(sent, "tm", 0, 0, tiled=True)
    every = jnp.concatenate(
        [lengths]
        + [
            lax.ppermute(lengths, "batch", [(z, (z + s) % PLANES) for z in range(PLANES)])
            for s in range(1, PLANES)
        ]
    )
    me = lax.axis_index("tm")
    pos = jnp.stack([me % 2, me // 4, me // 2 % 2, me]).astype(jnp.int32)
    mine, quarters = lax.optimization_barrier((mine, conv1_weight))
    quarters = to_quarters(pos, quarters.transpose(1, 0, 2))
    w2 = conv2_weight.transpose(1, 0, 2)
    norm2 = jnp.stack([norm2_gain, norm2_bias])
    flip = [(i, i ^ 1) for i in range(n)]
    w2_other, norm2_other = lax.ppermute(w2, "tm", flip), lax.ppermute(norm2, "tm", flip)
    norm2 = jnp.concatenate([norm2, norm2, norm2_other, norm2_other], axis=1)
    count = jnp.sum(every.astype(f32)).reshape(1, 1) * MELS
    orders = [
        frame_clips(lengths[0], frames, None),
        frame_clips(lengths[0], frames, (me, own_frames)),
    ]
    core = lax.axis_index("tm") % 2

    sizes = [frames * 23 // 56, frames * 3 // 7, frames // 2]
    late, start, small = clip_places(every, sizes)
    away = jnp.array(sizes, jnp.int32)[:, None]
    row = jnp.where(late[:, 0] == core, start[:, 0], start[:, 0] + away)
    targets = [
        jnp.max(jnp.where(x[None] >= 0, row[:, None, :] + x[None], -1), axis=2) for x in orders
    ]
    late, start, targets, small = lax.optimization_barrier((late, start, targets, small))
    packings = [(late[k], start[k], *[x[k] for x in targets]) for k in range(len(sizes))]
    return lax.switch(
        small,
        [functools.partial(on_rows, size, k) for k, size in enumerate(sizes)],
        mine,
        every,
        packings,
        quarters,
        norm1_gain,
        norm1_bias,
        w2,
        w2_other,
        norm2,
        out_grad[0],
        count,
        pos,
    )


def on_rows(
    rows,
    size,
    mine,
    every,
    places,
    w1,
    norm1_gain,
    norm1_bias,
    w2,
    w2_other,
    norm2,
    out_grad,
    count,
    pos,
):
    n = 2 * CHIPS
    me, plane = lax.axis_index("tm"), lax.axis_index("batch")
    core, chip = me % 2, me // 2
    py, px = chip // 2, chip % 2
    frames, lanes1 = mine.shape[0], mine.shape[1] // MELS
    own_frames, width1 = frames // n, n * lanes1
    part = w2.shape[1]
    half = part // 2
    same_core = [[c + 2 * p for p in range(CHIPS)] for c in range(2)]
    groups = range(PLANES)
    X, Y = 2, 4

    def swap(x, bits):
        return lax.ppermute(x, "tm", [(i, i ^ bits) for i in range(n)])

    def along(x, shift):
        return lax.ppermute(x, "batch", [(z, (z + shift) % PLANES) for z in groups])

    def route(x, pairs):
        flat = [(a * PLANES + b, c * PLANES + d) for (a, b), (c, d) in pairs]
        return lax.ppermute(x, ("tm", "batch"), flat)

    def plane_sum(x):
        got = [
            lax.ppermute(x, "batch", [(z, z ^ s) for z in groups]) for s in range(1, PLANES)
        ]
        return (x + got[0]) + (got[1] + got[2])

    def per_channel(x):
        return jnp.sum(x.reshape(MELS, -1), axis=0)

    def per_lane(x):
        return jnp.tile(x, MELS)[None]

    def rows_sum(x):
        return jnp.sum(x, axis=0)

    late, start, target, outward = places[size]
    picker = lax.broadcasted_iota(jnp.int32, (2 * rows, frames), 0) == target[None, :]
    picker = picker.astype(bf16)
    packed = mxu(picker, mine, NN).astype(bf16)
    other = swap(packed[rows:], 1)
    first = jnp.where(core == 0, packed[:rows], other)
    second = jnp.where(core == 0, other, packed[:rows])
    mine = [jnp.concatenate([first, second], axis=1)]
    outward = lax.broadcasted_iota(jnp.int32, (2 * rows, frames), 0) == outward[None, :]
    outward = outward.astype(bf16)

    def norm_of_block(own_norm):
        both = 0.0
        for y in range(2):
            for c in range(2):
                both += route(
                    own_norm[:, y],
                    [((2 * j + x, j), (4 * y + 2 * x + c, j)) for j in groups for x in range(2)],
                )
        return both

    own_norm = jnp.stack([norm1_gain, norm1_bias]).reshape(2, 2, half)
    nears, both1, weights2, mask = [], None, None, None
    for r in groups:
        x = mine[r]
        ahead = along(x, 1) if r < PLANES - 1 else None
        nears.append(swap(x, Y))
        if r == 0:
            w1 = [w1[0]] + [swap(after(w1[k], x), 2 * k) for k in range(1, CHIPS)]
            mask = row_masks(every, after(late, x), start, core, rows)
            mask = [mask[:, k : k + 1] for k in groups]
            ahead, *mask = lax.optimization_barrier((ahead, *mask))
        if r == 1:
            w1 = by_chip(pos, [after(w1[0], x)] + w1[1:])
            w1 = lax.all_to_all(w1, "batch", 0, 0, tiled=True)
            weights2 = taps2(pos, w2, after(w2_other, x))
            grad_in = list(to_lanes(pos, after(out_grad, x), n))
            sent = [swap(after(grad_in[k], weights2), k) for k in (1, 2, 3)]
            ahead, nears[0], nears[1], _, *sent = lax.optimization_barrier(
                (ahead, nears[0], nears[1], weights2, *sent)
            )
            grad_in[1:4] = sent
        if r == 2:
            both1 = norm_of_block(after(own_norm, x))
            sent = [swap(after(grad_in[k], x), k) for k in (4, 5, 6, 7)]
            ahead, nears[2], both1, *sent = lax.optimization_barrier(
                (ahead, nears[2], both1, *sent)
            )
            grad_in[4:] = sent
        if ahead is not None:
            mine.append(ahead)
    gain1, bias1 = both1[0], both1[1]

    w1_other = swap(after(w1, mine[3]), 1)
    weights1 = taps1(pos, w1, w1_other)
    inputs, pre1, send = [], [], None
    for r in groups:
        near = nears[r]
        if r == 3:
            near = after(near, send)
        inputs.append([mine[r], near])
        xs = inputs[r] if r == 0 else [after(mine[r], send), inputs[r][1]]
        keep, send = conv(xs, weights1, (f32, bf16), 512)
        pre1.append(keep + swap(send, X).astype(f32))

    def norm_stats(total, square_total):
        average = total / count[0, 0]
        variance = square_total / count[0, 0] - average * average
        return average, lax.rsqrt(variance + 1e-05)

    def chip_sum(x):
        return x + swap(x, 1)

    sums = jnp.stack(
        [
            per_channel(sum(rows_sum(x * v) for x, v in zip(pre1, mask))),
            per_channel(sum(rows_sum(x * x * v) for x, v in zip(pre1, mask))),
        ]
    )
    sums = chip_sum(sums)
    mean1, rstd1 = norm_stats(sums[0], sums[1])
    xhat1 = [(x - per_lane(mean1)) * per_lane(rstd1) for x in pre1]
    z1 = [per_lane(gain1) * x + per_lane(bias1) for x in xhat1]
    act1 = [(v * jax.nn.silu(z)).astype(bf16) for v, z in zip(mask, z1)]

    hidden = [None] * PLANES
    payload, term, got = None, None, None
    for r in (1, 2, 3, 0):
        x = act1[r] if r == 1 else after(act1[r], *got)
        got = [swap(x, X), swap(x, Y), swap(x, X + Y)]
        if r != 1:
            got[2] = after(got[2], term)
        hidden[r] = [x, *got]
        moved = None if r == 1 else along(payload, 1)
        (term,) = conv(hidden[r], weights2, (bf16 if r == 1 else f32,), 512)
        if r == 1:
            payload = term
        elif r != 0:
            payload = (term + after(moved, term).astype(f32)).astype(bf16)
        else:
            grad_in = jnp.concatenate(grad_in, axis=0)
            grad_in = mxu(outward, after(grad_in, payload), NN).astype(bf16)
            grad_in = jnp.concatenate([grad_in[:rows], swap(grad_in[rows:], 1)], axis=1)
            moved, grad_in, _ = lax.optimization_barrier((moved, grad_in, term))

    lanes2 = 2 * MELS * part

    def to_planes(sums):
        got = swap(sums, 1)
        turned = jnp.concatenate([got[:, lanes2 // 2 :], got[:, : lanes2 // 2]], axis=1)
        sums = sums + turned
        return [sums] + [
            lax.ppermute(sums, "batch", [(z, z ^ s) for z in groups]) for s in range(1, PLANES)
        ]

    v0 = mask[0]
    pre2, sums = lanes_kernel(norm2_kernel, [term, moved, v0], [f32, None])
    xhat2, dz2, out_local, scale2, sums = lanes_kernel(
        back2_kernel,
        [pre2, v0, grad_in, norm2, count, *to_planes(sums)],
        [f32, f32, bf16, None, None],
    )
    dpre2, grads2 = lanes_kernel(
        dpre2_kernel, [xhat2, dz2, v0, scale2, count, *to_planes(sums)], [bf16, None]
    )

    grad2 = [dpre2]
    dact1 = []
    for r in groups:
        ahead = along(grad2[r], 1) if r < PLANES - 1 else None
        keep, *sends = conv_t([grad2[r]], weights2, CHIPS)
        got = [swap(v, bits) for v, bits in zip(sends, (X, Y, X + Y))]
        dact1.append(
            (keep + got[0].astype(f32)) + (got[1].astype(f32) + got[2].astype(f32))
        )
        if ahead is not None:
            grad2.append(after(ahead, *got))

    dz1 = [d * v * silu_slope(z) for d, v, z in zip(dact1, mask, z1)]
    sums = jnp.stack(
        [
            per_channel(sum(rows_sum(d) for d in dz1)),
            per_channel(sum(rows_sum(d * x) for d, x in zip(dz1, xhat1))),
        ]
    )
    grads1 = chip_sum(sums)
    dpre1 = [
        (
            v
            * per_lane(gain1 * rstd1)
            * (d - (per_lane(grads1[0]) + x * per_lane(grads1[1])) / count[0, 0])
        ).astype(bf16)
        for v, d, x in zip(mask, dz1, xhat1)
    ]
    order = (1, 2, 3, 0)
    pairs1, terms, nears = [None] * PLANES, {}, {}
    pairs1[1] = [dpre1[1], swap(dpre1[1], X)]
    later = jnp.concatenate([dpre1[r] for r in order[1:]], axis=0)
    later_near = swap(after(later, pairs1[1][1]), X)
    grads1 = after(grads1, dpre1[1])
    whole1 = jnp.concatenate(
        [
            route(
                grads1,
                [((4 * y + 2 * x, j), (2 * j + x, j)) for j in groups for x in range(2)],
            )
            for y in range(2)
        ],
        axis=1,
    )
    pairs1[1][1], whole1 = lax.optimization_barrier((pairs1[1][1], whole1))
    terms[1] = conv_t(pairs1[1], weights1, 2)
    whole1 = after(whole1, terms[1][1])
    mine1 = jnp.where(chip == plane, whole1, 0.0)
    for s in range(1, PLANES):
        mine1 += route(
            whole1,
            [((2 * j + c, j), (2 * j + c, (j + s) % PLANES)) for j in groups for c in range(2)],
        )

    near, mine1 = lax.optimization_barrier((swap(terms[1][1], Y), mine1))
    bias1_grad, gain1_grad = mine1[0], mine1[1]
    first = (terms[1][0] + near.astype(f32)).astype(bf16)
    out_local = after(out_local, terms[1][1])
    out_local = jnp.concatenate(
        [out_local[:, : lanes2 // 2], swap(out_local[:, lanes2 // 2 :], 1)], axis=0
    )
    out_local = mxu(outward, out_local, TN).astype(bf16)
    out_local = after(out_local, first).reshape(n, own_frames, MELS * part)
    out_pieces = [out_local[k] for k in range(n)]
    later_near = after(later_near, first)
    for k, r in enumerate(order[1:]):
        pairs1[r] = [dpre1[r], later_near[k * rows : (k + 1) * rows]]
    terms[2] = conv_t(pairs1[2], weights1, 2)
    nears[2] = swap(terms[2][1], Y)
    before = terms[2][1]
    for r in (3, 0):
        pairs1[r][1] = after(pairs1[r][1], before)
        terms[r] = conv_t(pairs1[r], weights1, 2)
        nears[r] = swap(terms[r][1], Y)
        before = terms[r][1]

    second = ((terms[2][0] + nears[2].astype(f32)) + along(first, 1).astype(f32)).astype(bf16)
    moved = along(second, 1)
    pairs1[1][0] = after(pairs1[1][0], second)
    grad1_own, grad1_send = weight_grad_own(
        pos,
        [pairs1[r] for r in order],
        [inputs[r] for r in order],
        grad1_place,
        (PLANES, 9, half, 128),
        pl.BlockSpec(
            (1, 9, half, 128), lambda t, p: (2 * (p[1] ^ (t // 2)) + t % 2, 0, 0, 0)
        ),
        36,
    )
    grad1_send, moved, nears[3] = lax.optimization_barrier((grad1_send, moved, nears[3]))
    third = ((terms[3][0] + nears[3].astype(f32)) + moved.astype(f32)).astype(bf16)
    moved = along(third, 1)
    grad1 = (grad1_own + swap(grad1_send, 1).astype(f32)).astype(bf16)
    grad1_planes = lax.all_to_all(grad1, "batch", 0, 0, tiled=True)
    grad2_first = after(grad2[0], third, grad1)
    sent = [swap(after(out_pieces[k], grad1), k) for k in (4, 5, 6)]
    grad2_own, grad2_send = weight_grad_own(
        pos,
        [[grad2_first]] + [[g] for g in grad2[1:]],
        hidden,
        grad2_place,
        w2.shape,
        pl.BlockSpec(
            (9, part, 128), lambda t, p: (0, 0, 2 * (p[2] ^ (t % 2)) + (p[1] ^ (t // 2)))
        ),
        36,
    )
    grad2_send, nears[0], *sent = lax.optimization_barrier((grad2_send, nears[0], *sent))
    later = [swap(after(out_pieces[k], grad2_send), k) for k in (7, 1, 2, 3)]
    moved, grad1_planes, *later = lax.optimization_barrier((moved, grad1_planes, *later))
    out_pieces = out_pieces[:1] + later[1:] + sent + later[:1]

    def quarter(k):
        return lax.dynamic_index_in_dim(grad1_planes, chip ^ k, 0, keepdims=False)

    quads = [quarter(0)] + [swap(quarter(k), 2 * k) for k in range(1, CHIPS)]
    grad2_got = swap(after(grad2_send, moved), 1)
    dx = ((terms[0][0] + nears[0].astype(f32)) + moved.astype(f32)).astype(bf16)
    low, high = dx[:, : MELS * lanes1], dx[:, MELS * lanes1 :]
    other = swap(jnp.where(core == 0, high, low), 1)
    dx = jnp.concatenate([jnp.where(core == 0, low, high), other], axis=0)
    dx = mxu(picker, dx, TN).astype(bf16)
    dx, grad2_got, quads[0], *out_pieces = lax.optimization_barrier(
        (dx, grad2_got, quads[0], *out_pieces)
    )

    dx = lax.all_to_all(dx.reshape(n, own_frames, MELS * lanes1), "tm", 0, 0, tiled=True)
    dx = dx.reshape(2, 2, 2, own_frames, MELS, lanes1).transpose(3, 4, 0, 2, 1, 5)
    input_grad = dx.reshape(1, own_frames, MELS, width1)
    conv1_grad = from_quarters(pos, quads).transpose(1, 0, 2)
    block_out = from_lanes(pos, out_pieces)[None]
    conv2_grad = (grad2_own + grad2_got.astype(f32)).transpose(1, 0, 2)

    return (
        block_out,
        input_grad,
        conv1_grad,
        gain1_grad,
        bias1_grad,
        conv2_grad,
        grads2[1, :part],
        grads2[0, :part],
    )


def solution(mesh):
    return jax.shard_map(
        stationary if dict(mesh.shape) == {"tm": 8, "batch": 4} else gathered,
        mesh=mesh,
        in_specs=(
            P("batch", "tm", None, None),
            P("batch", None),
            P("tm", None, "batch"),
            P("tm"),
            P("tm"),
            P("tm", None, "batch"),
            P("tm"),
            P("tm"),
            P("batch", "tm", None, None),
        ),
        out_specs=(
            P("batch", "tm", None, None),
            P("batch", "tm", None, None),
            P("tm", None, "batch"),
            P("tm"),
            P("tm"),
            P("tm", None, "batch"),
            P("tm"),
            P("tm"),
        ),
        check_vma=False,
    )
```
